32 devices in a mesh: rep: 4 (over y, core), fsdp: 8 (over z, x).
Axes of the slice: x: 2, y: 2, z: 4, core: 2. Of those that a mesh axis runs over, the one named last changes fastest.
Arguments:
- hidden_in: bfloat16 [32, 512, 768], P(('rep', 'fsdp')), may hold values from -6 to 6
- memory: bfloat16 [32, 512, 768], P(('rep', 'fsdp')), may hold values from -6 to 6
- lengths: int32 [32], P(('rep', 'fsdp')), may hold values from 256 to 512, as said below
- buckets: int32 [512], replicated, may hold values from 0 to 31, as said below
- cotangent: bfloat16 [32, 512, 768], P(('rep', 'fsdp')), may hold values from -6 to 6
- self_gain: bfloat16 [768], P('fsdp'), may hold values from 0.099609375 to 1.8984375
- self_query: bfloat16 [768, 768], P('fsdp'), may hold values from -0.02734375 to 0.02734375
- self_key: bfloat16 [768, 768], P('fsdp'), may hold values from -0.21875 to 0.21875
- self_value: bfloat16 [768, 768], P('fsdp'), may hold values from -0.21875 to 0.21875
- self_out: bfloat16 [768, 768], P('fsdp'), may hold values from -0.875 to 0.875
- bias_table: bfloat16 [384], P('fsdp'), may hold values from -4 to 4
- cross_gain: bfloat16 [768], P('fsdp'), may hold values from 0.099609375 to 1.8984375
- cross_query: bfloat16 [768, 768], P('fsdp'), may hold values from -0.02734375 to 0.02734375
- cross_key: bfloat16 [768, 768], P('fsdp'), may hold values from -0.21875 to 0.21875
- cross_value: bfloat16 [768, 768], P('fsdp'), may hold values from -0.21875 to 0.21875
- cross_out: bfloat16 [768, 768], P('fsdp'), may hold values from -0.875 to 0.875
- feed_gain: bfloat16 [768], P('fsdp'), may hold values from 0.099609375 to 1.8984375
- feed_gate: bfloat16 [768, 2048], P('fsdp'), may hold values from -0.21875 to 0.21875
- feed_up: bfloat16 [768, 2048], P('fsdp'), may hold values from -0.21875 to 0.21875
- feed_down: bfloat16 [2048, 768], P('fsdp'), may hold values from -0.125 to 0.125
Outputs:
- layer_out: bfloat16 [32, 512, 768], P(('rep', 'fsdp'))
- input_grad: float32 [32, 512, 768], P(('rep', 'fsdp'))
- memory_grad: float32 [32, 512, 768], P(('rep', 'fsdp'))
- self_gain_grad: float32 [768], P('fsdp')
- self_query_grad: float32 [768, 768], P('fsdp')
- self_key_grad: float32 [768, 768], P('fsdp')
- self_value_grad: float32 [768, 768], P('fsdp')
- self_out_grad: float32 [768, 768], P('fsdp')
- bias_table_grad: float32 [384], P('fsdp')
- cross_gain_grad: float32 [768], P('fsdp')
- cross_query_grad: float32 [768, 768], P('fsdp')
- cross_key_grad: float32 [768, 768], P('fsdp')
- cross_value_grad: float32 [768, 768], P('fsdp')
- cross_out_grad: float32 [768, 768], P('fsdp')
- feed_gain_grad: float32 [768], P('fsdp')
- feed_gate_grad: float32 [768, 2048], P('fsdp')
- feed_up_grad: float32 [768, 2048], P('fsdp')
- feed_down_grad: float32 [2048, 768], P('fsdp')
The draws below stay inside these ranges and needn't reach their ends.
Inputs may be any that keep to these rules, and one draw needn't show every extreme that they name: `lengths`: every row's length is 256 or 512, and both occur. buckets never fall with the offset, start at 0 at offset 0 and reach 31; every bucket is used.
All inputs are finite; a program needn't handle non-finite values.
Results may differ from the reference program's by a relative error of at most 0.023.
Values may be sent and summed in bfloat16 or wider, within the bound.
No kernel may reach another device: no remote copies, remote signals or barrier semaphores. Data moves between devices by JAX's collectives and lax.ppermute only.
A program may use at most 192 MiB of HBM per device.

```python
import math
import jax
import jax.numpy as jnp
from jax import lax

D = 768
HEADS = 12
HEAD = 64
FF = 2048
BUCKETS = 32
LEN = 512
MEM = 512
ROWS = 32


def draw_lengths(key, part):
    key = jax.random.fold_in(key, 11)
    choose = jax.random.randint(key, (ROWS,), 0, 2)
    choose = choose.at[0].set(1).at[ROWS - 1].set(0)
    return (LEN // 2 + choose * (LEN // 2)).astype(jnp.int32)


def draw_buckets(key, part):
    key = jax.random.fold_in(key, 23)
    steps = jax.random.permutation(key, LEN - 1)[:BUCKETS - 1] + 1
    offsets = jnp.arange(LEN)
    return jnp.sum((steps[None, :] <= offsets[:, None]).astype(jnp.int32), axis=1).astype(jnp.int32)


def strengthened(drawn, key, source, target, shards_of, factor):
    def block_of(dim):
        return (jnp.arange(drawn.shape[dim]) // (drawn.shape[dim] // shards_of)).reshape((-1,) + (1,) * (drawn.ndim - 1 - dim))

    one_side = jax.random.permutation(key, shards_of)[block_of(target)]
    other_side = (block_of(target) + shards_of // 2) % shards_of
    return jnp.where((block_of(source) == one_side) | (block_of(source) == other_side), factor * drawn, drawn)


def levels(rng, extent, shards, low, top_value):
    factor_of = 1.0
    for dim, shards_of in shards:
        draws = jax.random.uniform(jax.random.fold_in(jax.random.fold_in(rng, 6), dim), (shards_of,), jnp.float32, low / len(shards), top_value / len(shards))
        factor_of = factor_of * jnp.repeat(jnp.exp(draws), extent[dim] // shards_of).reshape((-1,) + (1,) * (len(extent) - 1 - dim))
    return factor_of


def scatter_about(key, shape, spread, bound, pieces=(), held_as=jnp.bfloat16):
    values = jax.random.normal(key, shape, jnp.float32) * spread
    if len(pieces) > 0:
        values = levels(key, shape, pieces, -0.22, 0.18) * values
    return jnp.clip(values, min=-bound, max=bound).astype(held_as)


def bell_draw_with(key, dims, deviation, most, shards, heavy, kind=jnp.bfloat16):
    values = deviation * jax.random.normal(key, dims, jnp.float32)
    if shards:
        values = values * levels(key, dims, shards, -0.22, 0.18)
    return jnp.clip(strengthened(values, jax.random.fold_in(key, 3), *heavy), -most, most).astype(kind)


def setup_inputs(seed: int = 0) -> dict:
    key_of = jax.random.split(jax.random.key(seed), 21)
    hidden_in = bell_draw_with(key_of[0], (ROWS, LEN, D), 1.0, 6.0, ((0, 32),), (0, 2, 32, 2.75))
    memory = bell_draw_with(key_of[1], (ROWS, MEM, D), 1.0, 6.0, ((0, 32),), (0, 2, 32, 2.75))
    lengths = draw_lengths(jax.random.fold_in(key_of[20], 71), 0)
    buckets = draw_buckets(jax.random.fold_in(key_of[20], 71), 0)
    cotangent = scatter_about(key_of[4], (ROWS, LEN, D), 1.0, 6.0, ((0, 32),))
    self_gain = jnp.clip(1.0 + 0.18 * jax.random.normal(key_of[5], (D,), jnp.float32), 0.099609375, 1.8984375).astype(jnp.bfloat16)
    self_query = scatter_about(key_of[6], (D, D), (D * HEAD) ** -0.5, 0.02734375, ((0, 8),))
    self_key = scatter_about(key_of[7], (D, D), D ** -0.5, 0.21875, ((0, 8),))
    self_value = scatter_about(key_of[8], (D, D), D ** -0.5, 0.21875, ((0, 8),))
    self_out = scatter_about(key_of[9], (D, D), (D // 16) ** -0.5, 0.875, ((0, 8),))
    bias_table = scatter_about(key_of[10], (BUCKETS * HEADS,), 1.0, 4.0, ((0, 8),))
    cross_gain = jnp.clip(1.0 + 0.18 * jax.random.normal(key_of[11], (D,), jnp.float32), 0.099609375, 1.8984375).astype(jnp.bfloat16)
    cross_query = scatter_about(key_of[12], (D, D), (D * HEAD) ** -0.5, 0.02734375, ((0, 8),))
    cross_key = scatter_about(key_of[13], (D, D), D ** -0.5, 0.21875, ((0, 8),))
    cross_value = scatter_about(key_of[14], (D, D), D ** -0.5, 0.21875, ((0, 8),))
    cross_out = scatter_about(key_of[15], (D, D), (D // 16) ** -0.5, 0.875, ((0, 8),))
    feed_gain = jnp.clip(1.0 + 0.18 * jax.random.normal(key_of[16], (D,), jnp.float32), 0.099609375, 1.8984375).astype(jnp.bfloat16)
    feed_gate = scatter_about(key_of[17], (D, FF), D ** -0.5, 0.21875, ((0, 8),))
    feed_up = scatter_about(key_of[18], (D, FF), D ** -0.5, 0.21875, ((0, 8),))
    feed_down = scatter_about(key_of[19], (FF, D), FF ** -0.5, 0.125, ((0, 8),))
    return dict(hidden_in=hidden_in, memory=memory, lengths=lengths, buckets=buckets, cotangent=cotangent, self_gain=self_gain, self_query=self_query, self_key=self_key, self_value=self_value, self_out=self_out, bias_table=bias_table, cross_gain=cross_gain, cross_query=cross_query, cross_key=cross_key, cross_value=cross_value, cross_out=cross_out, feed_gain=feed_gain, feed_gate=feed_gate, feed_up=feed_up, feed_down=feed_down)


EPSILON = 1e-06
MASKED = -1e+30
PRECISE = lax.Precision.HIGHEST

@jax.custom_vjp
def low(v):
    return lax.optimization_barrier(v.astype(jnp.bfloat16)).astype(jnp.float32)

@jax.custom_vjp
def low_back(v):
    return v

def low_keep(v):
    return (low(v), None)

def low_pass(kept, grad):
    return (grad,)

def back_keep(v):
    return (v, None)

def back_low(kept, grad):
    return (low(grad),)
low.defvjp(low_keep, low_pass)
low_back.defvjp(back_keep, back_low)

def rounded_both(value):
    return low(low_back(value))

def rms_norm(hidden, gain):
    scale = lax.rsqrt(lax.optimization_barrier(jnp.mean(hidden * hidden, axis=-1, keepdims=True)) + EPSILON)
    return hidden * scale * gain

def project(rows, weight):
    return jnp.einsum('gtd,de->gte', rows, weight, precision=PRECISE)

def attention(query, keys, values, bias, mask):
    groups = query.shape[0]
    query_length = query.shape[1]
    key_length = keys.shape[1]
    heads_query = query.reshape(groups, query_length, HEADS, HEAD)
    heads_keys = keys.reshape(groups, key_length, HEADS, HEAD)
    heads_values = values.reshape(groups, key_length, HEADS, HEAD)
    scores = low_back(jnp.einsum('gihe,gjhe->ghij', heads_query, heads_keys, precision=PRECISE) + bias)
    scores = jnp.where(mask, scores, MASKED)
    highest = lax.optimization_barrier(jnp.max(scores, axis=-1, keepdims=True))
    weights = jnp.exp(scores - highest)
    probs = weights / lax.optimization_barrier(jnp.sum(weights, axis=-1, keepdims=True))
    mixed = jnp.einsum('ghij,gjhe->gihe', low(probs), heads_values, precision=PRECISE)
    return rounded_both(mixed.reshape(groups, query_length, HEADS * HEAD))

def layer_rows(hidden, memory, lengths, bias, params):
    self_gain, self_query, self_key, self_value, self_out, bias_table, cross_gain, cross_query, cross_key, cross_value, cross_out, feed_gain, feed_gate, feed_up, feed_down = params
    position = jnp.arange(LEN)
    valid = position[None, :] < lengths[:, None]
    causal = position[None, :] <= position[:, None]
    self_mask = causal[None, None, :, :] & valid[:, None, None, :]
    cross_mask = valid[:, None, None, :]
    normed = low(rms_norm(hidden, self_gain))
    query = rounded_both(project(normed, self_query))
    keys = rounded_both(project(normed, self_key))
    values = rounded_both(project(normed, self_value))
    mixed = attention(query, keys, values, bias, self_mask)
    after_self = hidden + low_back(project(mixed, self_out))
    normed = low(rms_norm(after_self, cross_gain))
    cross_queries = rounded_both(project(normed, cross_query))
    memory_keys = rounded_both(project(memory, cross_key))
    memory_values = rounded_both(project(memory, cross_value))
    mixed = attention(cross_queries, memory_keys, memory_values, 0.0, cross_mask)
    after_cross = after_self + low_back(project(mixed, cross_out))
    normed = low(rms_norm(after_cross, feed_gain))
    gate = low_back(project(normed, feed_gate))
    lift = low_back(project(normed, feed_up))
    inner = low(jax.nn.gelu(gate, approximate=True) * lift)
    return after_cross + low_back(project(inner, feed_down))

def reference(hidden_in, memory, lengths, buckets, cotangent, self_gain, self_query, self_key, self_value, self_out, bias_table, cross_gain, cross_query, cross_key, cross_value, cross_out, feed_gain, feed_gate, feed_up, feed_down):
    weights = tuple((item.astype(jnp.float32) for item in (self_gain, self_query, self_key, self_value, self_out, bias_table, cross_gain, cross_query, cross_key, cross_value, cross_out, feed_gain, feed_gate, feed_up, feed_down)))
    group = math.gcd(ROWS, 8)
    position = jnp.arange(LEN)
    offsets = jnp.maximum(position[:, None] - position[None, :], 0)
    picks = (buckets[:, None] == jnp.arange(BUCKETS)[None, :]).astype(jnp.float32)
    grouped_lengths = lengths.reshape(ROWS // group, group)

    def forward(hidden, memory_float, *params):
        table = params[5].reshape(BUCKETS, HEADS)
        per_offset = jnp.dot(picks, table, precision=PRECISE)
        bias = jnp.transpose(per_offset[offsets], (2, 0, 1))[None]

        def block(items):
            return layer_rows(items[0], items[1], items[2], bias, params)
        outputs = lax.map(jax.checkpoint(block), (hidden.reshape(ROWS // group, group, LEN, D), memory_float.reshape(ROWS // group, group, MEM, D), grouped_lengths))
        return outputs.reshape(ROWS, LEN, D)
    result, pullback = jax.vjp(forward, hidden_in.astype(jnp.float32), memory.astype(jnp.float32), *weights)
    grads = pullback(cotangent.astype(jnp.float32))
    return (result.astype(jnp.bfloat16), grads[0], grads[1], grads[2], grads[3], grads[4], grads[5], grads[6], grads[7], grads[8], grads[9], grads[10], grads[11], grads[12], grads[13], grads[14], grads[15], grads[16])
```

```python
import functools
import jax
import jax.numpy as jnp
from jax import lax
from jax.experimental import pallas as pl
from jax.experimental.pallas import tpu as pltpu
from jax.sharding import PartitionSpec as P

HEADS = 12
HEAD = 64
BUCKETS = 32
EPSILON = 1e-06
MASKED = -1e30
PRECISE = lax.Precision.HIGHEST
VMEM = 48 * 1024 * 1024
F32 = jnp.float32
BF16 = jnp.bfloat16
NT = (((1,), (1,)), ((), ()))
NN = (((1,), (0,)), ((), ()))
TN = (((0,), (0,)), ((), ()))
TILE = 128


def dot(a, b, dims):
    return lax.dot_general(a, b, dims, preferred_element_type=F32)


def bias_tiles(offs, length):
    base = pltpu.roll(jnp.broadcast_to(offs, (TILE, length)), 0, 1, stride=1, stride_axis=0)
    return jnp.concatenate([base[:, length - TILE :], base], axis=1)


def diagonal_sums(spread, length):
    total = spread[:8]
    for at in range(8, TILE, 8):
        total = total + pltpu.roll(spread[at : at + 8], length - at, 1)
    row = lax.broadcasted_iota(jnp.int32, total.shape, 0)
    for bit in (1, 2, 4):
        total = jnp.where((row & bit) != 0, pltpu.roll(total, length - bit, 1), total)
    return jnp.sum(total, axis=0, keepdims=True)


def bias_block(tiles, first, rows, step):
    parts = []
    for block in range(rows // TILE):
        at = first - block * TILE + TILE
        parts.append(tiles[:, at : at + step])
    return jnp.concatenate(parts, axis=0)


def allowed(rows, step, first, length, causal):
    key = lax.broadcasted_iota(jnp.int32, (rows, step), 0)
    ok = key < length
    if causal:
        item = lax.broadcasted_iota(jnp.int32, (rows, step), 1) + first
        ok = ok & (key <= item)
    return ok


def forward_kernel(causal, lengths, *refs):
    if causal:
        offs_ref, q_ref, k_ref, v_ref, mixed_ref, lse_ref = refs
    else:
        q_ref, k_ref, v_ref, mixed_ref, lse_ref = refs
    size = q_ref.shape[0]
    step = 256
    length = lengths[0]
    for head in range(2):
        cols = slice(head * HEAD, (head + 1) * HEAD)
        if causal:
            tiles = bias_tiles(offs_ref[0, head : head + 1, :], size)
        for first in range(0, size, step):
            rows = first + step if causal else size
            scores = dot(k_ref[:rows, cols], q_ref[first : first + step, cols], NT)
            if causal:
                scores = scores + bias_block(tiles, first, rows, step)
            scores = jnp.where(allowed(rows, step, first, length, causal), scores, MASKED)
            highest = jnp.max(scores, axis=0, keepdims=True)
            weights = jnp.exp(scores - highest)
            total = jnp.sum(weights, axis=0, keepdims=True)
            mixed = dot(v_ref[:rows, cols], weights.astype(BF16), TN) * (1.0 / total)
            mixed_ref[first : first + step, cols] = mixed.T.astype(BF16)
            lse_ref[0, head : head + 1, first : first + step] = highest + jnp.log(total)


def backward_kernel(causal, lengths, *refs):
    if causal:
        offs_ref, q_ref, k_ref, v_ref, g_ref, lse_ref, dq_ref, dk_ref, dv_ref, doffs_ref = refs
    else:
        q_ref, k_ref, v_ref, g_ref, lse_ref, dq_ref, dk_ref, dv_ref = refs
    size = q_ref.shape[0]
    step = 256
    length = lengths[0]
    for head in range(2):
        cols = slice(head * HEAD, (head + 1) * HEAD)
        if causal:
            tiles = bias_tiles(offs_ref[0, head : head + 1, :], size)
            spread = [jnp.zeros((TILE, TILE), F32) for _ in range(size // TILE)]
        dk = [None] * (size // step)
        dv = [None] * (size // step)
        for first in range(0, size, step):
            rows = first + step if causal else size
            q = q_ref[first : first + step, cols]
            g = g_ref[first : first + step, cols]
            k = k_ref[:rows, cols]
            scores = dot(k, q, NT)
            if causal:
                scores = scores + bias_block(tiles, first, rows, step)
            scores = jnp.where(allowed(rows, step, first, length, causal), scores, MASKED)
            probs = jnp.exp(scores - lse_ref[0, head : head + 1, first : first + step])
            prob_grad = dot(v_ref[:rows, cols], g, NT)
            delta = jnp.sum(probs * prob_grad, axis=0, keepdims=True)
            score_grad = (probs * (prob_grad - delta)).astype(BF16)
            if causal:
                for block in range(rows // TILE):
                    for lane in range(step // TILE):
                        at = first // TILE + lane - block
                        if at >= 0:
                            spread[at] = spread[at] + score_grad[
                                block * TILE : (block + 1) * TILE, lane * TILE : (lane + 1) * TILE
                            ].astype(F32)
            dk_now = dot(score_grad, q, NN)
            dv_now = dot(probs.astype(BF16), g, NN)
            for block in range(rows // step):
                part = slice(block * step, (block + 1) * step)
                dk[block] = dk_now[part] if dk[block] is None else dk[block] + dk_now[part]
                dv[block] = dv_now[part] if dv[block] is None else dv[block] + dv_now[part]
            dq_ref[first : first + step, cols] = dot(k, score_grad, TN).T.astype(BF16)
        for block in range(size // step):
            part = slice(block * step, (block + 1) * step)
            dk_ref[part, cols] = dk[block].astype(BF16)
            dv_ref[part, cols] = dv[block].astype(BF16)
        if causal:
            doffs_ref[0, head : head + 1, :] = diagonal_sums(jnp.concatenate(spread, axis=1), size)


def pair_spec(size):
    return pl.BlockSpec((size, 2 * HEAD), lambda p, *_: (0, p))


def lane_spec(size):
    return pl.BlockSpec((1, 2, size), lambda p, *_: (p, 0, 0))


def attend_forward(lengths, offs, q, k, v):
    causal = offs is not None
    size = q.shape[0]
    pairs = HEADS // 2
    ins = [pair_spec(size)] * 3
    args = (q, k, v)
    if causal:
        ins = [lane_spec(size)] + ins
        args = (offs.reshape(pairs, 2, size),) + args
    return pl.pallas_call(
        functools.partial(forward_kernel, causal),
        out_shape=(
            jax.ShapeDtypeStruct(q.shape, BF16),
            jax.ShapeDtypeStruct((pairs, 2, size), F32),
        ),
        grid_spec=pltpu.PrefetchScalarGridSpec(
            num_scalar_prefetch=1,
            grid=(pairs,),
            in_specs=ins,
            out_specs=[pair_spec(size), lane_spec(size)],
        ),
        compiler_params=pltpu.CompilerParams(vmem_limit_bytes=VMEM),
        cost_estimate=pl.CostEstimate(
            flops=11 * 10**9, bytes_accessed=4 * 2**20, transcendentals=3 * 2**20
        ),
        name="attend_forward_self" if causal else "attend_forward_cross",
    )(lengths, *args)


def attend_backward(lengths, offs, q, k, v, g, lse):
    causal = offs is not None
    size = q.shape[0]
    pairs = HEADS // 2
    ins = [pair_spec(size)] * 4 + [lane_spec(size)]
    args = (q, k, v, g, lse)
    outs = [pair_spec(size)] * 3
    shapes = [jax.ShapeDtypeStruct(q.shape, BF16)] * 3
    if causal:
        ins = [lane_spec(size)] + ins
        args = (offs.reshape(pairs, 2, size),) + args
        outs = outs + [lane_spec(size)]
        shapes = shapes + [jax.ShapeDtypeStruct((pairs, 2, size), F32)]
    return pl.pallas_call(
        functools.partial(backward_kernel, causal),
        out_shape=tuple(shapes),
        grid_spec=pltpu.PrefetchScalarGridSpec(
            num_scalar_prefetch=1, grid=(pairs,), in_specs=ins, out_specs=outs
        ),
        compiler_params=pltpu.CompilerParams(vmem_limit_bytes=VMEM),
        cost_estimate=pl.CostEstimate(
            flops=17 * 10**9, bytes_accessed=6 * 2**20, transcendentals=3 * 2**20
        ),
        name="attend_backward_self" if causal else "attend_backward_cross",
    )(lengths, *args)


def after(array, *earlier):
    return lax.optimization_barrier((array,) + earlier)[0]


class Links:
    def __init__(self, reps, owners):
        self.owners = owners
        self.bits = owners.bit_length() - 1
        self.count = reps * owners
        self.rep = lax.axis_index("rep")
        self.owner = lax.axis_index("fsdp")
        self.core = self.rep % 2
        self.side = self.rep // 2
        self.core_word = self.core.reshape(1).astype(jnp.int32)

    def move(self, array, target):
        return lax.ppermute(
            array, ("rep", "fsdp"), [(device, target(device)) for device in range(self.count)]
        )

    def over_owner(self, array, bit):
        return self.move(array, lambda device: device ^ (1 << bit))

    def over_core(self, array):
        return self.move(array, lambda device: device ^ self.owners)

    def over_side(self, array):
        return self.move(array, lambda device: device ^ (2 * self.owners))

    def over_pair(self, array, first):
        def target(device):
            core = (device // self.owners) % 2
            return device ^ (1 if (core == 0) == first else 2 * self.owners)

        return self.move(array, target)

    def step(self, array, name):
        if name == "first":
            return self.over_pair(array, True)
        if name == "second":
            return self.over_pair(array, False)
        return self.over_owner(array, name)

    def far_to_near(self):
        return tuple(range(self.bits - 1, 0, -1))

    def places(self, core, order):
        index = jnp.arange(2 * self.owners)
        owner = jnp.full_like(index, self.owner)
        side = jnp.full_like(index, self.side)
        for at, name in enumerate(order):
            flip = (index >> at) & 1
            if name == "first":
                owner = owner ^ jnp.where(core == 0, flip, 0)
                side = side ^ jnp.where(core == 0, 0, flip)
            elif name == "second":
                owner = owner ^ jnp.where(core == 0, 0, flip)
                side = side ^ jnp.where(core == 0, flip, 0)
            else:
                owner = owner ^ (flip << name)
        return (owner * 2 + side).astype(jnp.int32)


def assemble_kernel(places, core, *refs):
    sources, out_ref, sems = refs[:4], refs[4], refs[5]
    width = sources[0].shape[-1]
    copies = []
    for half in range(2):
        column = core[0] if half == 0 else 1 - core[0]
        start = pl.multiple_of(column * width, width)
        for part in range(2):
            source = sources[2 * half + part]
            for index in range(source.shape[0]):
                at = part * source.shape[0] + index
                copies.append(
                    pltpu.make_async_copy(
                        source.at[index],
                        out_ref.at[:, places[half, at], :, pl.ds(start, width)],
                        sems.at[half, at],
                    )
                )
    for copy in copies:
        copy.start()
    for copy in copies:
        copy.wait()


def assemble(links, order, own, other):
    places = jnp.stack([links.places(links.core, order), links.places(1 - links.core, order)])
    half, weights, rows, columns = own[0].shape
    shape = (weights, 2 * half, rows, 2 * columns)
    out = pl.pallas_call(
        assemble_kernel,
        out_shape=jax.ShapeDtypeStruct(shape, BF16),
        grid_spec=pltpu.PrefetchScalarGridSpec(
            num_scalar_prefetch=2,
            grid=(1,),
            in_specs=[pl.BlockSpec(memory_space=pl.ANY)] * 4,
            out_specs=pl.BlockSpec(shape, lambda *_: (0, 0, 0, 0)),
            scratch_shapes=[pltpu.SemaphoreType.DMA((2, 2 * half))],
        ),
        compiler_params=pltpu.CompilerParams(vmem_limit_bytes=VMEM),
        name="assemble",
    )(places, links.core_word, *own, *other)
    return out.reshape(weights, 2 * half * rows, 2 * columns)


def own_block(links, shards):
    rows = shards[0].shape[0] // 2
    columns = shards[0].shape[1] // 2
    at = (links.side * rows, links.core * columns)
    return jnp.stack([lax.dynamic_slice(shard, at, (rows, columns)) for shard in shards])[None]


def gather_group(links, order, shards, earlier):
    block = own_block(links, shards)
    done = []
    parts = None
    for at, name in enumerate(order):
        if earlier:
            block = after(block, earlier[at])
        got = links.step(block, name)
        done.append(got)
        parts = [block, got]
        if at < len(order) - 1:
            block = jnp.concatenate(parts, axis=0)
    other = [links.over_core(part) for part in parts]
    return assemble(links, order, parts, other), done


def gather_small(links, values):
    block = values[None]
    for bit in range(links.bits):
        block = jnp.concatenate([block, links.over_owner(block, bit)], axis=0)
    return block[jnp.arange(links.owners) ^ links.owner]


def sum_small(links, values):
    values = values + links.over_core(values)
    values = values + links.over_side(values)
    for bit in range(links.bits):
        values = values + links.over_owner(values, bit)
    return values


def split_sum_kernel(picks, kept_one, kept_two, got_one, got_two, keep_ref, send_ref):
    keep_ref[0] = (kept_one[:, 0].astype(F32) + got_one[:, 0].astype(F32)).astype(BF16)
    send_ref[0] = (kept_two[:, 0].astype(F32) + got_two[:, 0].astype(F32)).astype(BF16)


def split_sum(picks, kept, got):
    weights, count, rows, columns = kept.shape
    half = count // 2
    keep = pl.BlockSpec((weights, 1, rows, columns), lambda i, picks: (0, picks[i], 0, 0))
    send = pl.BlockSpec((weights, 1, rows, columns), lambda i, picks: (0, picks[half + i], 0, 0))
    out = pl.BlockSpec((1, weights, rows, columns), lambda i, picks: (i, 0, 0, 0))
    return pl.pallas_call(
        split_sum_kernel,
        out_shape=(jax.ShapeDtypeStruct((half, weights, rows, columns), BF16),) * 2,
        grid_spec=pltpu.PrefetchScalarGridSpec(
            num_scalar_prefetch=1, grid=(half,), in_specs=[keep, send, keep, send], out_specs=[out, out]
        ),
        name="split_sum",
    )(picks, kept, kept, got, got)


def reduce_group(links, order, keep, send):
    weights, rows, columns = keep.shape
    shape = (weights, 2 * links.owners, rows // (2 * links.owners), columns)
    got = links.over_core(send).reshape(shape)
    keep = keep.reshape(shape)
    picks = links.places(links.core, order[::-1])
    keep, send = split_sum(picks, keep, got)
    for at, name in enumerate(order):
        got = links.step(send, name)
        if at < len(order) - 1:
            half = keep.shape[0] // 2
            send = (keep[half:].astype(F32) + got[half:].astype(F32)).astype(BF16)
            keep = (keep[:half].astype(F32) + got[:half].astype(F32)).astype(BF16)
    mine = (keep.astype(F32) + got.astype(F32)).astype(BF16)[0]
    got = links.over_side(mine)
    first = links.side == 0
    pair = jnp.concatenate([jnp.where(first, mine, got), jnp.where(first, got, mine)], axis=1)
    got = links.over_core(pair)
    first = links.core == 0
    pair = jnp.concatenate([jnp.where(first, pair, got), jnp.where(first, got, pair)], axis=2)
    return pair.astype(F32)


def matmul(a, b):
    return dot(a, b, NN)


def matmul_nt(a, b):
    return dot(a, b, NT)


def norm_forward(hidden, gain):
    scale = lax.rsqrt(jnp.mean(hidden * hidden, axis=-1, keepdims=True) + EPSILON)
    return (hidden * scale * gain, scale)


def norm_backward(hidden, scale, gain, upstream):
    gain_grad = jnp.sum(upstream * (hidden * scale), axis=0)
    weighted = upstream * gain
    inner = jnp.mean(weighted * hidden, axis=-1, keepdims=True)
    return (scale * weighted - hidden * (scale * scale * scale) * inner, gain_grad)


def smooth_gate(value):
    return jax.nn.gelu(value, approximate=True)


def weight_grads_kernel(count, other, core, *refs):
    rows, grads, out_ref = refs[:count], refs[count : 2 * count], refs[2 * count]
    column = 1 - core[0] if other else core[0]
    width = out_ref.shape[-1]
    start = pl.multiple_of(column * width, width)
    for at in range(count):
        out_ref[at] = dot(rows[at][...], grads[at][:, pl.ds(start, width)], TN).astype(BF16)


def weight_grads_half(links, other, rows, grads):
    count = len(rows)
    shape = (count, rows[0].shape[1], grads[0].shape[1] // 2)
    return pl.pallas_call(
        functools.partial(weight_grads_kernel, count, other),
        out_shape=jax.ShapeDtypeStruct(shape, BF16),
        grid_spec=pltpu.PrefetchScalarGridSpec(
            num_scalar_prefetch=1,
            grid=(1,),
            in_specs=[pl.BlockSpec(item.shape, lambda *_: (0, 0)) for item in (*rows, *grads)],
            out_specs=pl.BlockSpec(shape, lambda *_: (0, 0, 0)),
        ),
        compiler_params=pltpu.CompilerParams(vmem_limit_bytes=VMEM),
        cost_estimate=pl.CostEstimate(
            flops=2 * shape[0] * shape[1] * shape[2] * rows[0].shape[0],
            bytes_accessed=2 * shape[0] * shape[1] * shape[2],
            transcendentals=0,
        ),
        name="weight_grads",
    )(links.core_word, *rows, *grads)


def weight_grads(links, rows, grads):
    send = weight_grads_half(links, True, rows, grads)
    keep = weight_grads_half(links, False, rows, grads)
    return keep, send


def on_device(
    reps,
    owners,
    hidden_in,
    memory,
    lengths,
    buckets,
    cotangent,
    self_gain,
    self_query,
    self_key,
    self_value,
    self_out,
    bias_table,
    cross_gain,
    cross_query,
    cross_key,
    cross_value,
    cross_out,
    feed_gain,
    feed_gate,
    feed_up,
    feed_down,
):
    links = Links(reps, owners)
    width = hidden_in.shape[2]
    share = width // owners
    memory = memory[0]
    cotangent = cotangent[0]
    hidden = hidden_in[0].astype(F32)
    small = jnp.concatenate([self_gain, cross_gain, feed_gain, bias_table])
    small = gather_small(links, small).astype(F32)
    gain_one = small[:, :share].reshape(1, -1)
    gain_two = small[:, share : 2 * share].reshape(1, -1)
    gain_three = small[:, 2 * share : 3 * share].reshape(1, -1)
    table = small[:, 3 * share :].reshape(BUCKETS, HEADS)

    order = links.far_to_near() + ("first", "second")
    back = order[::-1]
    qkv, done = gather_group(links, order, (self_query, self_key, self_value), None)
    five, done = gather_group(
        links, order, (self_out, cross_query, cross_key, cross_value, cross_out), done
    )
    gate_up, done = gather_group(links, order, (feed_gate, feed_up), done)
    down, done = gather_group(links, order, (feed_down,), done)
    w_query, w_key, w_value = qkv
    w_out, w_cross_query, w_cross_key, w_cross_value, w_cross_out = five
    w_gate, w_up = gate_up
    w_down = down[0]

    picks = (buckets[:, None] == jnp.arange(BUCKETS)[None, :]).astype(F32)
    offsets = jnp.dot(picks, table, precision=PRECISE).T

    normed_one, scale_one = norm_forward(hidden, gain_one)
    normed_one = normed_one.astype(BF16)
    query = matmul(normed_one, w_query).astype(BF16)
    keys = matmul(normed_one, w_key).astype(BF16)
    values = matmul(normed_one, w_value).astype(BF16)
    mixed_one, lse_one = attend_forward(lengths, offsets, query, keys, values)
    after_self = hidden + matmul(mixed_one, w_out)
    normed_two, scale_two = norm_forward(after_self, gain_two)
    normed_two = normed_two.astype(BF16)
    cross_queries = matmul(normed_two, w_cross_query).astype(BF16)
    memory_keys = matmul(memory, w_cross_key).astype(BF16)
    memory_values = matmul(memory, w_cross_value).astype(BF16)
    mixed_two, lse_two = attend_forward(lengths, None, cross_queries, memory_keys, memory_values)
    after_cross = after_self + matmul(mixed_two, w_cross_out)
    normed_three, scale_three = norm_forward(after_cross, gain_three)
    normed_three = normed_three.astype(BF16)
    gate = matmul(normed_three, w_gate)
    lift = matmul(normed_three, w_up)
    activated, gate_back = jax.vjp(smooth_gate, gate)
    inner = (activated * lift).astype(BF16)
    layer_out = (after_cross + matmul(inner, w_down)).astype(BF16)

    down_sum = reduce_group(links, back, *weight_grads(links, [inner], [cotangent]))
    inner_grad = matmul_nt(cotangent, w_down)
    gate_grad = gate_back(inner_grad * lift)[0].astype(BF16)
    lift_grad = (inner_grad * activated).astype(BF16)
    gate_up_sum = reduce_group(
        links, back, *weight_grads(links, [normed_three] * 2, [gate_grad, lift_grad])
    )
    normed_grad = matmul_nt(gate_grad, w_gate) + matmul_nt(lift_grad, w_up)
    residual_grad, gain_three_grad = norm_backward(after_cross, scale_three, gain_three, normed_grad)
    carried = cotangent.astype(F32) + residual_grad

    branch_two = carried.astype(BF16)
    mixed_two_grad = matmul_nt(branch_two, w_cross_out).astype(BF16)
    cross_queries_grad, memory_keys_grad, memory_values_grad = attend_backward(
        lengths, None, cross_queries, memory_keys, memory_values, mixed_two_grad, lse_two
    )
    memory_grad = matmul_nt(memory_keys_grad, w_cross_key) + matmul_nt(
        memory_values_grad, w_cross_value
    )
    normed_grad = matmul_nt(cross_queries_grad, w_cross_query)
    residual_grad, gain_two_grad = norm_backward(after_self, scale_two, gain_two, normed_grad)
    carried = carried + residual_grad
    branch_one = carried.astype(BF16)
    five_sum = reduce_group(
        links,
        back,
        *weight_grads(
            links,
            [mixed_two, normed_two, memory, memory, mixed_one],
            [branch_two, cross_queries_grad, memory_keys_grad, memory_values_grad, branch_one],
        ),
    )

    mixed_one_grad = matmul_nt(branch_one, w_out).astype(BF16)
    query_grad, keys_grad, values_grad, offset_grad = attend_backward(
        lengths, offsets, query, keys, values, mixed_one_grad, lse_one
    )
    qkv_sum = reduce_group(
        links,
        back,
        *weight_grads(links, [normed_one] * 3, [query_grad, keys_grad, values_grad]),
    )
    normed_grad = (
        matmul_nt(query_grad, w_query)
        + matmul_nt(keys_grad, w_key)
        + matmul_nt(values_grad, w_value)
    )
    residual_grad, gain_one_grad = norm_backward(hidden, scale_one, gain_one, normed_grad)
    input_grad = carried + residual_grad
    table_grad = jnp.dot(picks.T, offset_grad.reshape(HEADS, -1).T, precision=PRECISE)

    small = jnp.concatenate(
        [
            gain_one_grad.reshape(owners, -1),
            gain_two_grad.reshape(owners, -1),
            gain_three_grad.reshape(owners, -1),
            table_grad.reshape(owners, -1),
        ],
        axis=1,
    )
    small = sum_small(links, small)
    small = lax.dynamic_index_in_dim(small, links.owner, 0, keepdims=False)
    return (
        layer_out[None],
        input_grad[None],
        memory_grad[None],
        small[:share],
        qkv_sum[0],
        qkv_sum[1],
        qkv_sum[2],
        five_sum[4],
        small[3 * share :],
        small[share : 2 * share],
        five_sum[1],
        five_sum[2],
        five_sum[3],
        five_sum[0],
        small[2 * share : 3 * share],
        gate_up_sum[0],
        gate_up_sum[1],
        down_sum[0],
    )


def solution(mesh):
    rows = P(("rep", "fsdp"), None, None)
    vector = P("fsdp")
    matrix = P("fsdp", None)
    attention = (vector,) + (matrix,) * 4
    return jax.shard_map(
        functools.partial(on_device, mesh.shape["rep"], mesh.shape["fsdp"]),
        mesh=mesh,
        in_specs=(rows, rows, P(("rep", "fsdp")), P(), rows)
        + attention
        + (vector,)
        + attention
        + (vector, matrix, matrix, matrix),
        out_specs=(rows, rows, rows)
        + attention
        + (vector,)
        + attention
        + (vector, matrix, matrix, matrix),
        check_vma=False,
    )
```

```python
import functools
import jax
import jax.numpy as jnp
from jax import lax
from jax.experimental import pallas as pl
from jax.experimental.pallas import tpu as pltpu
from jax.sharding import PartitionSpec as P

HEADS = 12
HEAD = 64
BUCKETS = 32
EPSILON = 1e-06
MASKED = -1e30
PRECISE = lax.Precision.HIGHEST
MIB = 1024 * 1024
MICROSECOND = 5e8
F32 = jnp.float32
BF16 = jnp.bfloat16
NT = (((1,), (1,)), ((), ()))
NN = (((1,), (0,)), ((), ()))
TN = (((0,), (0,)), ((), ()))
TILE = 128


def dot(a, b, dims):
    return lax.dot_general(a, b, dims, preferred_element_type=F32)


def bias_tiles(offs, length):
    base = pltpu.roll(jnp.broadcast_to(offs, (TILE, length)), 0, 1, stride=1, stride_axis=0)
    return jnp.concatenate([base[:, length - TILE :], base], axis=1)


def diagonal_sums(spread, length):
    total = spread[:8]
    for at in range(8, TILE, 8):
        total = total + pltpu.roll(spread[at : at + 8], length - at, 1)
    row = lax.broadcasted_iota(jnp.int32, total.shape, 0)
    for bit in (1, 2, 4):
        total = jnp.where((row & bit) != 0, pltpu.roll(total, length - bit, 1), total)
    return jnp.sum(total, axis=0, keepdims=True)


def bias_block(tiles, first, rows, step):
    parts = []
    for block in range(rows // TILE):
        at = first - block * TILE + TILE
        parts.append(tiles[:, at : at + step])
    return jnp.concatenate(parts, axis=0)


def allowed(rows, step, first, length, causal):
    key = lax.broadcasted_iota(jnp.int32, (rows, step), 0)
    ok = key < length
    if causal:
        item = lax.broadcasted_iota(jnp.int32, (rows, step), 1) + first
        ok = ok & (key <= item)
    return ok


def forward_kernel(causal, lengths, *refs):
    if causal:
        offs_ref, q_ref, k_ref, v_ref, mixed_ref, lse_ref = refs
    else:
        q_ref, k_ref, v_ref, mixed_ref, lse_ref = refs
    q_ref, k_ref, v_ref = q_ref.at[0], k_ref.at[0], v_ref.at[0]
    size = q_ref.shape[0]
    step = 256
    length = lengths[0]
    for head in range(2):
        cols = slice(head * HEAD, (head + 1) * HEAD)
        if causal:
            tiles = bias_tiles(offs_ref[0, head : head + 1, :], size)
        for first in range(0, size, step):
            rows = first + step if causal else size
            scores = dot(k_ref[:rows, cols], q_ref[first : first + step, cols], NT)
            if causal:
                scores = scores + bias_block(tiles, first, rows, step)
            scores = jnp.where(allowed(rows, step, first, length, causal), scores, MASKED)
            highest = jnp.max(scores, axis=0, keepdims=True)
            weights = jnp.exp(scores - highest)
            total = jnp.sum(weights, axis=0, keepdims=True)
            mixed = dot(v_ref[:rows, cols], weights.astype(BF16), TN) * (1.0 / total)
            mixed_ref[first : first + step, cols] = mixed.T.astype(BF16)
            lse_ref[0, head : head + 1, first : first + step] = highest + jnp.log(total)


def backward_kernel(causal, lengths, core, *refs):
    if causal:
        offs_ref, q_ref, k_ref, v_ref, g_ref, lse_ref, grads_ref, doffs_ref = refs
    else:
        q_ref, k_ref, v_ref, g_ref, lse_ref, grads_ref = refs
    q_ref, k_ref, v_ref = q_ref.at[0], k_ref.at[0], v_ref.at[0]
    dq_ref, dk_ref, dv_ref = grads_ref.at[0], grads_ref.at[1], grads_ref.at[2]
    size = q_ref.shape[0]
    step = 256
    length = lengths[0]
    for head in range(2):
        cols = slice(head * HEAD, (head + 1) * HEAD)
        if causal:
            tiles = bias_tiles(offs_ref[0, head : head + 1, :], size)
            spread = [jnp.zeros((TILE, TILE), F32) for _ in range(size // TILE)]
        dk = [None] * (size // step)
        dv = [None] * (size // step)
        for first in range(0, size, step):
            rows = first + step if causal else size
            q = q_ref[first : first + step, cols]
            g = g_ref[first : first + step, cols]
            k = k_ref[:rows, cols]
            scores = dot(k, q, NT)
            if causal:
                scores = scores + bias_block(tiles, first, rows, step)
            scores = jnp.where(allowed(rows, step, first, length, causal), scores, MASKED)
            probs = jnp.exp(scores - lse_ref[0, head : head + 1, first : first + step])
            prob_grad = dot(v_ref[:rows, cols], g, NT)
            delta = jnp.sum(probs * prob_grad, axis=0, keepdims=True)
            score_grad = (probs * (prob_grad - delta)).astype(BF16)
            if causal:
                for block in range(rows // TILE):
                    for lane in range(step // TILE):
                        at = first // TILE + lane - block
                        if at >= 0:
                            spread[at] = spread[at] + score_grad[
                                block * TILE : (block + 1) * TILE, lane * TILE : (lane + 1) * TILE
                            ].astype(F32)
            dk_now = dot(score_grad, q, NN)
            dv_now = dot(probs.astype(BF16), g, NN)
            for block in range(rows // step):
                part = slice(block * step, (block + 1) * step)
                dk[block] = dk_now[part] if dk[block] is None else dk[block] + dk_now[part]
                dv[block] = dv_now[part] if dv[block] is None else dv[block] + dv_now[part]
            dq_ref[first : first + step, cols] = dot(k, score_grad, TN).T.astype(BF16)
        for block in range(size // step):
            part = slice(block * step, (block + 1) * step)
            dk_ref[part, cols] = dk[block].astype(BF16)
            dv_ref[part, cols] = dv[block].astype(BF16)
        if causal:
            doffs_ref[0, head : head + 1, :] = diagonal_sums(jnp.concatenate(spread, axis=1), size)


def full_spec(shape):
    zeros = (0,) * len(shape)
    return pl.BlockSpec(shape, lambda *_: zeros, pipeline_mode=pl.Buffered(1))


def rms(hidden, gain):
    scale = lax.rsqrt(jnp.mean(hidden * hidden, axis=-1, keepdims=True) + EPSILON)
    return hidden * scale * gain


def rms_backward(hidden, gain, upstream):
    scale = lax.rsqrt(jnp.mean(hidden * hidden, axis=-1, keepdims=True) + EPSILON)
    gain_grad = jnp.sum(upstream * (hidden * scale), axis=0, keepdims=True)
    weighted = upstream * gain
    inner = jnp.mean(weighted * hidden, axis=-1, keepdims=True)
    return scale * weighted - hidden * (scale * scale * scale) * inner, gain_grad


def half_at(core, other, width):
    return pl.multiple_of((1 - core if other else core) * width, width)


TICK = (8, 128)


def ticking(kernel, at, count, outputs, *refs):
    refs[outputs][...] = jnp.zeros(TICK, F32)
    kernel(*refs[:at], *refs[at + count : outputs], *refs[outputs + 1 :])


class Flow:
    def __init__(self):
        self.ticks = []

    def after(self, *arrays):
        self.ticks.extend(arrays)

    def call(self, kernel, name, scalars, grid, ins, outs, scratch=(), room=16, cost=1.0):
        count = len(scalars) + len(ins)
        late = len(self.ticks)
        *results, tick = pl.pallas_call(
            functools.partial(ticking, kernel, count, late, count + late + len(outs)),
            out_shape=tuple(jax.ShapeDtypeStruct(shape, kind) for shape, kind, _ in outs)
            + (jax.ShapeDtypeStruct(TICK, F32),),
            grid_spec=pltpu.PrefetchScalarGridSpec(
                num_scalar_prefetch=len(scalars),
                grid=grid,
                in_specs=[spec for _, spec in ins]
                + [
                    full_spec(item.shape) if item.size <= 2**14 else pl.BlockSpec(memory_space=pl.ANY)
                    for item in self.ticks
                ],
                out_specs=[spec for _, _, spec in outs] + [full_spec(TICK)],
                scratch_shapes=list(scratch),
            ),
            compiler_params=pltpu.CompilerParams(vmem_limit_bytes=room * MIB),
            cost_estimate=pl.CostEstimate(flops=int(cost * MICROSECOND), bytes_accessed=0, transcendentals=0),
            name=name,
        )(*scalars, *[array for array, _ in ins], *self.ticks)
        self.ticks = [tick]
        return results


def double_kernel(*refs):
    count = len(refs) // 3
    for one_ref, two_ref, out_ref in zip(refs[:count], refs[count : 2 * count], refs[2 * count :]):
        half = one_ref.shape[0]
        out_ref[:half] = one_ref[...]
        out_ref[half:] = two_ref[...]


def double(flow, pairs):
    shapes = [(2 * one.shape[0],) + one.shape[1:] for one, _ in pairs]
    return flow.call(
        double_kernel,
        "double",
        (),
        (1,),
        [whole(one) for one, _ in pairs] + [whole(two) for _, two in pairs],
        [(shape, BF16, full_spec(shape)) for shape in shapes],
    )


def halve_kernel(keep_one, keep_two, got_one, got_two, keep_ref, send_ref):
    keep_ref[...] = (keep_one[...].astype(F32) + got_one[...].astype(F32)).astype(BF16)
    send_ref[...] = (keep_two[...].astype(F32) + got_two[...].astype(F32)).astype(BF16)


def halve(flow, keep, got):
    half = keep.shape[0] // 2
    steps = min(half, 2)
    rest = keep.shape[1:]
    one = pl.BlockSpec((half // steps,) + rest, lambda i: (i, 0, 0, 0))
    two = pl.BlockSpec((half // steps,) + rest, lambda i: (steps + i, 0, 0, 0))
    out = ((half,) + rest, BF16, one)
    return flow.call(
        halve_kernel,
        "halve",
        (),
        (steps,),
        [(keep, one), (keep, two), (got, one), (got, two)],
        [out, out],
    )


def whole(array):
    return (array, full_spec(array.shape))


def query_kernel(core, hidden_ref, gain_ref, weight_ref, normed_ref, out_ref):
    @pl.when(pl.program_id(0) == 0)
    def _():
        normed_ref[...] = rms(hidden_ref[...].astype(F32), gain_ref[...]).astype(BF16)

    out_ref[0] = dot(normed_ref[...], weight_ref[0], NN).astype(BF16)


def query_step(flow, core, hidden, gain, weights):
    size, width = hidden.shape
    return flow.call(
        query_kernel,
        "query_step",
        (core,),
        (3,),
        [whole(hidden), whole(gain), (weights, pl.BlockSpec((1, width, width), lambda i, _: (i, 0, 0)))],
        [
            ((size, width), BF16, full_spec((size, width))),
            ((3, size, width), BF16, pl.BlockSpec((1, size, width), lambda i, _: (i, 0, 0))),
        ], cost=3)


def cross_kernel(core, mixed_ref, hidden_ref, memory_ref, gain_ref, weight_ref, after_ref, normed_ref, out_ref):
    step = pl.program_id(0)

    @pl.when(step == 0)
    def _():
        after = hidden_ref[...].astype(F32) + dot(mixed_ref[...], weight_ref[0], NN)
        after_ref[...] = after
        normed_ref[...] = rms(after, gain_ref[...]).astype(BF16)

    @pl.when(step == 1)
    def _():
        out_ref[0] = dot(normed_ref[...], weight_ref[0], NN).astype(BF16)

    @pl.when(step >= 2)
    def _():
        out_ref[0] = dot(memory_ref[...], weight_ref[0], NN).astype(BF16)


def cross_step(flow, core, mixed, hidden, memory, gain, weights):
    size, width = hidden.shape
    return flow.call(
        cross_kernel,
        "cross_step",
        (core,),
        (4,),
        [
            whole(mixed),
            whole(hidden),
            whole(memory),
            whole(gain),
            (weights, pl.BlockSpec((1, width, width), lambda i, _: (i, 0, 0))),
        ],
        [
            ((size, width), F32, full_spec((size, width))),
            ((size, width), BF16, full_spec((size, width))),
            (
                (3, size, width),
                BF16,
                pl.BlockSpec((1, size, width), lambda i, _: (jnp.maximum(i - 1, 0), 0, 0)),
            ),
        ], cost=5)


def out_kernel(core, mixed_ref, after_ref, gain_ref, weight_ref, out_ref, normed_ref):
    after = after_ref[...] + dot(mixed_ref[...], weight_ref[0], NN)
    out_ref[...] = after
    normed_ref[...] = rms(after, gain_ref[...]).astype(BF16)


def out_step(flow, core, mixed, after, gain, weights, at):
    size, width = mixed.shape
    return flow.call(
        out_kernel,
        "out_step",
        (core,),
        (1,),
        [
            whole(mixed),
            whole(after),
            whole(gain),
            (weights, pl.BlockSpec((1, width, width), lambda *_: (at, 0, 0))),
        ],
        [
            ((size, width), F32, full_spec((size, width))),
            ((size, width), BF16, full_spec((size, width))),
        ], cost=2.5)


def feed_tile(normed, cotangent, gate_w, up_w, down_w):
    gate = dot(normed, gate_w, NN)
    lift = dot(normed, up_w, NN)
    root = 0.7978845608028654
    square = gate * gate
    bend = jnp.tanh(root * gate * (1.0 + 0.044715 * square))
    half = 0.5 + 0.5 * bend
    active = gate * half
    slope = half + 0.5 * gate * (1.0 - bend * bend) * (root * (1.0 + 3 * 0.044715 * square))
    inner = (active * lift).astype(BF16)
    inner_grad = dot(cotangent, down_w, NT)
    gate_grad = (inner_grad * lift * slope).astype(BF16)
    lift_grad = (inner_grad * active).astype(BF16)
    out = dot(inner, down_w, NN)
    back = dot(gate_grad, gate_w, NT) + dot(lift_grad, up_w, NT)
    return inner, gate_grad, lift_grad, out, back


def feed_weights(half, gate_ref, up_ref, down_ref, down_w):
    start = pl.multiple_of(half * 128, 128)
    wide = []
    for ref in (gate_ref, up_ref):
        owners, _, _, rows, columns = ref.shape
        wide.append(
            jnp.concatenate(
                [
                    ref[:, 0, 0, :, pl.ds(start + at, 128)].reshape(owners * rows, 128)
                    for at in range(0, columns, 256)
                ],
                axis=1,
            )
        )
    for owner in range(2):
        for piece in range(2):
            for row in range(4):
                for column in range(6):
                    first = owner * 128 + piece * 64 + row * 16
                    down_w[first : first + 16, column * 128 : column * 128 + 128] = down_ref[
                        owner,
                        2 * half + piece,
                        0,
                        column * 16 : column * 16 + 16,
                        row * 128 : row * 128 + 128,
                    ]
    return wide[0], wide[1], down_w[...]


def feed_add(first, second, outs, values):
    step = pl.program_id(0)

    @pl.when(step == 0)
    def _():
        for ref, start, value in zip(outs, first, values):
            ref[...] = value if second is None else start[...] + value

    @pl.when(step > 0)
    def _():
        for ref, value in zip(outs, values):
            ref[...] += value


def feed_first_kernel(
    core, normed_ref, cot_ref, gate_ref, up_ref, down_ref, parts_ref, out_ref, back_ref, down_w
):
    weights = feed_weights(1 - core[0], gate_ref, up_ref, down_ref, down_w)
    inner, gate_grad, lift_grad, out, back = feed_tile(normed_ref[...], cot_ref[...], *weights)
    parts_ref[0] = inner
    parts_ref[1] = gate_grad
    parts_ref[2] = lift_grad
    feed_add((None, None), None, (out_ref, back_ref), (out, back))


def feed_second_kernel(
    core,
    normed_ref,
    cot_ref,
    gate_ref,
    up_ref,
    down_ref,
    out_in_ref,
    back_in_ref,
    after_ref,
    gain_ref,
    weight_ref,
    parts_ref,
    layer_ref,
    carry_ref,
    gain_grad_ref,
    other_ref,
    mine_ref,
    mixed_grad_ref,
    down_w,
    out_ref,
    back_ref,
    branch_ref,
):
    weights = feed_weights(core[0], gate_ref, up_ref, down_ref, down_w)
    inner, gate_grad, lift_grad, out, back = feed_tile(normed_ref[...], cot_ref[...], *weights)
    parts_ref[0] = inner
    parts_ref[1] = gate_grad
    parts_ref[2] = lift_grad
    feed_add((out_in_ref, back_in_ref), True, (out_ref, back_ref), (out, back))

    @pl.when(pl.program_id(0) == pl.num_programs(0) - 1)
    def _():
        after = after_ref[...]
        layer_ref[...] = (after + out_ref[...]).astype(BF16)
        residual, gain_grad = rms_backward(after, gain_ref[...], back_ref[...])
        gain_grad_ref[...] = gain_grad
        carry = cot_ref[...].astype(F32) + residual
        carry_ref[...] = carry
        branch_ref[...] = carry.astype(BF16)
        width = other_ref.shape[1]
        other_ref[...] = branch_ref[:, pl.ds(half_at(core[0], True, width), width)]
        mine_ref[...] = branch_ref[:, pl.ds(half_at(core[0], False, width), width)]
        mixed_grad_ref[...] = dot(branch_ref[...], weight_ref[0], NT).astype(BF16)


def feed_ins(normed, cotangent, weights):
    owners, pieces, _, rows, columns = weights.shape
    size = normed.shape[0]
    wide = [
        (
            weights,
            pl.BlockSpec(
                (owners, 1, 1, rows, columns), functools.partial(lambda at, i, _: (0, i, at, 0, 0), at)
            ),
        )
        for at in range(2)
    ]
    tall = (weights, pl.BlockSpec((2, pieces, 1, rows, columns), lambda i, _: (i, 0, 2, 0, 0)))
    units = pieces * columns // 2
    return (
        (owners // 2,),
        [whole(normed), whole(cotangent)] + wide + [tall],
        ((3, size, units), BF16, pl.BlockSpec((3, size, 256), lambda i, _: (0, 0, i))),
        pltpu.VMEM((256, normed.shape[1]), BF16),
    )


def feed_first(flow, core, normed, cotangent, weights):
    grid, ins, parts, scratch = feed_ins(normed, cotangent, weights)
    total = (normed.shape, F32, full_spec(normed.shape))
    return flow.call(
        feed_first_kernel, "feed_first", (core,), grid, ins, [parts, total, total], [scratch], room=28, cost=9
    )


def feed_second(flow, core, normed, cotangent, weights, out, back, after, gain, last, at):
    grid, ins, parts, scratch = feed_ins(normed, cotangent, weights)
    size, width = normed.shape
    ins = ins + [
        whole(out),
        whole(back),
        whole(after),
        whole(gain),
        (last, pl.BlockSpec((1, width, width), lambda *_: (at, 0, 0))),
    ]
    narrow = ((size, width // 2), BF16, full_spec((size, width // 2)))
    return flow.call(
        feed_second_kernel,
        "feed_second",
        (core,),
        grid,
        ins,
        [
            parts,
            ((size, width), BF16, full_spec((size, width))),
            ((size, width), F32, full_spec((size, width))),
            ((1, width), F32, full_spec((1, width))),
            narrow,
            narrow,
            ((size, width), BF16, full_spec((size, width))),
        ],
        [
            scratch,
            pltpu.VMEM((size, width), F32),
            pltpu.VMEM((size, width), F32),
            pltpu.VMEM((size, width), BF16),
        ],
        room=44,
        cost=11,
    )


def back_product(core, others, mines, weight_ref, at):
    width = others.shape[-1]
    return dot(
        others[at], weight_ref[0, :, pl.ds(half_at(core[0], True, width), width)], NT
    ) + dot(mines[at], weight_ref[0, :, pl.ds(half_at(core[0], False, width), width)], NT)


def middle_kernel(
    core,
    others,
    mines,
    after_ref,
    gain_ref,
    carry_in_ref,
    query_ref,
    weight_ref,
    carry_ref,
    gain_grad_ref,
    other_ref,
    mine_ref,
    mixed_grad_ref,
    branch_ref,
):
    back = back_product(core, others, mines, query_ref, 0)
    residual, gain_grad = rms_backward(after_ref[...], gain_ref[...], back)
    gain_grad_ref[...] = gain_grad
    carry = carry_in_ref[...] + residual
    carry_ref[...] = carry
    branch_ref[...] = carry.astype(BF16)
    width = other_ref.shape[1]
    other_ref[...] = branch_ref[:, pl.ds(half_at(core[0], True, width), width)]
    mine_ref[...] = branch_ref[:, pl.ds(half_at(core[0], False, width), width)]
    mixed_grad_ref[...] = dot(branch_ref[...], weight_ref[0], NT).astype(BF16)


def middle_step(flow, core, others, mines, after, gain, carry, weights, query_at, out_at):
    size, width = after.shape
    narrow = ((size, width // 2), BF16, full_spec((size, width // 2)))
    return flow.call(
        middle_kernel,
        "middle_step",
        (core,),
        (1,),
        [
            whole(others),
            whole(mines),
            whole(after),
            whole(gain),
            whole(carry),
            (weights, pl.BlockSpec((1, width, width), lambda *_: (query_at, 0, 0))),
            (weights, pl.BlockSpec((1, width, width), lambda *_: (out_at, 0, 0))),
        ],
        [
            ((size, width), F32, full_spec((size, width))),
            ((1, width), F32, full_spec((1, width))),
            narrow,
            narrow,
            ((size, width), BF16, full_spec((size, width))),
        ],
        [pltpu.VMEM((size, width), BF16)], cost=3)


def memory_kernel(core, others, mines, key_ref, value_ref, out_ref):
    out_ref[...] = back_product(core, others, mines, key_ref, 1) + back_product(
        core, others, mines, value_ref, 2
    )


def memory_step(flow, core, others, mines, weights, at):
    size, width = others.shape[1], weights.shape[2]
    return flow.call(
        memory_kernel,
        "memory_step",
        (core,),
        (1,),
        [
            whole(others),
            whole(mines),
            (weights, pl.BlockSpec((1, width, width), lambda *_: (at, 0, 0))),
            (weights, pl.BlockSpec((1, width, width), lambda *_: (at + 1, 0, 0))),
        ],
        [((size, width), F32, full_spec((size, width)))], cost=3)[0]


def last_kernel(core, others, mines, hidden_ref, gain_ref, carry_ref, w_one, w_two, w_three, out_ref, gain_grad_ref):
    back = (
        back_product(core, others, mines, w_one, 0)
        + back_product(core, others, mines, w_two, 1)
        + back_product(core, others, mines, w_three, 2)
    )
    residual, gain_grad = rms_backward(hidden_ref[...].astype(F32), gain_ref[...], back)
    gain_grad_ref[...] = gain_grad
    out_ref[...] = carry_ref[...] + residual


def last_step(flow, core, others, mines, hidden, gain, carry, weights):
    size, width = hidden.shape
    return flow.call(
        last_kernel,
        "last_step",
        (core,),
        (1,),
        [whole(others), whole(mines), whole(hidden), whole(gain), whole(carry)]
        + [
            (weights, pl.BlockSpec((1, width, width), functools.partial(lambda at, *_: (at, 0, 0), at)))
            for at in range(3)
        ],
        [
            ((size, width), F32, full_spec((size, width))),
            ((1, width), F32, full_spec((1, width))),
        ], cost=5.5)


def take(array, part):
    return array[...] if part is None else array[part]


def weight_grads_kernel(plan, row_count, grad_count, picks, *refs):
    rows, rows_got = refs[:row_count], refs[row_count : 2 * row_count]
    refs = refs[2 * row_count :]
    grads, grads_got = refs[:grad_count], refs[grad_count : 2 * grad_count]
    keep_ref, send_ref, total_ref = refs[2 * grad_count :]
    half, tall = keep_ref.shape[0], keep_ref.shape[2]
    for at, (row, row_part, grad, part) in enumerate(plan):
        total = dot(take(rows[row], row_part), take(grads[grad], part), TN)
        total = total + dot(take(rows_got[row], row_part), take(grads_got[grad], part), TN)
        total_ref[...] = total.astype(BF16).reshape(total_ref.shape)
        for place in range(half):
            keep_ref[place, at] = total_ref[picks[place]]
            send_ref[place, at] = total_ref[picks[half + place]]


def weight_grads(links, flow, order, plan, rows, rows_got, grads, grads_got):
    picks = links.places(links.core, order[::-1])
    count = 2 * links.owners
    height = rows[plan[0][0]].shape[-1]
    columns = grads[plan[0][2]].shape[-1]
    tall = height // count
    if tall % 16 == 0:
        shape = (count // 2, len(plan), tall, columns)
        return flow.call(
            functools.partial(weight_grads_kernel, plan, len(rows), len(grads)),
            "weight_grads",
            (picks,),
            (1,),
            [whole(item) for item in (*rows, *rows_got, *grads, *grads_got)],
            [(shape, BF16, full_spec(shape)), (shape, BF16, full_spec(shape))],
            [pltpu.VMEM((count, tall, columns), BF16)],
            room=24, cost=5)
    stack = []
    for row, row_part, grad, part in plan:
        total = dot(take(rows[row], row_part), take(grads[grad], part), TN)
        total = total + dot(take(rows_got[row], row_part), take(grads_got[grad], part), TN)
        stack.append(total.astype(BF16).reshape(count, tall, columns))
    stack = jnp.stack(stack, axis=1)[picks]
    return stack[: count // 2], stack[count // 2 :]


def attend_forward(flow, lengths, offs, stack):
    causal = offs is not None
    _, size, width = stack.shape
    pairs = HEADS // 2

    def part(at):
        return (stack, pl.BlockSpec((1, size, 2 * HEAD), lambda p, *_: (at, 0, p)))

    lanes = pl.BlockSpec((1, 2, size), lambda p, *_: (p, 0, 0))
    ins = [part(0), part(1), part(2)]
    if causal:
        ins = [(offs, lanes)] + ins
    return flow.call(
        functools.partial(forward_kernel, causal),
        "attend_forward_self" if causal else "attend_forward_cross",
        (lengths,),
        (pairs,),
        ins,
        [
            ((size, width), BF16, pl.BlockSpec((size, 2 * HEAD), lambda p, *_: (0, p))),
            ((pairs, 2, size), F32, lanes),
        ],
        cost=11,
    )


def attend_backward(flow, lengths, core, other, offs, stack, g, lse):
    causal = offs is not None
    _, size, width = stack.shape
    pairs = HEADS // 4

    def pair(p, core):
        return (1 - core[0] if other else core[0]) * pairs + p

    def part(at):
        return (stack, pl.BlockSpec((1, size, 2 * HEAD), lambda p, _, core: (at, 0, pair(p, core))))

    lanes = pl.BlockSpec((1, 2, size), lambda p, _, core: (pair(p, core), 0, 0))
    ins = [part(0), part(1), part(2)]
    ins = ins + [(g, pl.BlockSpec((size, 2 * HEAD), lambda p, _, core: (0, pair(p, core)))), (lse, lanes)]
    outs = [((3, size, width // 2), BF16, pl.BlockSpec((3, size, 2 * HEAD), lambda p, *_: (0, 0, p)))]
    if causal:
        ins = [(offs, lanes)] + ins
        outs = outs + [((pairs, 2, size), F32, pl.BlockSpec((1, 2, size), lambda p, *_: (p, 0, 0)))]
    return flow.call(
        functools.partial(backward_kernel, causal),
        "attend_backward_self" if causal else "attend_backward_cross",
        (lengths, core),
        (pairs,),
        ins,
        outs,
        cost=8,
    )


class Links:
    def __init__(self, reps, owners, width):
        self.owners = owners
        self.width = width
        self.bits = owners.bit_length() - 1
        self.count = reps * owners
        self.rep = lax.axis_index("rep")
        self.owner = lax.axis_index("fsdp")
        self.core = self.rep % 2
        self.side = self.rep // 2
        self.core_word = self.core.reshape(1).astype(jnp.int32)
        self.side_word = self.side.reshape(1).astype(jnp.int32)

    def move(self, array, target):
        return lax.ppermute(
            array, ("rep", "fsdp"), [(device, target(device)) for device in range(self.count)]
        )

    def over_owner(self, array, bit):
        return self.move(array, lambda device: device ^ (1 << bit))

    def over_core(self, array):
        return self.move(array, lambda device: device ^ self.owners)

    def over_side(self, array):
        return self.move(array, lambda device: device ^ (2 * self.owners))

    def over_pair(self, array, first):
        def target(device):
            core = (device // self.owners) % 2
            return device ^ (1 if (core == 0) == first else 2 * self.owners)

        return self.move(array, target)

    def step(self, array, name):
        if name == "first":
            return self.over_pair(array, True)
        if name == "second":
            return self.over_pair(array, False)
        return self.over_owner(array, name)

    def far_to_near(self):
        return tuple(range(self.bits - 1, 0, -1))

    def places(self, core, order):
        index = jnp.arange(2 * self.owners)
        owner = jnp.full_like(index, self.owner)
        side = jnp.full_like(index, self.side)
        for at, name in enumerate(order):
            flip = (index >> at) & 1
            if name == "first":
                owner = owner ^ jnp.where(core == 0, flip, 0)
                side = side ^ jnp.where(core == 0, 0, flip)
            elif name == "second":
                owner = owner ^ jnp.where(core == 0, 0, flip)
                side = side ^ jnp.where(core == 0, flip, 0)
            else:
                owner = owner ^ (flip << name)
        return (owner * 2 + side).astype(jnp.int32)


def assemble_kernel(places, core, *refs):
    sources, out_ref, sems = refs[:2], refs[2], refs[3]
    width = sources[0].shape[-1]
    copies = []
    for half in range(2):
        column = core[0] if half == 0 else 1 - core[0]
        start = pl.multiple_of(column * width, width)
        tall = out_ref.shape[-1] == width
        for at in range(sources[half].shape[0]):
            copies.append(
                pltpu.make_async_copy(
                    sources[half].at[at],
                        out_ref.at[pl.ds(column, 1), places[half, at]]
                        if tall
                        else out_ref.at[:, places[half, at], :, pl.ds(start, width)],
                    sems.at[half, at],
                )
            )
    for copy in copies:
        copy.start()
    for copy in copies:
        copy.wait()


def assemble(links, flow, order, own, other, tall=False):
    places = jnp.stack([links.places(links.core, order), links.places(1 - links.core, order)])
    count, weights, rows, columns = own.shape
    if tall:
        shape = (2, count, rows, columns)
    else:
        shape = (weights, count, rows, 2 * columns)
    out = flow.call(
        assemble_kernel,
        "assemble",
        (places, links.core_word),
        (1,),
        [whole(own), whole(other)],
        [(shape, BF16, full_spec(shape))],
        [pltpu.SemaphoreType.DMA((2, count))],
        room=20,
        cost=3.5,
    )[0]
    if tall:
        return out.reshape(2 * count * rows, columns)
    return out.reshape(weights, count * rows, 2 * columns)


def pack_kernel(counts, core, *refs):
    total = sum(counts)
    shards, blocks, sems = refs[:total], refs[total:-1], refs[-1]
    copies = []
    for count, block in zip(counts, blocks):
        high, wide = block.shape[2], block.shape[3]
        rows = pl.ds(pl.multiple_of(core[1] * high, high), high)
        columns = pl.ds(pl.multiple_of(core[0] * wide, wide), wide)
        for index in range(count):
            copies.append(
                pltpu.make_async_copy(
                    shards[len(copies)].at[rows, columns], block.at[0, index], sems.at[len(copies)]
                )
            )
    for copy in copies:
        copy.start()
    for copy in copies:
        copy.wait()


def pack(links, flow, groups):
    high, wide = groups[0][0].shape
    high, wide = high // 2, wide // 2
    counts = [len(group) for group in groups]
    if high % 16 == 0:
        shapes = [(1, count, high, wide) for count in counts]
        return flow.call(
            functools.partial(pack_kernel, counts),
            "pack",
            (jnp.stack([links.core, links.side]).astype(jnp.int32),),
            (1,),
            [(shard, pl.BlockSpec(memory_space=pl.ANY)) for group in groups for shard in group],
            [(shape, BF16, full_spec(shape)) for shape in shapes],
            [pltpu.SemaphoreType.DMA((sum(counts),))],
        )
    at = (links.side * high, links.core * wide)
    return [
        jnp.stack([lax.dynamic_slice(shard, at, (high, wide)) for shard in group])[None] for group in groups
    ]


def gather_feed(links, reps, gate, up, down):
    owners = links.owners
    share, units = gate.shape
    wide = units // reps
    high, width = down.shape
    high = high // reps
    gate = lax.dynamic_slice_in_dim(gate, links.rep * wide, wide, 1)
    up = lax.dynamic_slice_in_dim(up, links.rep * wide, wide, 1)
    down = lax.dynamic_slice_in_dim(down, links.rep * high, high, 0)
    fine = share == width // 8
    if fine:
        down = down.reshape(wide // 128, 16, share // 16, 128).transpose(2, 1, 0, 3)
    down = down.reshape(share, wide)
    full = lax.all_gather(jnp.stack([gate, up, down]), ("fsdp", "rep"), axis=0)
    full = full.reshape(owners, reps, 3, share, wide)
    if fine:
        return full
    half = units // owners // 2
    parts = []
    for at in range(2):
        part = full[:, :, at].transpose(0, 2, 1, 3).reshape(width, 8, owners // 8, 2, half)
        part = part.transpose(0, 1, 3, 2, 4).reshape(8, width // 8, reps, wide)
        parts.append(part.transpose(0, 2, 1, 3))
    down = full[:, :, 2].reshape(8, owners // 8, 2, half, width).transpose(0, 2, 1, 3, 4)
    down = down.reshape(8, reps, wide // 128, 16, width // 128, 128).transpose(0, 1, 4, 3, 2, 5)
    parts.append(down.reshape(8, reps, width // 8, wide))
    return jnp.stack(parts, axis=2)


class Reduce:
    def __init__(self, links, flow, order, keep, send, tall=False):
        self.links, self.flow, self.order, self.tall = links, flow, order, tall
        self.keep, self.send = keep, send
        self.taken = 0
        self.start()

    def start(self):
        self.got = self.links.step(self.send, self.order[self.taken])
        self.taken += 1

    def advance(self):
        if self.taken < len(self.order):
            self.keep, self.send = halve(self.flow, self.keep, self.got)
            self.start()

    def sides(self):
        while self.taken < len(self.order):
            self.advance()
        mine = add(self.flow, self.keep, self.got)
        self.keep, self.got = mine, self.links.over_side(mine)

    def cores(self):
        mine = stack(self.flow, self.links.side_word, self.keep, self.got)
        self.keep, self.got = mine, self.links.over_core(mine)

    def outs(self):
        return unpack(self.flow, self.links, self.keep, self.got, self.tall)


def add_kernel(one_ref, two_ref, out_ref):
    out_ref[...] = (one_ref[0].astype(F32) + two_ref[0].astype(F32)).astype(BF16)


def add(flow, one, two):
    shape = one.shape[1:]
    return flow.call(
        add_kernel, "add", (), (1,), [whole(one), whole(two)], [(shape, BF16, full_spec(shape))]
    )[0]


def stack_kernel(first, one_ref, two_ref, out_ref):
    out_ref[:, pl.ds(first[0], 1)] = one_ref[...][:, None]
    out_ref[:, pl.ds(1 - first[0], 1)] = two_ref[...][:, None]


def stack(flow, first, one, two):
    weights, rows, columns = one.shape
    shape = (weights, 2, rows, columns)
    out = flow.call(
        stack_kernel,
        "stack",
        (first,),
        (1,),
        [whole(one), whole(two)],
        [(shape, BF16, full_spec(shape))],
    )[0]
    return out.reshape(weights, 2 * rows, columns)


def unpack_kernel(tall, owners, core, one_ref, two_ref, *out_refs):
    for index, out_ref in enumerate(out_refs):
        for half, ref in enumerate((one_ref, two_ref)):
            at = core[0] if half == 0 else 1 - core[0]
            value = ref[index].astype(F32)
            rows, columns = value.shape
            parts = owners if columns % (owners * 128) == 0 else 1
            wide = columns // parts
            if tall:
                out_ref[pl.ds(pl.multiple_of(at * rows, rows), rows)] = value
            else:
                for part in range(parts):
                    start = pl.multiple_of((2 * part + at) * wide, wide)
                    out_ref[:, pl.ds(start, wide)] = value[:, part * wide : (part + 1) * wide]


def unpack(flow, links, one, two, tall):
    weights, rows, columns = one.shape
    if rows % 16:
        first = links.core == 0
        one, two = jnp.where(first, one, two), jnp.where(first, two, one)
        if tall:
            mine = jnp.concatenate([one, two], axis=1)
        elif 2 * columns > links.width:
            mine = jnp.stack([one, two], axis=2).reshape(weights, rows, 2, links.owners, -1)
            mine = mine.transpose(0, 1, 3, 2, 4).reshape(weights, rows, 2 * columns)
        else:
            mine = jnp.concatenate([one, two], axis=2)
        return list(mine.astype(F32))
    shape = (2 * rows, columns) if tall else (rows, 2 * columns)
    return flow.call(
        functools.partial(unpack_kernel, tall, links.owners),
        "unpack",
        (links.core_word,),
        (1,),
        [whole(one), whole(two)],
        [(shape, F32, full_spec(shape))] * weights,
    )


def pack_small_kernel(*refs):
    out_ref = refs[-1]
    for index, ref in enumerate(refs[:-1]):
        out_ref[index : index + 1, : ref.shape[1]] = ref[...]


def pack_small(flow, vectors):
    width = max(item.shape[1] for item in vectors)
    shape = (8, width)
    return flow.call(
        pack_small_kernel, "pack_small", (), (1,), [whole(item) for item in vectors], [(shape, F32, full_spec(shape))]
    )[0]


def on_device(
    reps,
    owners,
    hidden,
    memory,
    lengths,
    buckets,
    cotangent,
    self_gain,
    self_query,
    self_key,
    self_value,
    self_out,
    bias_table,
    cross_gain,
    cross_query,
    cross_key,
    cross_value,
    cross_out,
    feed_gain,
    feed_gate,
    feed_up,
    feed_down,
):
    width = hidden.shape[2]
    share = width // owners
    links = Links(reps, owners, width)
    hidden, memory, cotangent = hidden[0], memory[0], cotangent[0]
    flow = Flow()
    core = links.core_word
    far = links.far_to_near()
    order = far + ("first", "second")
    w_feed = gather_feed(links, reps, feed_gate, feed_up, feed_down)
    small = jnp.concatenate([self_gain, cross_gain, feed_gain, bias_table])[None]
    bits = list(range(links.bits - 1, -1, -1))
    a, b = pack(
        links,
        flow,
        (
            (self_query, self_key, self_value),
            (self_out, cross_query, cross_key, cross_value, cross_out),
        ),
    )
    for at, name in enumerate(order[:-1]):
        pairs = [(a, links.step(a, name))]
        if at > 0:
            pairs.append((b, links.step(b, order[at - 1])))
        if bits:
            tiny = links.over_owner(small, bits.pop(0))
            flow.after(tiny)
            small = jnp.concatenate([small, tiny], axis=0)
        if at > 0:
            a, b = double(flow, pairs)
        else:
            (a,) = double(flow, pairs)
    apart = jnp.arange(owners) ^ links.owner
    place = sum(((apart >> bit) & 1) << (links.bits - 1 - bit) for bit in range(links.bits))
    small = small[place].astype(F32)
    gain_one = small[:, :share].reshape(1, -1)
    gain_two = small[:, share : 2 * share].reshape(1, -1)
    gain_three = small[:, 2 * share : 3 * share].reshape(1, -1)
    table = small[:, 3 * share :].reshape(BUCKETS, HEADS)
    picks = (buckets[:, None] == jnp.arange(BUCKETS)[None, :]).astype(F32)
    offsets = jnp.dot(picks, table, precision=PRECISE).T.reshape(HEADS // 2, 2, -1)

    memory_got = links.over_core(memory)
    (a,) = double(flow, [(a, links.step(a, order[-1]))])
    flow.after(memory_got)
    cotangent_got = links.over_core(cotangent)
    b_got = links.step(b, order[-2])
    w_self = assemble(links, flow, order, a, links.over_core(a))
    flow.after(cotangent_got)
    normed_one, qkv = query_step(flow, core, hidden, gain_one, w_self)
    normed_one_got = links.over_core(normed_one)
    (b,) = double(flow, [(b, b_got)])
    b_got = links.step(b, order[-1])
    mixed_one, lse_one = attend_forward(flow, lengths, offsets, qkv)
    mixed_one_got = links.over_core(mixed_one)
    flow.after(normed_one_got)
    (b,) = double(flow, [(b, b_got)])
    flow.after(mixed_one_got)
    w_cross = assemble(links, flow, order, b, links.over_core(b))
    after_self, normed_two, cross_qkv = cross_step(
        flow, core, mixed_one, hidden, memory, gain_two, w_cross
    )
    normed_two_got = links.over_core(normed_two)
    mixed_two, lse_two = attend_forward(flow, lengths, None, cross_qkv)
    mixed_two_got = links.over_core(mixed_two)
    flow.after(normed_two_got)
    after_cross, normed_three = out_step(flow, core, mixed_two, after_self, gain_three, w_cross, 4)
    normed_three_got = links.over_core(normed_three)
    flow.after(mixed_two_got, normed_three_got)
    parts_other, out, back = feed_first(flow, core, normed_three, cotangent, w_feed)
    parts_got = links.over_core(parts_other)
    (
        parts,
        layer_out,
        carry_two,
        gain_three_grad,
        branch_other,
        branch_two,
        mixed_grad,
    ) = feed_second(
        flow,
        core,
        normed_three,
        cotangent,
        w_feed,
        out,
        back,
        after_cross,
        gain_three,
        w_cross,
        4,
    )
    branch_two_got = links.over_core(branch_other)

    down = order[::-1]
    sums_d = Reduce(
        links,
        flow,
        down,
        *weight_grads(
            links,
            flow,
            down,
            [(0, 0, 0, None)],
            [parts],
            [parts_got],
            [cotangent],
            [cotangent_got],
        ),
        tall=True,
    )
    sums_c = Reduce(
        links,
        flow,
        down,
        *weight_grads(
            links,
            flow,
            down,
            [(0, None, 0, 1), (0, None, 0, 2)],
            [normed_three],
            [normed_three_got],
            [parts],
            [parts_got],
        ),
    )
    (cross_other,) = attend_backward(flow, lengths, core, True, None, cross_qkv, mixed_grad, lse_two)
    cross_got = links.over_core(cross_other)
    sums_d.advance()
    flow.after(branch_two_got)
    (cross_mine,) = attend_backward(flow, lengths, core, False, None, cross_qkv, mixed_grad, lse_two)
    sums_d.advance()
    carry_one, gain_two_grad, branch_other, branch_one, mixed_grad = middle_step(
        flow, core, cross_other, cross_mine, after_self, gain_two, carry_two, w_cross, 1, 0
    )
    branch_one_got = links.over_core(branch_other)
    sums_c.advance()
    sums_d.advance()
    sums_b = Reduce(
        links,
        flow,
        down,
        *weight_grads(
            links,
            flow,
            down,
            [
                (0, None, 0, None),
                (1, None, 1, 0),
                (2, None, 1, 1),
                (2, None, 1, 2),
                (3, None, 2, None),
            ],
            [mixed_one, normed_two, memory, mixed_two],
            [mixed_one_got, normed_two_got, memory_got, mixed_two_got],
            [branch_one, cross_mine, branch_two],
            [branch_one_got, cross_got, branch_two_got],
        ),
    )
    self_other, offsets_other = attend_backward(
        flow, lengths, core, True, offsets, qkv, mixed_grad, lse_one
    )
    self_got = links.over_core(self_other)
    sums_c.advance()
    sums_d.advance()
    self_mine, offsets_mine = attend_backward(
        flow, lengths, core, False, offsets, qkv, mixed_grad, lse_one
    )
    sums_a = Reduce(
        links,
        flow,
        down,
        *weight_grads(
            links,
            flow,
            down,
            [(0, None, 0, 0), (0, None, 0, 1), (0, None, 0, 2)],
            [normed_one],
            [normed_one_got],
            [self_mine],
            [self_got],
        ),
    )
    sums_b.advance()
    sums_c.advance()
    input_grad, gain_one_grad = last_step(
        flow, core, self_other, self_mine, hidden, gain_one, carry_one, w_self
    )
    first = links.core == 0
    offset_grad = jnp.concatenate(
        [
            jnp.where(first, offsets_mine, offsets_other),
            jnp.where(first, offsets_other, offsets_mine),
        ],
        axis=0,
    ).reshape(HEADS, -1)
    table_grad = jnp.dot(picks.T, offset_grad.T, precision=PRECISE).reshape(1, -1)
    sums_a.advance()
    small = pack_small(flow, [gain_one_grad, gain_two_grad, gain_three_grad, table_grad])
    small = small + links.over_core(small)
    small = small + links.over_side(small)
    for bit in range(links.bits):
        small = small + links.over_owner(small, bit)
    sums_d.sides()
    sums_b.advance()
    sums_c.sides()
    memory_grad = memory_step(flow, core, cross_other, cross_mine, w_cross, 2)
    sums_a.advance()
    sums_d.cores()
    sums_b.advance()
    sums_c.cores()
    (total_d,) = sums_d.outs()
    sums_a.advance()
    sums_b.sides()
    sums_a.sides()
    total_c = sums_c.outs()
    sums_a.cores()
    sums_b.cores()
    total_a = sums_a.outs()
    total_b = sums_b.outs()
    small_table = lax.dynamic_slice_in_dim(
        small[3], links.owner * bias_table.shape[0], bias_table.shape[0], 0
    )
    small = lax.dynamic_slice_in_dim(small, links.owner * share, share, 1)
    return (
        layer_out[None],
        input_grad[None],
        memory_grad[None],
        small[0],
        total_a[0],
        total_a[1],
        total_a[2],
        total_b[0],
        small_table,
        small[1],
        total_b[1],
        total_b[2],
        total_b[3],
        total_b[4],
        small[2],
        total_c[0],
        total_c[1],
        total_d,
    )


def solution(mesh):
    rows = P(("rep", "fsdp"), None, None)
    vector = P("fsdp")
    matrix = P("fsdp", None)
    attention = (vector,) + (matrix,) * 4
    return jax.shard_map(
        functools.partial(on_device, mesh.shape["rep"], mesh.shape["fsdp"]),
        mesh=mesh,
        in_specs=(rows, rows, P(("rep", "fsdp")), P(), rows)
        + attention
        + (vector,)
        + attention
        + (vector, matrix, matrix, matrix),
        out_specs=(rows, rows, rows)
        + attention
        + (vector,)
        + attention
        + (vector, matrix, matrix, matrix),
        check_vma=False,
    )
```

```python
import functools
import jax
import jax.numpy as jnp
from jax import lax
from jax.experimental import pallas as pl
from jax.experimental.pallas import tpu as pltpu
from jax.sharding import PartitionSpec as P

HEADS = 12
HEAD = 64
BUCKETS = 32
EPSILON = 1e-06
MASKED = -1e30
PRECISE = lax.Precision.HIGHEST
MIB = 1024 * 1024
MICROSECOND = 1e9
F32 = jnp.float32
BF16 = jnp.bfloat16
NT = (((1,), (1,)), ((), ()))
NN = (((1,), (0,)), ((), ()))
TN = (((0,), (0,)), ((), ()))
TILE = 128


def dot(a, b, dims):
    return lax.dot_general(a, b, dims, preferred_element_type=F32)


def bias_tiles(offs, length):
    base = pltpu.roll(jnp.broadcast_to(offs, (TILE, length)), 0, 1, stride=1, stride_axis=0)
    return jnp.concatenate([base[:, length - TILE :], base], axis=1)


def diagonal_sums(spread, length):
    total = spread[:8]
    for at in range(8, TILE, 8):
        total = total + pltpu.roll(spread[at : at + 8], length - at, 1)
    row = lax.broadcasted_iota(jnp.int32, total.shape, 0)
    for bit in (1, 2, 4):
        total = jnp.where((row & bit) != 0, pltpu.roll(total, length - bit, 1), total)
    return jnp.sum(total, axis=0, keepdims=True)


def bias_block(tiles, first, rows, step):
    parts = []
    for block in range(rows // TILE):
        at = first - block * TILE + TILE
        parts.append(tiles[:, at : at + step])
    return jnp.concatenate(parts, axis=0)


def allowed(rows, step, first, length, causal):
    key = lax.broadcasted_iota(jnp.int32, (rows, step), 0)
    ok = key < length
    if causal:
        item = lax.broadcasted_iota(jnp.int32, (rows, step), 1) + first
        ok = ok & (key <= item)
    return ok


def forward_kernel(causal, lengths, *refs):
    if causal:
        offs_ref, q_ref, k_ref, v_ref, mixed_ref, lse_ref = refs
    else:
        q_ref, k_ref, v_ref, mixed_ref, lse_ref = refs
    q_ref, k_ref, v_ref = q_ref.at[0], k_ref.at[0], v_ref.at[0]
    size = q_ref.shape[0]
    step = 256
    length = lengths[0]
    for head in range(2):
        cols = slice(head * HEAD, (head + 1) * HEAD)
        if causal:
            tiles = bias_tiles(offs_ref[0, head : head + 1, :], size)
        for first in range(0, size, step):
            rows = first + step if causal else size
            scores = dot(k_ref[:rows, cols], q_ref[first : first + step, cols], NT)
            if causal:
                scores = scores + bias_block(tiles, first, rows, step)
            scores = jnp.where(allowed(rows, step, first, length, causal), scores, MASKED)
            highest = jnp.max(scores, axis=0, keepdims=True)
            weights = jnp.exp(scores - highest)
            total = jnp.sum(weights, axis=0, keepdims=True)
            mixed = dot(v_ref[:rows, cols], weights.astype(BF16), TN) * (1.0 / total)
            mixed_ref[first : first + step, cols] = mixed.T.astype(BF16)
            lse_ref[0, head : head + 1, first : first + step] = highest + jnp.log(total)


def backward_kernel(causal, lengths, core, *refs):
    if causal:
        offs_ref, q_ref, k_ref, v_ref, g_ref, lse_ref, grads_ref, doffs_ref = refs
    else:
        q_ref, k_ref, v_ref, g_ref, lse_ref, grads_ref = refs
    q_ref, k_ref, v_ref = q_ref.at[0], k_ref.at[0], v_ref.at[0]
    dq_ref, dk_ref, dv_ref = grads_ref.at[0], grads_ref.at[1], grads_ref.at[2]
    size = q_ref.shape[0]
    step = 256
    length = lengths[0]
    for head in range(2):
        cols = slice(head * HEAD, (head + 1) * HEAD)
        if causal:
            tiles = bias_tiles(offs_ref[0, head : head + 1, :], size)
            spread = [jnp.zeros((TILE, TILE), F32) for _ in range(size // TILE)]
        dk = [None] * (size // step)
        dv = [None] * (size // step)
        for first in range(0, size, step):
            rows = first + step if causal else size
            q = q_ref[first : first + step, cols]
            g = g_ref[first : first + step, cols]
            k = k_ref[:rows, cols]
            scores = dot(k, q, NT)
            if causal:
                scores = scores + bias_block(tiles, first, rows, step)
            scores = jnp.where(allowed(rows, step, first, length, causal), scores, MASKED)
            probs = jnp.exp(scores - lse_ref[0, head : head + 1, first : first + step])
            prob_grad = dot(v_ref[:rows, cols], g, NT)
            delta = jnp.sum(probs * prob_grad, axis=0, keepdims=True)
            score_grad = (probs * (prob_grad - delta)).astype(BF16)
            if causal:
                for block in range(rows // TILE):
                    for lane in range(step // TILE):
                        at = first // TILE + lane - block
                        if at >= 0:
                            spread[at] = spread[at] + score_grad[
                                block * TILE : (block + 1) * TILE, lane * TILE : (lane + 1) * TILE
                            ].astype(F32)
            dk_now = dot(score_grad, q, NN)
            dv_now = dot(probs.astype(BF16), g, NN)
            for block in range(rows // step):
                part = slice(block * step, (block + 1) * step)
                dk[block] = dk_now[part] if dk[block] is None else dk[block] + dk_now[part]
                dv[block] = dv_now[part] if dv[block] is None else dv[block] + dv_now[part]
            dq_ref[first : first + step, cols] = dot(k, score_grad, TN).T.astype(BF16)
        for block in range(size // step):
            part = slice(block * step, (block + 1) * step)
            dk_ref[part, cols] = dk[block].astype(BF16)
            dv_ref[part, cols] = dv[block].astype(BF16)
        if causal:
            doffs_ref[0, head : head + 1, :] = diagonal_sums(jnp.concatenate(spread, axis=1), size)


def full_spec(shape):
    zeros = (0,) * len(shape)
    return pl.BlockSpec(shape, lambda *_: zeros, pipeline_mode=pl.Buffered(1))


def corner_spec(shape):
    rows = 16 if shape[-2] % 16 == 0 else shape[-2]
    columns = 128 if shape[-1] % 128 == 0 else shape[-1]
    zeros = (0,) * len(shape)
    return pl.BlockSpec(
        (1,) * (len(shape) - 2) + (rows, columns), lambda *_: zeros, pipeline_mode=pl.Buffered(1)
    )


def rms(hidden, gain):
    scale = lax.rsqrt(jnp.mean(hidden * hidden, axis=-1, keepdims=True) + EPSILON)
    return hidden * scale * gain


def rms_backward(hidden, gain, upstream):
    scale = lax.rsqrt(jnp.mean(hidden * hidden, axis=-1, keepdims=True) + EPSILON)
    gain_grad = jnp.sum(upstream * (hidden * scale), axis=0, keepdims=True)
    weighted = upstream * gain
    inner = jnp.mean(weighted * hidden, axis=-1, keepdims=True)
    return scale * weighted - hidden * (scale * scale * scale) * inner, gain_grad


def half_at(core, other, width):
    return pl.multiple_of((1 - core if other else core) * width, width)


TICK = (8, 128)


def ticking(kernel, at, count, outputs, *refs):
    refs[outputs][...] = jnp.zeros(TICK, F32)
    kernel(*refs[:at], *refs[at + count : outputs], *refs[outputs + 1 :])


class Flow:
    def __init__(self):
        self.ticks = []

    def after(self, *arrays):
        self.ticks.extend(arrays)

    def call(self, kernel, name, scalars, grid, ins, outs, scratch=(), room=10, cost=1.0):
        count = len(scalars) + len(ins)
        late = len(self.ticks)
        *results, tick = pl.pallas_call(
            functools.partial(ticking, kernel, count, late, count + late + len(outs)),
            out_shape=tuple(jax.ShapeDtypeStruct(shape, kind) for shape, kind, _ in outs)
            + (jax.ShapeDtypeStruct(TICK, F32),),
            grid_spec=pltpu.PrefetchScalarGridSpec(
                num_scalar_prefetch=len(scalars),
                grid=grid,
                in_specs=[spec for _, spec in ins]
                + [corner_spec(item.shape) for item in self.ticks],
                out_specs=[spec for _, _, spec in outs] + [full_spec(TICK)],
                scratch_shapes=list(scratch),
            ),
            compiler_params=pltpu.CompilerParams(vmem_limit_bytes=room * MIB),
            cost_estimate=pl.CostEstimate(flops=int(cost * MICROSECOND), bytes_accessed=0, transcendentals=0),
            name=name,
        )(*scalars, *[array for array, _ in ins], *self.ticks)
        self.ticks = [tick]
        return results


def double_kernel(*refs):
    count = len(refs) // 3
    for one_ref, two_ref, out_ref in zip(refs[:count], refs[count : 2 * count], refs[2 * count :]):
        half = one_ref.shape[0]
        out_ref[:half] = one_ref[...]
        out_ref[half:] = two_ref[...]


def double(flow, pairs):
    shapes = [(2 * one.shape[0],) + one.shape[1:] for one, _ in pairs]
    return flow.call(
        double_kernel,
        "double",
        (),
        (1,),
        [whole(one) for one, _ in pairs] + [whole(two) for _, two in pairs],
        [(shape, BF16, full_spec(shape)) for shape in shapes],
    )


def halve_kernel(*refs):
    keep_one, keep_two, got_one, got_two = refs[:4]
    keep_ref, send_ref = refs[-3:-1] if len(refs) > 6 else refs[-2:]
    keep_ref[...] = (keep_one[...].astype(F32) + got_one[...].astype(F32)).astype(BF16)
    send_ref[...] = (keep_two[...].astype(F32) + got_two[...].astype(F32)).astype(BF16)
    if len(refs) > 6:
        refs[-1][...] = refs[4][...] + refs[5][...]


def extra_ins(extra):
    return [whole(item) for item in extra]


def extra_outs(extra):
    return [(extra[0].shape, F32, full_spec(extra[0].shape))] if extra else []


def halve(flow, keep, got, extra=()):
    half = keep.shape[0] // 2
    steps = min(half, 2)
    rest = keep.shape[1:]
    one = pl.BlockSpec((half // steps,) + rest, lambda i: (i, 0, 0, 0))
    two = pl.BlockSpec((half // steps,) + rest, lambda i: (steps + i, 0, 0, 0))
    out = ((half,) + rest, BF16, one)
    return flow.call(
        halve_kernel,
        "halve",
        (),
        (steps,),
        [(keep, one), (keep, two), (got, one), (got, two)] + extra_ins(extra),
        [out, out] + extra_outs(extra),
    )


def whole(array):
    return (array, full_spec(array.shape))


def query_kernel(core, hidden_ref, gain_ref, weight_ref, normed_ref, out_ref):
    @pl.when(pl.program_id(0) == 0)
    def _():
        normed_ref[...] = rms(hidden_ref[...].astype(F32), gain_ref[...]).astype(BF16)

    out_ref[0] = dot(normed_ref[...], weight_ref[0], NN).astype(BF16)


def query_step(flow, core, hidden, gain, weights):
    size, width = hidden.shape
    return flow.call(
        query_kernel,
        "query_step",
        (core,),
        (3,),
        [whole(hidden), whole(gain), (weights, pl.BlockSpec((1, width, width), lambda i, _: (i, 0, 0)))],
        [
            ((size, width), BF16, full_spec((size, width))),
            ((3, size, width), BF16, pl.BlockSpec((1, size, width), lambda i, _: (i, 0, 0))),
        ], cost=3)


def cross_kernel(core, mixed_ref, hidden_ref, memory_ref, gain_ref, weight_ref, after_ref, normed_ref, out_ref):
    step = pl.program_id(0)

    @pl.when(step == 0)
    def _():
        after = hidden_ref[...].astype(F32) + dot(mixed_ref[...], weight_ref[0], NN)
        after_ref[...] = after
        normed_ref[...] = rms(after, gain_ref[...]).astype(BF16)

    @pl.when(step == 1)
    def _():
        out_ref[0] = dot(normed_ref[...], weight_ref[0], NN).astype(BF16)

    @pl.when(step >= 2)
    def _():
        out_ref[0] = dot(memory_ref[...], weight_ref[0], NN).astype(BF16)


def cross_step(flow, core, mixed, hidden, memory, gain, weights):
    size, width = hidden.shape
    return flow.call(
        cross_kernel,
        "cross_step",
        (core,),
        (4,),
        [
            whole(mixed),
            whole(hidden),
            whole(memory),
            whole(gain),
            (weights, pl.BlockSpec((1, width, width), lambda i, _: (i, 0, 0))),
        ],
        [
            ((size, width), F32, full_spec((size, width))),
            ((size, width), BF16, full_spec((size, width))),
            (
                (3, size, width),
                BF16,
                pl.BlockSpec((1, size, width), lambda i, _: (jnp.maximum(i - 1, 0), 0, 0)),
            ),
        ], cost=5)


def out_kernel(core, mixed_ref, after_ref, gain_ref, weight_ref, out_ref, normed_ref):
    after = after_ref[...] + dot(mixed_ref[...], weight_ref[0], NN)
    out_ref[...] = after
    normed_ref[...] = rms(after, gain_ref[...]).astype(BF16)


def out_step(flow, core, mixed, after, gain, weights, at):
    size, width = mixed.shape
    return flow.call(
        out_kernel,
        "out_step",
        (core,),
        (1,),
        [
            whole(mixed),
            whole(after),
            whole(gain),
            (weights, pl.BlockSpec((1, width, width), lambda *_: (at, 0, 0))),
        ],
        [
            ((size, width), F32, full_spec((size, width))),
            ((size, width), BF16, full_spec((size, width))),
        ], cost=2.5)


def feed_tile(normed, cotangent, gate_w, up_w, down_w):
    gate = dot(normed, gate_w, NN)
    lift = dot(normed, up_w, NN)
    root = 0.7978845608028654
    square = gate * gate
    bend = jnp.tanh(root * gate * (1.0 + 0.044715 * square))
    half = 0.5 + 0.5 * bend
    active = gate * half
    slope = half + 0.5 * gate * (1.0 - bend * bend) * (root * (1.0 + 3 * 0.044715 * square))
    inner = (active * lift).astype(BF16)
    inner_grad = dot(cotangent, down_w, NT)
    gate_grad = (inner_grad * lift * slope).astype(BF16)
    lift_grad = (inner_grad * active).astype(BF16)
    out = dot(inner, down_w, NN)
    back = dot(gate_grad, gate_w, NT) + dot(lift_grad, up_w, NT)
    return inner, gate_grad, lift_grad, out, back


def feed_weights(half, gate_ref, up_ref, down_ref, down_w):
    start = pl.multiple_of(half * 128, 128)
    wide = []
    for ref in (gate_ref, up_ref):
        owners, _, _, rows, columns = ref.shape
        wide.append(
            jnp.concatenate(
                [
                    ref[:, 0, 0, :, pl.ds(start + at, 128)].reshape(owners * rows, 128)
                    for at in range(0, columns, 256)
                ],
                axis=1,
            )
        )
    for owner in range(2):
        for piece in range(2):
            for row in range(4):
                for column in range(6):
                    first = owner * 128 + piece * 64 + row * 16
                    down_w[first : first + 16, column * 128 : column * 128 + 128] = down_ref[
                        owner,
                        2 * half + piece,
                        0,
                        column * 16 : column * 16 + 16,
                        row * 128 : row * 128 + 128,
                    ]
    return wide[0], wide[1], down_w[...]


def feed_add(first, second, outs, values):
    step = pl.program_id(0)

    @pl.when(step == 0)
    def _():
        for ref, start, value in zip(outs, first, values):
            ref[...] = value if second is None else start[...] + value

    @pl.when(step > 0)
    def _():
        for ref, value in zip(outs, values):
            ref[...] += value


def feed_first_kernel(
    core, normed_ref, cot_ref, gate_ref, up_ref, down_ref, parts_ref, out_ref, back_ref, down_w
):
    weights = feed_weights(1 - core[0], gate_ref, up_ref, down_ref, down_w)
    inner, gate_grad, lift_grad, out, back = feed_tile(normed_ref[...], cot_ref[...], *weights)
    parts_ref[0] = inner
    parts_ref[1] = gate_grad
    parts_ref[2] = lift_grad
    feed_add((None, None), None, (out_ref, back_ref), (out, back))


def feed_second_kernel(
    core,
    normed_ref,
    cot_ref,
    gate_ref,
    up_ref,
    down_ref,
    out_in_ref,
    back_in_ref,
    after_ref,
    gain_ref,
    weight_ref,
    parts_ref,
    layer_ref,
    carry_ref,
    gain_grad_ref,
    other_ref,
    mine_ref,
    mixed_grad_ref,
    down_w,
    out_ref,
    back_ref,
    branch_ref,
):
    weights = feed_weights(core[0], gate_ref, up_ref, down_ref, down_w)
    inner, gate_grad, lift_grad, out, back = feed_tile(normed_ref[...], cot_ref[...], *weights)
    parts_ref[0] = inner
    parts_ref[1] = gate_grad
    parts_ref[2] = lift_grad
    feed_add((out_in_ref, back_in_ref), True, (out_ref, back_ref), (out, back))

    @pl.when(pl.program_id(0) == pl.num_programs(0) - 1)
    def _():
        after = after_ref[...]
        layer_ref[...] = (after + out_ref[...]).astype(BF16)
        residual, gain_grad = rms_backward(after, gain_ref[...], back_ref[...])
        gain_grad_ref[...] = gain_grad
        carry = cot_ref[...].astype(F32) + residual
        carry_ref[...] = carry
        branch_ref[...] = carry.astype(BF16)
        width = other_ref.shape[1]
        other_ref[...] = branch_ref[:, pl.ds(half_at(core[0], True, width), width)]
        mine_ref[...] = branch_ref[:, pl.ds(half_at(core[0], False, width), width)]
        mixed_grad_ref[...] = dot(branch_ref[...], weight_ref[0], NT).astype(BF16)


def feed_ins(normed, cotangent, weights):
    owners, pieces, _, rows, columns = weights.shape
    size = normed.shape[0]
    wide = [
        (
            weights,
            pl.BlockSpec(
                (owners, 1, 1, rows, columns), functools.partial(lambda at, i, _: (0, i, at, 0, 0), at)
            ),
        )
        for at in range(2)
    ]
    tall = (weights, pl.BlockSpec((2, pieces, 1, rows, columns), lambda i, _: (i, 0, 2, 0, 0)))
    units = pieces * columns // 2
    return (
        (owners // 2,),
        [whole(normed), whole(cotangent)] + wide + [tall],
        ((3, size, units), BF16, pl.BlockSpec((3, size, 256), lambda i, _: (0, 0, i))),
        pltpu.VMEM((256, normed.shape[1]), BF16),
    )


def feed_first(flow, core, normed, cotangent, weights):
    grid, ins, parts, scratch = feed_ins(normed, cotangent, weights)
    total = (normed.shape, F32, full_spec(normed.shape))
    return flow.call(
        feed_first_kernel, "feed_first", (core,), grid, ins, [parts, total, total], [scratch], room=50, cost=9
    )


def feed_second(flow, core, normed, cotangent, weights, out, back, after, gain, last, at):
    grid, ins, parts, scratch = feed_ins(normed, cotangent, weights)
    size, width = normed.shape
    ins = ins + [
        whole(out),
        whole(back),
        whole(after),
        whole(gain),
        (last, pl.BlockSpec((1, width, width), lambda *_: (at, 0, 0))),
    ]
    narrow = ((size, width // 2), BF16, full_spec((size, width // 2)))
    return flow.call(
        feed_second_kernel,
        "feed_second",
        (core,),
        grid,
        ins,
        [
            parts,
            ((size, width), BF16, full_spec((size, width))),
            ((size, width), F32, full_spec((size, width))),
            ((1, width), F32, full_spec((1, width))),
            narrow,
            narrow,
            ((size, width), BF16, full_spec((size, width))),
        ],
        [
            scratch,
            pltpu.VMEM((size, width), F32),
            pltpu.VMEM((size, width), F32),
            pltpu.VMEM((size, width), BF16),
        ],
        room=50,
        cost=11,
    )


def back_product(core, others, mines, weight_ref, at):
    width = others.shape[-1]
    return dot(
        others[at], weight_ref[0, :, pl.ds(half_at(core[0], True, width), width)], NT
    ) + dot(mines[at], weight_ref[0, :, pl.ds(half_at(core[0], False, width), width)], NT)


def middle_kernel(
    core,
    others,
    mines,
    after_ref,
    gain_ref,
    carry_in_ref,
    query_ref,
    weight_ref,
    carry_ref,
    gain_grad_ref,
    other_ref,
    mine_ref,
    mixed_grad_ref,
    branch_ref,
):
    back = back_product(core, others, mines, query_ref, 0)
    residual, gain_grad = rms_backward(after_ref[...], gain_ref[...], back)
    gain_grad_ref[...] = gain_grad
    carry = carry_in_ref[...] + residual
    carry_ref[...] = carry
    branch_ref[...] = carry.astype(BF16)
    width = other_ref.shape[1]
    other_ref[...] = branch_ref[:, pl.ds(half_at(core[0], True, width), width)]
    mine_ref[...] = branch_ref[:, pl.ds(half_at(core[0], False, width), width)]
    mixed_grad_ref[...] = dot(branch_ref[...], weight_ref[0], NT).astype(BF16)


def middle_step(flow, core, others, mines, after, gain, carry, weights, query_at, out_at):
    size, width = after.shape
    narrow = ((size, width // 2), BF16, full_spec((size, width // 2)))
    return flow.call(
        middle_kernel,
        "middle_step",
        (core,),
        (1,),
        [
            whole(others),
            whole(mines),
            whole(after),
            whole(gain),
            whole(carry),
            (weights, pl.BlockSpec((1, width, width), lambda *_: (query_at, 0, 0))),
            (weights, pl.BlockSpec((1, width, width), lambda *_: (out_at, 0, 0))),
        ],
        [
            ((size, width), F32, full_spec((size, width))),
            ((1, width), F32, full_spec((1, width))),
            narrow,
            narrow,
            ((size, width), BF16, full_spec((size, width))),
        ],
        [pltpu.VMEM((size, width), BF16)], cost=3)


def memory_kernel(core, others, mines, key_ref, value_ref, out_ref):
    out_ref[...] = back_product(core, others, mines, key_ref, 1) + back_product(
        core, others, mines, value_ref, 2
    )


def memory_step(flow, core, others, mines, weights, at):
    size, width = others.shape[1], weights.shape[2]
    return flow.call(
        memory_kernel,
        "memory_step",
        (core,),
        (1,),
        [
            whole(others),
            whole(mines),
            (weights, pl.BlockSpec((1, width, width), lambda *_: (at, 0, 0))),
            (weights, pl.BlockSpec((1, width, width), lambda *_: (at + 1, 0, 0))),
        ],
        [((size, width), F32, full_spec((size, width)))], cost=3)[0]


def last_kernel(core, others, mines, hidden_ref, gain_ref, carry_ref, w_one, w_two, w_three, out_ref, gain_grad_ref):
    back = (
        back_product(core, others, mines, w_one, 0)
        + back_product(core, others, mines, w_two, 1)
        + back_product(core, others, mines, w_three, 2)
    )
    residual, gain_grad = rms_backward(hidden_ref[...].astype(F32), gain_ref[...], back)
    gain_grad_ref[...] = gain_grad
    out_ref[...] = carry_ref[...] + residual


def last_step(flow, core, others, mines, hidden, gain, carry, weights):
    size, width = hidden.shape
    return flow.call(
        last_kernel,
        "last_step",
        (core,),
        (1,),
        [whole(others), whole(mines), whole(hidden), whole(gain), whole(carry)]
        + [
            (weights, pl.BlockSpec((1, width, width), functools.partial(lambda at, *_: (at, 0, 0), at)))
            for at in range(3)
        ],
        [
            ((size, width), F32, full_spec((size, width))),
            ((1, width), F32, full_spec((1, width))),
        ], cost=5.5)


def take(array, part):
    return array[...] if part is None else array[part]


def weight_grads_kernel(plan, row_count, grad_count, picks, *refs):
    rows, rows_got = refs[:row_count], refs[row_count : 2 * row_count]
    refs = refs[2 * row_count :]
    grads, grads_got = refs[:grad_count], refs[grad_count : 2 * grad_count]
    keep_ref, send_ref, total_ref = refs[2 * grad_count :]
    half, tall = keep_ref.shape[0], keep_ref.shape[2]
    for at, (row, row_part, grad, part) in enumerate(plan):
        total = dot(take(rows[row], row_part), take(grads[grad], part), TN)
        total = total + dot(take(rows_got[row], row_part), take(grads_got[grad], part), TN)
        total_ref[...] = total.astype(BF16).reshape(total_ref.shape)
        for place in range(half):
            keep_ref[place, at] = total_ref[picks[place]]
            send_ref[place, at] = total_ref[picks[half + place]]


def weight_grads(links, flow, order, plan, rows, rows_got, grads, grads_got):
    picks = links.places(links.core, order[::-1])
    count = 2 * links.owners
    height = rows[plan[0][0]].shape[-1]
    columns = grads[plan[0][2]].shape[-1]
    tall = height // count
    if tall % 16 == 0:
        shape = (count // 2, len(plan), tall, columns)
        return flow.call(
            functools.partial(weight_grads_kernel, plan, len(rows), len(grads)),
            "weight_grads",
            (picks,),
            (1,),
            [whole(item) for item in (*rows, *rows_got, *grads, *grads_got)],
            [(shape, BF16, full_spec(shape)), (shape, BF16, full_spec(shape))],
            [pltpu.VMEM((count, tall, columns), BF16)],
            room=16, cost=5)
    stack = []
    for row, row_part, grad, part in plan:
        total = dot(take(rows[row], row_part), take(grads[grad], part), TN)
        total = total + dot(take(rows_got[row], row_part), take(grads_got[grad], part), TN)
        stack.append(total.astype(BF16).reshape(count, tall, columns))
    stack = jnp.stack(stack, axis=1)[picks]
    return stack[: count // 2], stack[count // 2 :]


def attend_forward(flow, lengths, offs, stack):
    causal = offs is not None
    _, size, width = stack.shape
    pairs = HEADS // 2

    def part(at):
        return (stack, pl.BlockSpec((1, size, 2 * HEAD), lambda p, *_: (at, 0, p)))

    lanes = pl.BlockSpec((1, 2, size), lambda p, *_: (p, 0, 0))
    ins = [part(0), part(1), part(2)]
    if causal:
        ins = [(offs, lanes)] + ins
    return flow.call(
        functools.partial(forward_kernel, causal),
        "attend_forward_self" if causal else "attend_forward_cross",
        (lengths,),
        (pairs,),
        ins,
        [
            ((size, width), BF16, pl.BlockSpec((size, 2 * HEAD), lambda p, *_: (0, p))),
            ((pairs, 2, size), F32, lanes),
        ],
        cost=11,
    )


def attend_backward(flow, lengths, core, other, offs, stack, g, lse):
    causal = offs is not None
    _, size, width = stack.shape
    pairs = HEADS // 4

    def pair(p, core):
        return (1 - core[0] if other else core[0]) * pairs + p

    def part(at):
        return (stack, pl.BlockSpec((1, size, 2 * HEAD), lambda p, _, core: (at, 0, pair(p, core))))

    lanes = pl.BlockSpec((1, 2, size), lambda p, _, core: (pair(p, core), 0, 0))
    ins = [part(0), part(1), part(2)]
    ins = ins + [(g, pl.BlockSpec((size, 2 * HEAD), lambda p, _, core: (0, pair(p, core)))), (lse, lanes)]
    outs = [((3, size, width // 2), BF16, pl.BlockSpec((3, size, 2 * HEAD), lambda p, *_: (0, 0, p)))]
    if causal:
        ins = [(offs, lanes)] + ins
        outs = outs + [((pairs, 2, size), F32, pl.BlockSpec((1, 2, size), lambda p, *_: (p, 0, 0)))]
    return flow.call(
        functools.partial(backward_kernel, causal),
        "attend_backward_self" if causal else "attend_backward_cross",
        (lengths, core),
        (pairs,),
        ins,
        outs,
        cost=8,
    )


class Links:
    def __init__(self, reps, owners, width):
        self.owners = owners
        self.width = width
        self.bits = owners.bit_length() - 1
        self.count = reps * owners
        self.rep = lax.axis_index("rep")
        self.owner = lax.axis_index("fsdp")
        self.core = self.rep % 2
        self.side = self.rep // 2
        self.core_word = self.core.reshape(1).astype(jnp.int32)
        self.side_word = self.side.reshape(1).astype(jnp.int32)

    def move(self, array, target):
        return lax.ppermute(
            array, ("rep", "fsdp"), [(device, target(device)) for device in range(self.count)]
        )

    def over_owner(self, array, bit):
        return self.move(array, lambda device: device ^ (1 << bit))

    def over_core(self, array):
        return self.move(array, lambda device: device ^ self.owners)

    def over_side(self, array):
        return self.move(array, lambda device: device ^ (2 * self.owners))

    def over_pair(self, array, first):
        def target(device):
            core = (device // self.owners) % 2
            return device ^ (1 if (core == 0) == first else 2 * self.owners)

        return self.move(array, target)

    def step(self, array, name):
        if name == "first":
            return self.over_pair(array, True)
        if name == "second":
            return self.over_pair(array, False)
        return self.over_owner(array, name)

    def far_to_near(self):
        return tuple(range(self.bits - 1, 0, -1))

    def places(self, core, order):
        index = jnp.arange(2 * self.owners)
        owner = jnp.full_like(index, self.owner)
        side = jnp.full_like(index, self.side)
        for at, name in enumerate(order):
            flip = (index >> at) & 1
            if name == "first":
                owner = owner ^ jnp.where(core == 0, flip, 0)
                side = side ^ jnp.where(core == 0, 0, flip)
            elif name == "second":
                owner = owner ^ jnp.where(core == 0, 0, flip)
                side = side ^ jnp.where(core == 0, flip, 0)
            else:
                owner = owner ^ (flip << name)
        return (owner * 2 + side).astype(jnp.int32)


def assemble_kernel(places, core, *refs):
    sources, out_ref, sems = refs[:2], refs[2], refs[3]
    width = sources[0].shape[-1]
    copies = []
    for half in range(2):
        column = core[0] if half == 0 else 1 - core[0]
        start = pl.multiple_of(column * width, width)
        tall = out_ref.shape[-1] == width
        for at in range(sources[half].shape[0]):
            copies.append(
                pltpu.make_async_copy(
                    sources[half].at[at],
                        out_ref.at[pl.ds(column, 1), places[half, at]]
                        if tall
                        else out_ref.at[:, places[half, at], :, pl.ds(start, width)],
                    sems.at[half, at],
                )
            )
    for copy in copies:
        copy.start()
    for copy in copies:
        copy.wait()


def assemble(links, flow, order, own, other, tall=False):
    places = jnp.stack([links.places(links.core, order), links.places(1 - links.core, order)])
    count, weights, rows, columns = own.shape
    if tall:
        shape = (2, count, rows, columns)
    else:
        shape = (weights, count, rows, 2 * columns)
    out = flow.call(
        assemble_kernel,
        "assemble",
        (places, links.core_word),
        (1,),
        [whole(own), whole(other)],
        [(shape, BF16, full_spec(shape))],
        [pltpu.SemaphoreType.DMA((2, count))],
        room=14,
        cost=3.5,
    )[0]
    if tall:
        return out.reshape(2 * count * rows, columns)
    return out.reshape(weights, count * rows, 2 * columns)


def pack_kernel(counts, core, *refs):
    total = sum(counts)
    shards, blocks, sems = refs[:total], refs[total:-1], refs[-1]
    copies = []
    for count, block in zip(counts, blocks):
        high, wide = block.shape[2], block.shape[3]
        rows = pl.ds(pl.multiple_of(core[1] * high, high), high)
        columns = pl.ds(pl.multiple_of(core[0] * wide, wide), wide)
        for index in range(count):
            copies.append(
                pltpu.make_async_copy(
                    shards[len(copies)].at[rows, columns], block.at[0, index], sems.at[len(copies)]
                )
            )
    for copy in copies:
        copy.start()
    for copy in copies:
        copy.wait()


def pack(links, flow, groups):
    high, wide = groups[0][0].shape
    high, wide = high // 2, wide // 2
    counts = [len(group) for group in groups]
    if high % 16 == 0:
        shapes = [(1, count, high, wide) for count in counts]
        return flow.call(
            functools.partial(pack_kernel, counts),
            "pack",
            (jnp.stack([links.core, links.side]).astype(jnp.int32),),
            (1,),
            [(shard, pl.BlockSpec(memory_space=pl.ANY)) for group in groups for shard in group],
            [(shape, BF16, full_spec(shape)) for shape in shapes],
            [pltpu.SemaphoreType.DMA((sum(counts),))],
        )
    at = (links.side * high, links.core * wide)
    return [
        jnp.stack([lax.dynamic_slice(shard, at, (high, wide)) for shard in group])[None] for group in groups
    ]


def gather_feed(links, reps, gate, up, down):
    owners = links.owners
    share, units = gate.shape
    wide = units // reps
    high, width = down.shape
    high = high // reps
    gate = lax.dynamic_slice_in_dim(gate, links.rep * wide, wide, 1)
    up = lax.dynamic_slice_in_dim(up, links.rep * wide, wide, 1)
    down = lax.dynamic_slice_in_dim(down, links.rep * high, high, 0)
    fine = share == width // 8
    if fine:
        down = down.reshape(wide // 128, 16, share // 16, 128).transpose(2, 1, 0, 3)
    down = down.reshape(share, wide)
    full = lax.all_gather(jnp.stack([gate, up, down]), ("fsdp", "rep"), axis=0)
    full = full.reshape(owners, reps, 3, share, wide)
    if fine:
        return full
    half = units // owners // 2
    parts = []
    for at in range(2):
        part = full[:, :, at].transpose(0, 2, 1, 3).reshape(width, 8, owners // 8, 2, half)
        part = part.transpose(0, 1, 3, 2, 4).reshape(8, width // 8, reps, wide)
        parts.append(part.transpose(0, 2, 1, 3))
    down = full[:, :, 2].reshape(8, owners // 8, 2, half, width).transpose(0, 2, 1, 3, 4)
    down = down.reshape(8, reps, wide // 128, 16, width // 128, 128).transpose(0, 1, 4, 3, 2, 5)
    parts.append(down.reshape(8, reps, width // 8, wide))
    return jnp.stack(parts, axis=2)


class Reduce:
    def __init__(self, links, flow, order, keep, send, tall=False):
        self.links, self.flow, self.order, self.tall = links, flow, order, tall
        self.keep, self.send = keep, send
        self.taken = 0
        self.start()

    def start(self):
        self.got = self.links.step(self.send, self.order[self.taken])
        self.taken += 1

    def advance(self, *extra):
        self.keep, self.send, *more = halve(self.flow, self.keep, self.got, extra)
        self.start()
        return more[0] if more else None

    def rest(self):
        while self.taken < len(self.order):
            self.advance()

    def sides(self, *extra):
        mine, *more = add(self.flow, self.keep, self.got, extra)
        self.keep, self.got = mine, self.links.over_side(mine)
        return more[0] if more else None

    def cores(self, *extra):
        mine, *more = stack(self.flow, self.links.side_word, self.keep, self.got, extra)
        self.keep, self.got = mine, self.links.over_core(mine)
        return more[0] if more else None

    def outs(self):
        return unpack(self.flow, self.links, self.keep, self.got, self.tall)


def add_kernel(*refs):
    out_ref = refs[-1] if len(refs) == 3 else refs[-2]
    out_ref[...] = (refs[0][0].astype(F32) + refs[1][0].astype(F32)).astype(BF16)
    if len(refs) > 3:
        refs[-1][...] = refs[2][...] + refs[3][...]


def add(flow, one, two, extra):
    shape = one.shape[1:]
    return flow.call(
        add_kernel,
        "add",
        (),
        (1,),
        [whole(one), whole(two)] + extra_ins(extra),
        [(shape, BF16, full_spec(shape))] + extra_outs(extra),
    )


def stack_kernel(first, *refs):
    out_ref = refs[-1] if len(refs) == 3 else refs[-2]
    out_ref[:, pl.ds(first[0], 1)] = refs[0][...][:, None]
    out_ref[:, pl.ds(1 - first[0], 1)] = refs[1][...][:, None]
    if len(refs) > 3:
        refs[-1][...] = refs[2][...] + refs[3][...]


def stack(flow, first, one, two, extra):
    weights, rows, columns = one.shape
    shape = (weights, 2, rows, columns)
    out, *more = flow.call(
        stack_kernel,
        "stack",
        (first,),
        (1,),
        [whole(one), whole(two)] + extra_ins(extra),
        [(shape, BF16, full_spec(shape))] + extra_outs(extra),
    )
    return (out.reshape(weights, 2 * rows, columns), *more)


def unpack_kernel(tall, owners, core, one_ref, two_ref, *out_refs):
    for index, out_ref in enumerate(out_refs):
        for half, ref in enumerate((one_ref, two_ref)):
            at = core[0] if half == 0 else 1 - core[0]
            value = ref[index].astype(F32)
            rows, columns = value.shape
            parts = owners if columns % (owners * 128) == 0 else 1
            wide = columns // parts
            if tall:
                out_ref[pl.ds(pl.multiple_of(at * rows, rows), rows)] = value
            else:
                for part in range(parts):
                    start = pl.multiple_of((2 * part + at) * wide, wide)
                    out_ref[:, pl.ds(start, wide)] = value[:, part * wide : (part + 1) * wide]


def unpack(flow, links, one, two, tall):
    weights, rows, columns = one.shape
    if rows % 16:
        first = links.core == 0
        one, two = jnp.where(first, one, two), jnp.where(first, two, one)
        if tall:
            mine = jnp.concatenate([one, two], axis=1)
        elif 2 * columns > links.width:
            mine = jnp.stack([one, two], axis=2).reshape(weights, rows, 2, links.owners, -1)
            mine = mine.transpose(0, 1, 3, 2, 4).reshape(weights, rows, 2 * columns)
        else:
            mine = jnp.concatenate([one, two], axis=2)
        return list(mine.astype(F32))
    shape = (2 * rows, columns) if tall else (rows, 2 * columns)
    return flow.call(
        functools.partial(unpack_kernel, tall, links.owners),
        "unpack",
        (links.core_word,),
        (1,),
        [whole(one), whole(two)],
        [(shape, F32, full_spec(shape))] * weights,
    )


def pack_small_kernel(*refs):
    out_ref = refs[-1]
    for index, ref in enumerate(refs[:-1]):
        out_ref[index : index + 1, : ref.shape[1]] = ref[...]


def pack_small(flow, vectors):
    width = max(item.shape[1] for item in vectors)
    shape = (8, width)
    return flow.call(
        pack_small_kernel, "pack_small", (), (1,), [whole(item) for item in vectors], [(shape, F32, full_spec(shape))]
    )[0]


def on_device(
    reps,
    owners,
    hidden,
    memory,
    lengths,
    buckets,
    cotangent,
    self_gain,
    self_query,
    self_key,
    self_value,
    self_out,
    bias_table,
    cross_gain,
    cross_query,
    cross_key,
    cross_value,
    cross_out,
    feed_gain,
    feed_gate,
    feed_up,
    feed_down,
):
    width = hidden.shape[2]
    share = width // owners
    links = Links(reps, owners, width)
    hidden, memory, cotangent = hidden[0], memory[0], cotangent[0]
    flow = Flow()
    core = links.core_word
    far = links.far_to_near()
    order = far + ("first", "second")
    w_feed = gather_feed(links, reps, feed_gate, feed_up, feed_down)
    small = jnp.concatenate([self_gain, cross_gain, feed_gain, bias_table])[None]
    bits = list(range(links.bits - 1, -1, -1))
    a, b = pack(
        links,
        flow,
        (
            (self_query, self_key, self_value),
            (self_out, cross_query, cross_key, cross_value, cross_out),
        ),
    )
    for at, name in enumerate(order[:-1]):
        pairs = [(a, links.step(a, name))]
        if at > 0:
            pairs.append((b, links.step(b, order[at - 1])))
        if bits:
            tiny = links.over_owner(small, bits.pop(0))
            flow.after(tiny)
            small = jnp.concatenate([small, tiny], axis=0)
        if at > 0:
            (a,) = double(flow, pairs[:1])
            (b,) = double(flow, pairs[1:])
        else:
            (a,) = double(flow, pairs)
    apart = jnp.arange(owners) ^ links.owner
    place = sum(((apart >> bit) & 1) << (links.bits - 1 - bit) for bit in range(links.bits))
    small = small[place].astype(F32)
    gain_one = small[:, :share].reshape(1, -1)
    gain_two = small[:, share : 2 * share].reshape(1, -1)
    gain_three = small[:, 2 * share : 3 * share].reshape(1, -1)
    table = small[:, 3 * share :].reshape(BUCKETS, HEADS)
    picks = (buckets[:, None] == jnp.arange(BUCKETS)[None, :]).astype(F32)
    offsets = jnp.dot(picks, table, precision=PRECISE).T.reshape(HEADS // 2, 2, -1)

    memory_got = links.over_core(memory)
    (a,) = double(flow, [(a, links.step(a, order[-1]))])
    flow.after(memory_got)
    cotangent_got = links.over_core(cotangent)
    flow.after(offsets)
    b_got = links.step(b, order[-2])
    w_self = assemble(links, flow, order, a, links.over_core(a))
    flow.after(cotangent_got)
    normed_one, qkv = query_step(flow, core, hidden, gain_one, w_self)
    normed_one_got = links.over_core(normed_one)
    (b,) = double(flow, [(b, b_got)])
    b_got = links.step(b, order[-1])
    mixed_one, lse_one = attend_forward(flow, lengths, offsets, qkv)
    mixed_one_got = links.over_core(mixed_one)
    flow.after(normed_one_got)
    (b,) = double(flow, [(b, b_got)])
    w_cross = assemble(links, flow, order, b, links.over_core(b))
    after_self, normed_two, cross_qkv = cross_step(
        flow, core, mixed_one, hidden, memory, gain_two, w_cross
    )
    normed_two_got = links.over_core(normed_two)
    mixed_two, lse_two = attend_forward(flow, lengths, None, cross_qkv)
    mixed_two_got = links.over_core(mixed_two)
    flow.after(normed_two_got, mixed_one_got)
    after_cross, normed_three = out_step(flow, core, mixed_two, after_self, gain_three, w_cross, 4)
    normed_three_got = links.over_core(normed_three)
    flow.after(mixed_two_got, normed_three_got)
    parts_other, out, back = feed_first(flow, core, normed_three, cotangent, w_feed)
    parts_got = links.over_core(parts_other)
    (
        parts,
        layer_out,
        carry_two,
        gain_three_grad,
        branch_other,
        branch_two,
        mixed_grad,
    ) = feed_second(
        flow,
        core,
        normed_three,
        cotangent,
        w_feed,
        out,
        back,
        after_cross,
        gain_three,
        w_cross,
        4,
    )
    branch_two_got = links.over_core(branch_other)

    down = order[::-1]
    sums_c = Reduce(
        links,
        flow,
        down,
        *weight_grads(
            links,
            flow,
            down,
            [(0, None, 0, 1), (0, None, 0, 2)],
            [normed_three],
            [normed_three_got],
            [parts],
            [parts_got],
        ),
    )
    sums_d = Reduce(
        links,
        flow,
        down,
        *weight_grads(
            links,
            flow,
            down,
            [(0, 0, 0, None)],
            [parts],
            [parts_got],
            [cotangent],
            [cotangent_got],
        ),
        tall=True,
    )
    (cross_other,) = attend_backward(flow, lengths, core, True, None, cross_qkv, mixed_grad, lse_two)
    cross_got = links.over_core(cross_other)
    flow.after(branch_two_got)
    (cross_mine,) = attend_backward(flow, lengths, core, False, None, cross_qkv, mixed_grad, lse_two)
    sums_c.advance()
    carry_one, gain_two_grad, branch_other, branch_one, mixed_grad = middle_step(
        flow, core, cross_other, cross_mine, after_self, gain_two, carry_two, w_cross, 1, 0
    )
    branch_one_got = links.over_core(branch_other)
    sums_d.advance()
    sums_b = Reduce(
        links,
        flow,
        down,
        *weight_grads(
            links,
            flow,
            down,
            [
                (0, None, 0, None),
                (1, None, 1, 0),
                (2, None, 1, 1),
                (2, None, 1, 2),
                (3, None, 2, None),
            ],
            [mixed_one, normed_two, memory, mixed_two],
            [mixed_one_got, normed_two_got, memory_got, mixed_two_got],
            [branch_one, cross_mine, branch_two],
            [branch_one_got, cross_got, branch_two_got],
        ),
    )
    sums_c.advance()
    self_other, offsets_other = attend_backward(
        flow, lengths, core, True, offsets, qkv, mixed_grad, lse_one
    )
    self_got = links.over_core(self_other)
    sums_d.advance()
    self_mine, offsets_mine = attend_backward(
        flow, lengths, core, False, offsets, qkv, mixed_grad, lse_one
    )
    sums_b.advance()
    sums_c.advance()
    sums_d.advance()
    sums_a = Reduce(
        links,
        flow,
        down,
        *weight_grads(
            links,
            flow,
            down,
            [(0, None, 0, 0), (0, None, 0, 1), (0, None, 0, 2)],
            [normed_one],
            [normed_one_got],
            [self_mine],
            [self_got],
        ),
    )
    sums_b.advance()
    input_grad, gain_one_grad = last_step(
        flow, core, self_other, self_mine, hidden, gain_one, carry_one, w_self
    )
    first = links.core == 0
    offset_grad = jnp.concatenate(
        [
            jnp.where(first, offsets_mine, offsets_other),
            jnp.where(first, offsets_other, offsets_mine),
        ],
        axis=0,
    ).reshape(HEADS, -1)
    table_grad = jnp.dot(picks.T, offset_grad.T, precision=PRECISE).reshape(1, -1)
    small = pack_small(flow, [gain_one_grad, gain_two_grad, gain_three_grad, table_grad])
    sums_a.advance()
    moves = [links.over_core, links.over_side] + [
        functools.partial(links.over_owner, bit=bit) for bit in range(links.bits)
    ]
    small_got = moves.pop(0)(small)
    sums_c.rest()
    sums_c.sides()
    sums_d.rest()
    sums_d.sides()
    memory_grad = memory_step(flow, core, cross_other, cross_mine, w_cross, 2)
    while sums_a.taken < len(down):
        if sums_b.taken < len(down):
            sums_b.advance()
        else:
            sums_b.sides()
        small = sums_a.advance(small, small_got)
        small_got = moves.pop(0)(small)
        if sums_a.taken == len(down) - 1:
            sums_c.cores()
            sums_d.cores()
    small = sums_a.sides(small, small_got)
    small_got = moves.pop(0)(small)
    (total_d,) = sums_d.outs()
    total_c = sums_c.outs()
    sums_b.cores()
    small = sums_a.cores(small, small_got)
    small_got = moves.pop(0)(small)
    while moves:
        small = small + small_got
        small_got = moves.pop(0)(small)
    small = small + small_got
    total_b = sums_b.outs()
    total_a = sums_a.outs()
    small_table = lax.dynamic_slice_in_dim(
        small[3], links.owner * bias_table.shape[0], bias_table.shape[0], 0
    )
    small = lax.dynamic_slice_in_dim(small, links.owner * share, share, 1)
    return (
        layer_out[None],
        input_grad[None],
        memory_grad[None],
        small[0],
        total_a[0],
        total_a[1],
        total_a[2],
        total_b[0],
        small_table,
        small[1],
        total_b[1],
        total_b[2],
        total_b[3],
        total_b[4],
        small[2],
        total_c[0],
        total_c[1],
        total_d,
    )


def solution(mesh):
    rows = P(("rep", "fsdp"), None, None)
    vector = P("fsdp")
    matrix = P("fsdp", None)
    attention = (vector,) + (matrix,) * 4
    return jax.shard_map(
        functools.partial(on_device, mesh.shape["rep"], mesh.shape["fsdp"]),
        mesh=mesh,
        in_specs=(rows, rows, P(("rep", "fsdp")), P(), rows)
        + attention
        + (vector,)
        + attention
        + (vector, matrix, matrix, matrix),
        out_specs=(rows, rows, rows)
        + attention
        + (vector,)
        + attention
        + (vector, matrix, matrix, matrix),
        check_vma=False,
    )
```

```python
import functools
import jax
import jax.numpy as jnp
from jax import lax
from jax.experimental import pallas as pl
from jax.experimental.pallas import tpu as pltpu
from jax.sharding import PartitionSpec as P

HEADS = 12
HEAD = 64
BUCKETS = 32
EPSILON = 1e-06
MASKED = -1e30
PRECISE = lax.Precision.HIGHEST
MIB = 1024 * 1024
MICROSECOND = 3e9
F32 = jnp.float32
BF16 = jnp.bfloat16
NT = (((1,), (1,)), ((), ()))
NN = (((1,), (0,)), ((), ()))
TN = (((0,), (0,)), ((), ()))
TILE = 128


def dot(a, b, dims):
    return lax.dot_general(a, b, dims, preferred_element_type=F32)


def bias_tiles(offs, length):
    base = pltpu.roll(jnp.broadcast_to(offs, (TILE, length)), 0, 1, stride=1, stride_axis=0)
    key = lax.broadcasted_iota(jnp.int32, (TILE, TILE), 0)
    item = lax.broadcasted_iota(jnp.int32, (TILE, TILE), 1)
    first = jnp.where(item >= key, base[:, :TILE], MASKED)
    return jnp.concatenate([jnp.full((TILE, TILE), MASKED, F32), first, base[:, TILE:]], axis=1)


def diagonal_sums(spread, length):
    total = spread[:8]
    for at in range(8, TILE, 8):
        total = total + pltpu.roll(spread[at : at + 8], length - at, 1)
    row = lax.broadcasted_iota(jnp.int32, total.shape, 0)
    for bit in (1, 2, 4):
        total = jnp.where((row & bit) != 0, pltpu.roll(total, length - bit, 1), total)
    return jnp.sum(total, axis=0, keepdims=True)


def bias_block(tiles, first, rows, step):
    parts = []
    for block in range(rows // TILE):
        at = first - block * TILE + TILE
        parts.append(tiles[:, at : at + step])
    return jnp.concatenate(parts, axis=0)


def refused(rows, length):
    key = lax.broadcasted_iota(jnp.int32, (rows, 1), 0)
    return jnp.where(key < length, 0.0, MASKED)


def forward_kernel(causal, lengths, *refs):
    if causal:
        offs_ref, q_ref, k_ref, v_ref, mixed_ref, lse_ref = refs
    else:
        q_ref, k_ref, v_ref, mixed_ref, lse_ref = refs
    q_ref, k_ref, v_ref = q_ref.at[0], k_ref.at[0], v_ref.at[0]
    size = q_ref.shape[0]
    step = 256
    length = lengths[0]
    for head in range(2):
        cols = slice(head * HEAD, (head + 1) * HEAD)
        if causal:
            tiles = bias_tiles(offs_ref[0, head : head + 1, :], size)
        for first in range(0, size, step):
            rows = first + step if causal else size
            scores = dot(k_ref[:rows, cols], q_ref[first : first + step, cols], NT)
            if causal:
                scores = scores + bias_block(tiles, first, rows, step)
            scores = scores + refused(rows, length)
            highest = jnp.max(scores, axis=0, keepdims=True)
            weights = jnp.exp(scores - highest)
            total = jnp.sum(weights, axis=0, keepdims=True)
            mixed = dot(v_ref[:rows, cols], weights.astype(BF16), TN) * (1.0 / total)
            mixed_ref[first : first + step, cols] = mixed.T.astype(BF16)
            lse_ref[0, head : head + 1, first : first + step] = highest + jnp.log(total)


def backward_kernel(causal, lengths, core, *refs):
    if causal:
        offs_ref, q_ref, k_ref, v_ref, g_ref, lse_ref, grads_ref, doffs_ref = refs
    else:
        q_ref, k_ref, v_ref, g_ref, lse_ref, grads_ref = refs
    q_ref, k_ref, v_ref = q_ref.at[0], k_ref.at[0], v_ref.at[0]
    dq_ref, dk_ref, dv_ref = grads_ref.at[0], grads_ref.at[1], grads_ref.at[2]
    size = q_ref.shape[0]
    step = 256
    length = lengths[0]
    for head in range(2):
        cols = slice(head * HEAD, (head + 1) * HEAD)
        if causal:
            tiles = bias_tiles(offs_ref[0, head : head + 1, :], size)
            spread = [jnp.zeros((TILE, TILE), F32) for _ in range(size // TILE)]
        dk = [None] * (size // step)
        dv = [None] * (size // step)
        for first in range(0, size, step):
            rows = first + step if causal else size
            q = q_ref[first : first + step, cols]
            g = g_ref[first : first + step, cols]
            k = k_ref[:rows, cols]
            scores = dot(k, q, NT)
            if causal:
                scores = scores + bias_block(tiles, first, rows, step)
            scores = scores + refused(rows, length)
            probs = jnp.exp(scores - lse_ref[0, head : head + 1, first : first + step])
            prob_grad = dot(v_ref[:rows, cols], g, NT)
            delta = jnp.sum(probs * prob_grad, axis=0, keepdims=True)
            score_grad = (probs * (prob_grad - delta)).astype(BF16)
            if causal:
                for block in range(rows // TILE):
                    for lane in range(step // TILE):
                        at = first // TILE + lane - block
                        if at >= 0:
                            spread[at] = spread[at] + score_grad[
                                block * TILE : (block + 1) * TILE, lane * TILE : (lane + 1) * TILE
                            ].astype(F32)
            dk_now = dot(score_grad, q, NN)
            dv_now = dot(probs.astype(BF16), g, NN)
            for block in range(rows // step):
                part = slice(block * step, (block + 1) * step)
                dk[block] = dk_now[part] if dk[block] is None else dk[block] + dk_now[part]
                dv[block] = dv_now[part] if dv[block] is None else dv[block] + dv_now[part]
            dq_ref[first : first + step, cols] = dot(k, score_grad, TN).T.astype(BF16)
        for block in range(size // step):
            part = slice(block * step, (block + 1) * step)
            dk_ref[part, cols] = dk[block].astype(BF16)
            dv_ref[part, cols] = dv[block].astype(BF16)
        if causal:
            doffs_ref[0, head : head + 1, :] = diagonal_sums(jnp.concatenate(spread, axis=1), size)


def full_spec(shape):
    zeros = (0,) * len(shape)
    return pl.BlockSpec(shape, lambda *_: zeros, pipeline_mode=pl.Buffered(1))


def corner_spec(shape):
    rows = 16 if shape[-2] % 16 == 0 else shape[-2]
    columns = 128 if shape[-1] % 128 == 0 else shape[-1]
    zeros = (0,) * len(shape)
    return pl.BlockSpec(
        (1,) * (len(shape) - 2) + (rows, columns), lambda *_: zeros, pipeline_mode=pl.Buffered(1)
    )


def rms(hidden, gain):
    scale = lax.rsqrt(jnp.mean(hidden * hidden, axis=-1, keepdims=True) + EPSILON)
    return hidden * scale * gain


def rms_backward(hidden, gain, upstream):
    scale = lax.rsqrt(jnp.mean(hidden * hidden, axis=-1, keepdims=True) + EPSILON)
    gain_grad = jnp.sum(upstream * (hidden * scale), axis=0, keepdims=True)
    weighted = upstream * gain
    inner = jnp.mean(weighted * hidden, axis=-1, keepdims=True)
    return scale * weighted - hidden * (scale * scale * scale) * inner, gain_grad


def half_at(core, other, width):
    return pl.multiple_of((1 - core if other else core) * width, width)


TICK = (8, 128)


def ticking(kernel, at, count, outputs, *refs):
    refs[outputs][...] = jnp.zeros(TICK, F32)
    kernel(*refs[:at], *refs[at + count : outputs], *refs[outputs + 1 :])


class Flow:
    def __init__(self):
        self.ticks = []

    def after(self, *arrays):
        self.ticks.extend(arrays)

    def call(self, kernel, name, scalars, grid, ins, outs, scratch=(), room=10, cost=1.0):
        count = len(scalars) + len(ins)
        late = len(self.ticks)
        *results, tick = pl.pallas_call(
            functools.partial(ticking, kernel, count, late, count + late + len(outs)),
            out_shape=tuple(jax.ShapeDtypeStruct(shape, kind) for shape, kind, _ in outs)
            + (jax.ShapeDtypeStruct(TICK, F32),),
            grid_spec=pltpu.PrefetchScalarGridSpec(
                num_scalar_prefetch=len(scalars),
                grid=grid,
                in_specs=[spec for _, spec in ins]
                + [corner_spec(item.shape) for item in self.ticks],
                out_specs=[spec for _, _, spec in outs] + [full_spec(TICK)],
                scratch_shapes=list(scratch),
            ),
            compiler_params=pltpu.CompilerParams(vmem_limit_bytes=room * MIB),
            cost_estimate=pl.CostEstimate(flops=int(cost * MICROSECOND), bytes_accessed=0, transcendentals=0),
            name=name,
        )(*scalars, *[array for array, _ in ins], *self.ticks)
        self.ticks = [tick]
        return results


def double_kernel(*refs):
    count = len(refs) // 3
    for one_ref, two_ref, out_ref in zip(refs[:count], refs[count : 2 * count], refs[2 * count :]):
        half = one_ref.shape[0]
        out_ref[:half] = one_ref[...]
        out_ref[half:] = two_ref[...]


def double(flow, pairs):
    shapes = [(2 * one.shape[0],) + one.shape[1:] for one, _ in pairs]
    return flow.call(
        double_kernel,
        "double",
        (),
        (1,),
        [whole(one) for one, _ in pairs] + [whole(two) for _, two in pairs],
        [(shape, BF16, full_spec(shape)) for shape in shapes],
    )


def halve_kernel(*refs):
    keep_one, keep_two, got_one, got_two = refs[:4]
    keep_ref, send_ref = refs[-3:-1] if len(refs) > 6 else refs[-2:]
    keep_ref[...] = (keep_one[...].astype(F32) + got_one[...].astype(F32)).astype(BF16)
    send_ref[...] = (keep_two[...].astype(F32) + got_two[...].astype(F32)).astype(BF16)
    if len(refs) > 6:
        refs[-1][...] = refs[4][...] + refs[5][...]


def extra_ins(extra):
    return [whole(item) for item in extra]


def extra_outs(extra):
    return [(extra[0].shape, F32, full_spec(extra[0].shape))] if extra else []


def halve(flow, keep, got, extra=()):
    half = keep.shape[0] // 2
    steps = min(half, 2)
    rest = keep.shape[1:]
    one = pl.BlockSpec((half // steps,) + rest, lambda i: (i, 0, 0, 0))
    two = pl.BlockSpec((half // steps,) + rest, lambda i: (steps + i, 0, 0, 0))
    out = ((half,) + rest, BF16, one)
    return flow.call(
        halve_kernel,
        "halve",
        (),
        (steps,),
        [(keep, one), (keep, two), (got, one), (got, two)] + extra_ins(extra),
        [out, out] + extra_outs(extra),
    )


def whole(array):
    return (array, full_spec(array.shape))


def query_kernel(core, hidden_ref, gain_ref, weight_ref, normed_ref, out_ref):
    @pl.when(pl.program_id(0) == 0)
    def _():
        normed_ref[...] = rms(hidden_ref[...].astype(F32), gain_ref[...]).astype(BF16)

    out_ref[0] = dot(normed_ref[...], weight_ref[0], NN).astype(BF16)


def query_step(flow, core, hidden, gain, weights):
    size, width = hidden.shape
    return flow.call(
        query_kernel,
        "query_step",
        (core,),
        (3,),
        [whole(hidden), whole(gain), (weights, pl.BlockSpec((1, width, width), lambda i, _: (i, 0, 0)))],
        [
            ((size, width), BF16, full_spec((size, width))),
            ((3, size, width), BF16, pl.BlockSpec((1, size, width), lambda i, _: (i, 0, 0))),
        ], cost=3)


def cross_kernel(core, mixed_ref, hidden_ref, memory_ref, gain_ref, weight_ref, after_ref, normed_ref, out_ref):
    step = pl.program_id(0)

    @pl.when(step == 0)
    def _():
        after = hidden_ref[...].astype(F32) + dot(mixed_ref[...], weight_ref[0], NN)
        after_ref[...] = after
        normed_ref[...] = rms(after, gain_ref[...]).astype(BF16)

    @pl.when(step == 1)
    def _():
        out_ref[0] = dot(normed_ref[...], weight_ref[0], NN).astype(BF16)

    @pl.when(step >= 2)
    def _():
        out_ref[0] = dot(memory_ref[...], weight_ref[0], NN).astype(BF16)


def cross_step(flow, core, mixed, hidden, memory, gain, weights):
    size, width = hidden.shape
    return flow.call(
        cross_kernel,
        "cross_step",
        (core,),
        (4,),
        [
            whole(mixed),
            whole(hidden),
            whole(memory),
            whole(gain),
            (weights, pl.BlockSpec((1, width, width), lambda i, _: (i, 0, 0))),
        ],
        [
            ((size, width), F32, full_spec((size, width))),
            ((size, width), BF16, full_spec((size, width))),
            (
                (3, size, width),
                BF16,
                pl.BlockSpec((1, size, width), lambda i, _: (jnp.maximum(i - 1, 0), 0, 0)),
            ),
        ], cost=5)


def out_kernel(core, mixed_ref, after_ref, gain_ref, weight_ref, out_ref, normed_ref):
    after = after_ref[...] + dot(mixed_ref[...], weight_ref[0], NN)
    out_ref[...] = after
    normed_ref[...] = rms(after, gain_ref[...]).astype(BF16)


def out_step(flow, core, mixed, after, gain, weights, at):
    size, width = mixed.shape
    return flow.call(
        out_kernel,
        "out_step",
        (core,),
        (1,),
        [
            whole(mixed),
            whole(after),
            whole(gain),
            (weights, pl.BlockSpec((1, width, width), lambda *_: (at, 0, 0))),
        ],
        [
            ((size, width), F32, full_spec((size, width))),
            ((size, width), BF16, full_spec((size, width))),
        ], cost=2.5)


def feed_tile(normed, cotangent, gate_w, up_w, down_w):
    gate = dot(normed, gate_w, NN)
    lift = dot(normed, up_w, NN)
    root = 0.7978845608028654
    square = gate * gate
    bend = jnp.tanh(root * gate * (1.0 + 0.044715 * square))
    half = 0.5 + 0.5 * bend
    active = gate * half
    slope = half + 0.5 * gate * (1.0 - bend * bend) * (root * (1.0 + 3 * 0.044715 * square))
    inner = (active * lift).astype(BF16)
    inner_grad = dot(cotangent, down_w, NT)
    gate_grad = (inner_grad * lift * slope).astype(BF16)
    lift_grad = (inner_grad * active).astype(BF16)
    out = dot(inner, down_w, NN)
    back = dot(gate_grad, gate_w, NT) + dot(lift_grad, up_w, NT)
    return inner, gate_grad, lift_grad, out, back


def feed_weights(half, gate_ref, up_ref, down_ref, down_w):
    start = pl.multiple_of(half * 128, 128)
    wide = []
    for ref in (gate_ref, up_ref):
        owners, _, _, rows, columns = ref.shape
        wide.append(
            jnp.concatenate(
                [
                    ref[:, 0, 0, :, pl.ds(start + at, 128)].reshape(owners * rows, 128)
                    for at in range(0, columns, 256)
                ],
                axis=1,
            )
        )
    for owner in range(2):
        for piece in range(2):
            for row in range(4):
                for column in range(6):
                    first = owner * 128 + piece * 64 + row * 16
                    down_w[first : first + 16, column * 128 : column * 128 + 128] = down_ref[
                        owner,
                        2 * half + piece,
                        0,
                        column * 16 : column * 16 + 16,
                        row * 128 : row * 128 + 128,
                    ]
    return wide[0], wide[1], down_w[...]


def feed_add(first, second, outs, values):
    step = pl.program_id(0)

    @pl.when(step == 0)
    def _():
        for ref, start, value in zip(outs, first, values):
            ref[...] = value if second is None else start[...] + value

    @pl.when(step > 0)
    def _():
        for ref, value in zip(outs, values):
            ref[...] += value


def feed_first_kernel(
    core, normed_ref, cot_ref, gate_ref, up_ref, down_ref, parts_ref, out_ref, back_ref, down_w
):
    weights = feed_weights(1 - core[0], gate_ref, up_ref, down_ref, down_w)
    inner, gate_grad, lift_grad, out, back = feed_tile(normed_ref[...], cot_ref[...], *weights)
    parts_ref[0] = inner
    parts_ref[1] = gate_grad
    parts_ref[2] = lift_grad
    feed_add((None, None), None, (out_ref, back_ref), (out, back))


def feed_second_kernel(
    core,
    normed_ref,
    cot_ref,
    gate_ref,
    up_ref,
    down_ref,
    out_in_ref,
    back_in_ref,
    after_ref,
    gain_ref,
    weight_ref,
    parts_ref,
    layer_ref,
    carry_ref,
    gain_grad_ref,
    other_ref,
    mine_ref,
    mixed_grad_ref,
    down_w,
    out_ref,
    back_ref,
    branch_ref,
):
    weights = feed_weights(core[0], gate_ref, up_ref, down_ref, down_w)
    inner, gate_grad, lift_grad, out, back = feed_tile(normed_ref[...], cot_ref[...], *weights)
    parts_ref[0] = inner
    parts_ref[1] = gate_grad
    parts_ref[2] = lift_grad
    feed_add((out_in_ref, back_in_ref), True, (out_ref, back_ref), (out, back))

    @pl.when(pl.program_id(0) == pl.num_programs(0) - 1)
    def _():
        after = after_ref[...]
        layer_ref[...] = (after + out_ref[...]).astype(BF16)
        residual, gain_grad = rms_backward(after, gain_ref[...], back_ref[...])
        gain_grad_ref[...] = gain_grad
        carry = cot_ref[...].astype(F32) + residual
        carry_ref[...] = carry
        branch_ref[...] = carry.astype(BF16)
        width = other_ref.shape[1]
        other_ref[...] = branch_ref[:, pl.ds(half_at(core[0], True, width), width)]
        mine_ref[...] = branch_ref[:, pl.ds(half_at(core[0], False, width), width)]
        mixed_grad_ref[...] = dot(branch_ref[...], weight_ref[0], NT).astype(BF16)


def feed_ins(normed, cotangent, weights):
    owners, pieces, _, rows, columns = weights.shape
    size = normed.shape[0]
    wide = [
        (
            weights,
            pl.BlockSpec(
                (owners, 1, 1, rows, columns), functools.partial(lambda at, i, _: (0, i, at, 0, 0), at)
            ),
        )
        for at in range(2)
    ]
    tall = (weights, pl.BlockSpec((2, pieces, 1, rows, columns), lambda i, _: (i, 0, 2, 0, 0)))
    units = pieces * columns // 2
    return (
        (owners // 2,),
        [whole(normed), whole(cotangent)] + wide + [tall],
        ((3, size, units), BF16, pl.BlockSpec((3, size, 256), lambda i, _: (0, 0, i))),
        pltpu.VMEM((256, normed.shape[1]), BF16),
    )


def feed_first(flow, core, normed, cotangent, weights):
    grid, ins, parts, scratch = feed_ins(normed, cotangent, weights)
    total = (normed.shape, F32, full_spec(normed.shape))
    return flow.call(
        feed_first_kernel, "feed_first", (core,), grid, ins, [parts, total, total], [scratch], room=50, cost=9
    )


def feed_second(flow, core, normed, cotangent, weights, out, back, after, gain, last, at):
    grid, ins, parts, scratch = feed_ins(normed, cotangent, weights)
    size, width = normed.shape
    ins = ins + [
        whole(out),
        whole(back),
        whole(after),
        whole(gain),
        (last, pl.BlockSpec((1, width, width), lambda *_: (at, 0, 0))),
    ]
    narrow = ((size, width // 2), BF16, full_spec((size, width // 2)))
    return flow.call(
        feed_second_kernel,
        "feed_second",
        (core,),
        grid,
        ins,
        [
            parts,
            ((size, width), BF16, full_spec((size, width))),
            ((size, width), F32, full_spec((size, width))),
            ((1, width), F32, full_spec((1, width))),
            narrow,
            narrow,
            ((size, width), BF16, full_spec((size, width))),
        ],
        [
            scratch,
            pltpu.VMEM((size, width), F32),
            pltpu.VMEM((size, width), F32),
            pltpu.VMEM((size, width), BF16),
        ],
        room=50,
        cost=11,
    )


def back_product(core, others, mines, weight_ref, at):
    width = others.shape[-1]
    return dot(
        others[at], weight_ref[0, :, pl.ds(half_at(core[0], True, width), width)], NT
    ) + dot(mines[at], weight_ref[0, :, pl.ds(half_at(core[0], False, width), width)], NT)


def middle_kernel(
    core,
    others,
    mines,
    after_ref,
    gain_ref,
    carry_in_ref,
    query_ref,
    weight_ref,
    carry_ref,
    gain_grad_ref,
    other_ref,
    mine_ref,
    mixed_grad_ref,
    branch_ref,
):
    back = back_product(core, others, mines, query_ref, 0)
    residual, gain_grad = rms_backward(after_ref[...], gain_ref[...], back)
    gain_grad_ref[...] = gain_grad
    carry = carry_in_ref[...] + residual
    carry_ref[...] = carry
    branch_ref[...] = carry.astype(BF16)
    width = other_ref.shape[1]
    other_ref[...] = branch_ref[:, pl.ds(half_at(core[0], True, width), width)]
    mine_ref[...] = branch_ref[:, pl.ds(half_at(core[0], False, width), width)]
    mixed_grad_ref[...] = dot(branch_ref[...], weight_ref[0], NT).astype(BF16)


def middle_step(flow, core, others, mines, after, gain, carry, weights, query_at, out_at):
    size, width = after.shape
    narrow = ((size, width // 2), BF16, full_spec((size, width // 2)))
    return flow.call(
        middle_kernel,
        "middle_step",
        (core,),
        (1,),
        [
            whole(others),
            whole(mines),
            whole(after),
            whole(gain),
            whole(carry),
            (weights, pl.BlockSpec((1, width, width), lambda *_: (query_at, 0, 0))),
            (weights, pl.BlockSpec((1, width, width), lambda *_: (out_at, 0, 0))),
        ],
        [
            ((size, width), F32, full_spec((size, width))),
            ((1, width), F32, full_spec((1, width))),
            narrow,
            narrow,
            ((size, width), BF16, full_spec((size, width))),
        ],
        [pltpu.VMEM((size, width), BF16)], cost=3)


def memory_kernel(core, others, mines, key_ref, value_ref, out_ref):
    out_ref[...] = back_product(core, others, mines, key_ref, 1) + back_product(
        core, others, mines, value_ref, 2
    )


def memory_step(flow, core, others, mines, weights, at):
    size, width = others.shape[1], weights.shape[2]
    return flow.call(
        memory_kernel,
        "memory_step",
        (core,),
        (1,),
        [
            whole(others),
            whole(mines),
            (weights, pl.BlockSpec((1, width, width), lambda *_: (at, 0, 0))),
            (weights, pl.BlockSpec((1, width, width), lambda *_: (at + 1, 0, 0))),
        ],
        [((size, width), F32, full_spec((size, width)))], cost=3)[0]


def last_kernel(core, others, mines, hidden_ref, gain_ref, carry_ref, w_one, w_two, w_three, out_ref, gain_grad_ref):
    back = (
        back_product(core, others, mines, w_one, 0)
        + back_product(core, others, mines, w_two, 1)
        + back_product(core, others, mines, w_three, 2)
    )
    residual, gain_grad = rms_backward(hidden_ref[...].astype(F32), gain_ref[...], back)
    gain_grad_ref[...] = gain_grad
    out_ref[...] = carry_ref[...] + residual


def last_step(flow, core, others, mines, hidden, gain, carry, weights):
    size, width = hidden.shape
    return flow.call(
        last_kernel,
        "last_step",
        (core,),
        (1,),
        [whole(others), whole(mines), whole(hidden), whole(gain), whole(carry)]
        + [
            (weights, pl.BlockSpec((1, width, width), functools.partial(lambda at, *_: (at, 0, 0), at)))
            for at in range(3)
        ],
        [
            ((size, width), F32, full_spec((size, width))),
            ((1, width), F32, full_spec((1, width))),
        ], cost=5.5)


def take(array, part):
    return array[...] if part is None else array[part]


def weight_grads_kernel(plan, row_count, grad_count, picks, *refs):
    rows, rows_got = refs[:row_count], refs[row_count : 2 * row_count]
    refs = refs[2 * row_count :]
    grads, grads_got = refs[:grad_count], refs[grad_count : 2 * grad_count]
    keep_ref, send_ref, total_ref = refs[2 * grad_count :]
    half, tall = keep_ref.shape[0], keep_ref.shape[2]
    for at, (row, row_part, grad, part) in enumerate(plan):
        total = dot(take(rows[row], row_part), take(grads[grad], part), TN)
        total = total + dot(take(rows_got[row], row_part), take(grads_got[grad], part), TN)
        total_ref[...] = total.astype(BF16).reshape(total_ref.shape)
        for place in range(half):
            keep_ref[place, at] = total_ref[picks[place]]
            send_ref[place, at] = total_ref[picks[half + place]]


def weight_grads(links, flow, order, plan, rows, rows_got, grads, grads_got):
    picks = links.places(links.core, order[::-1])
    count = 2 * links.owners
    height = rows[plan[0][0]].shape[-1]
    columns = grads[plan[0][2]].shape[-1]
    tall = height // count
    if tall % 16 == 0:
        shape = (count // 2, len(plan), tall, columns)
        return flow.call(
            functools.partial(weight_grads_kernel, plan, len(rows), len(grads)),
            "weight_grads",
            (picks,),
            (1,),
            [whole(item) for item in (*rows, *rows_got, *grads, *grads_got)],
            [(shape, BF16, full_spec(shape)), (shape, BF16, full_spec(shape))],
            [pltpu.VMEM((count, tall, columns), BF16)],
            room=16, cost=5)
    stack = []
    for row, row_part, grad, part in plan:
        total = dot(take(rows[row], row_part), take(grads[grad], part), TN)
        total = total + dot(take(rows_got[row], row_part), take(grads_got[grad], part), TN)
        stack.append(total.astype(BF16).reshape(count, tall, columns))
    stack = jnp.stack(stack, axis=1)[picks]
    return stack[: count // 2], stack[count // 2 :]


def attend_forward(flow, lengths, offs, stack):
    causal = offs is not None
    _, size, width = stack.shape
    pairs = HEADS // 2

    def part(at):
        return (stack, pl.BlockSpec((1, size, 2 * HEAD), lambda p, *_: (at, 0, p)))

    lanes = pl.BlockSpec((1, 2, size), lambda p, *_: (p, 0, 0))
    ins = [part(0), part(1), part(2)]
    if causal:
        ins = [(offs, lanes)] + ins
    return flow.call(
        functools.partial(forward_kernel, causal),
        "attend_forward_self" if causal else "attend_forward_cross",
        (lengths,),
        (pairs,),
        ins,
        [
            ((size, width), BF16, pl.BlockSpec((size, 2 * HEAD), lambda p, *_: (0, p))),
            ((pairs, 2, size), F32, lanes),
        ],
        cost=11,
    )


def attend_backward(flow, lengths, core, other, offs, stack, g, lse):
    causal = offs is not None
    _, size, width = stack.shape
    pairs = HEADS // 4

    def pair(p, core):
        return (1 - core[0] if other else core[0]) * pairs + p

    def part(at):
        return (stack, pl.BlockSpec((1, size, 2 * HEAD), lambda p, _, core: (at, 0, pair(p, core))))

    lanes = pl.BlockSpec((1, 2, size), lambda p, _, core: (pair(p, core), 0, 0))
    ins = [part(0), part(1), part(2)]
    ins = ins + [(g, pl.BlockSpec((size, 2 * HEAD), lambda p, _, core: (0, pair(p, core)))), (lse, lanes)]
    outs = [((3, size, width // 2), BF16, pl.BlockSpec((3, size, 2 * HEAD), lambda p, *_: (0, 0, p)))]
    if causal:
        ins = [(offs, lanes)] + ins
        outs = outs + [((pairs, 2, size), F32, pl.BlockSpec((1, 2, size), lambda p, *_: (p, 0, 0)))]
    return flow.call(
        functools.partial(backward_kernel, causal),
        "attend_backward_self" if causal else "attend_backward_cross",
        (lengths, core),
        (pairs,),
        ins,
        outs,
        cost=8,
    )


class Links:
    def __init__(self, reps, owners, width):
        self.owners = owners
        self.width = width
        self.bits = owners.bit_length() - 1
        self.count = reps * owners
        self.rep = lax.axis_index("rep")
        self.owner = lax.axis_index("fsdp")
        self.core = self.rep % 2
        self.side = self.rep // 2
        self.core_word = self.core.reshape(1).astype(jnp.int32)
        self.side_word = self.side.reshape(1).astype(jnp.int32)

    def move(self, array, target):
        return lax.ppermute(
            array, ("rep", "fsdp"), [(device, target(device)) for device in range(self.count)]
        )

    def over_owner(self, array, bit):
        return self.move(array, lambda device: device ^ (1 << bit))

    def over_core(self, array):
        return self.move(array, lambda device: device ^ self.owners)

    def over_side(self, array):
        return self.move(array, lambda device: device ^ (2 * self.owners))

    def over_pair(self, array, first):
        def target(device):
            core = (device // self.owners) % 2
            return device ^ (1 if (core == 0) == first else 2 * self.owners)

        return self.move(array, target)

    def step(self, array, name):
        if name == "first":
            return self.over_pair(array, True)
        if name == "second":
            return self.over_pair(array, False)
        return self.over_owner(array, name)

    def far_to_near(self):
        return tuple(range(self.bits - 1, 0, -1))

    def places(self, core, order):
        index = jnp.arange(2 * self.owners)
        owner = jnp.full_like(index, self.owner)
        side = jnp.full_like(index, self.side)
        for at, name in enumerate(order):
            flip = (index >> at) & 1
            if name == "first":
                owner = owner ^ jnp.where(core == 0, flip, 0)
                side = side ^ jnp.where(core == 0, 0, flip)
            elif name == "second":
                owner = owner ^ jnp.where(core == 0, 0, flip)
                side = side ^ jnp.where(core == 0, flip, 0)
            else:
                owner = owner ^ (flip << name)
        return (owner * 2 + side).astype(jnp.int32)


def assemble_kernel(places, core, *refs):
    sources, out_ref, sems = refs[:2], refs[2], refs[3]
    width = sources[0].shape[-1]
    copies = []
    for half in range(2):
        column = core[0] if half == 0 else 1 - core[0]
        start = pl.multiple_of(column * width, width)
        tall = out_ref.shape[-1] == width
        for at in range(sources[half].shape[0]):
            copies.append(
                pltpu.make_async_copy(
                    sources[half].at[at],
                        out_ref.at[pl.ds(column, 1), places[half, at]]
                        if tall
                        else out_ref.at[:, places[half, at], :, pl.ds(start, width)],
                    sems.at[half, at],
                )
            )
    for copy in copies:
        copy.start()
    for copy in copies:
        copy.wait()


def assemble(links, flow, order, own, other, tall=False):
    places = jnp.stack([links.places(links.core, order), links.places(1 - links.core, order)])
    count, weights, rows, columns = own.shape
    if tall:
        shape = (2, count, rows, columns)
    else:
        shape = (weights, count, rows, 2 * columns)
    out = flow.call(
        assemble_kernel,
        "assemble",
        (places, links.core_word),
        (1,),
        [whole(own), whole(other)],
        [(shape, BF16, full_spec(shape))],
        [pltpu.SemaphoreType.DMA((2, count))],
        room=14,
        cost=3.5,
    )[0]
    if tall:
        return out.reshape(2 * count * rows, columns)
    return out.reshape(weights, count * rows, 2 * columns)


def pack_kernel(counts, core, *refs):
    total = sum(counts)
    shards, blocks, sems = refs[:total], refs[total:-1], refs[-1]
    copies = []
    for count, block in zip(counts, blocks):
        high, wide = block.shape[2], block.shape[3]
        rows = pl.ds(pl.multiple_of(core[1] * high, high), high)
        columns = pl.ds(pl.multiple_of(core[0] * wide, wide), wide)
        for index in range(count):
            copies.append(
                pltpu.make_async_copy(
                    shards[len(copies)].at[rows, columns], block.at[0, index], sems.at[len(copies)]
                )
            )
    for copy in copies:
        copy.start()
    for copy in copies:
        copy.wait()


def pack(links, flow, groups):
    high, wide = groups[0][0].shape
    high, wide = high // 2, wide // 2
    counts = [len(group) for group in groups]
    if high % 16 == 0:
        shapes = [(1, count, high, wide) for count in counts]
        return flow.call(
            functools.partial(pack_kernel, counts),
            "pack",
            (jnp.stack([links.core, links.side]).astype(jnp.int32),),
            (1,),
            [(shard, pl.BlockSpec(memory_space=pl.ANY)) for group in groups for shard in group],
            [(shape, BF16, full_spec(shape)) for shape in shapes],
            [pltpu.SemaphoreType.DMA((sum(counts),))],
        )
    at = (links.side * high, links.core * wide)
    return [
        jnp.stack([lax.dynamic_slice(shard, at, (high, wide)) for shard in group])[None] for group in groups
    ]


def gather_feed(links, reps, gate, up, down):
    owners = links.owners
    share, units = gate.shape
    wide = units // reps
    high, width = down.shape
    high = high // reps
    gate = lax.dynamic_slice_in_dim(gate, links.rep * wide, wide, 1)
    up = lax.dynamic_slice_in_dim(up, links.rep * wide, wide, 1)
    down = lax.dynamic_slice_in_dim(down, links.rep * high, high, 0)
    fine = share == width // 8
    if fine:
        down = down.reshape(wide // 128, 16, share // 16, 128).transpose(2, 1, 0, 3)
    down = down.reshape(share, wide)
    full = lax.all_gather(jnp.stack([gate, up, down]), ("fsdp", "rep"), axis=0)
    full = full.reshape(owners, reps, 3, share, wide)
    if fine:
        return full
    half = units // owners // 2
    parts = []
    for at in range(2):
        part = full[:, :, at].transpose(0, 2, 1, 3).reshape(width, 8, owners // 8, 2, half)
        part = part.transpose(0, 1, 3, 2, 4).reshape(8, width // 8, reps, wide)
        parts.append(part.transpose(0, 2, 1, 3))
    down = full[:, :, 2].reshape(8, owners // 8, 2, half, width).transpose(0, 2, 1, 3, 4)
    down = down.reshape(8, reps, wide // 128, 16, width // 128, 128).transpose(0, 1, 4, 3, 2, 5)
    parts.append(down.reshape(8, reps, width // 8, wide))
    return jnp.stack(parts, axis=2)


class Reduce:
    def __init__(self, links, flow, order, keep, send, tall=False):
        self.links, self.flow, self.order, self.tall = links, flow, order, tall
        self.keep, self.send = keep, send
        self.taken = 0
        self.start()

    def start(self):
        self.got = self.links.step(self.send, self.order[self.taken])
        self.taken += 1

    def advance(self, *extra):
        self.keep, self.send, *more = halve(self.flow, self.keep, self.got, extra)
        self.start()
        return more[0] if more else None

    def rest(self):
        while self.taken < len(self.order):
            self.advance()

    def sides(self, *extra):
        mine, *more = add(self.flow, self.keep, self.got, extra)
        self.keep, self.got = mine, self.links.over_side(mine)
        return more[0] if more else None

    def cores(self, *extra):
        mine, *more = stack(self.flow, self.links.side_word, self.keep, self.got, extra)
        self.keep, self.got = mine, self.links.over_core(mine)
        return more[0] if more else None

    def outs(self):
        return unpack(self.flow, self.links, self.keep, self.got, self.tall)


def add_kernel(*refs):
    out_ref = refs[-1] if len(refs) == 3 else refs[-2]
    out_ref[...] = (refs[0][0].astype(F32) + refs[1][0].astype(F32)).astype(BF16)
    if len(refs) > 3:
        refs[-1][...] = refs[2][...] + refs[3][...]


def add(flow, one, two, extra):
    shape = one.shape[1:]
    return flow.call(
        add_kernel,
        "add",
        (),
        (1,),
        [whole(one), whole(two)] + extra_ins(extra),
        [(shape, BF16, full_spec(shape))] + extra_outs(extra),
    )


def stack_kernel(first, *refs):
    out_ref = refs[-1] if len(refs) == 3 else refs[-2]
    out_ref[:, pl.ds(first[0], 1)] = refs[0][...][:, None]
    out_ref[:, pl.ds(1 - first[0], 1)] = refs[1][...][:, None]
    if len(refs) > 3:
        refs[-1][...] = refs[2][...] + refs[3][...]


def stack(flow, first, one, two, extra):
    weights, rows, columns = one.shape
    shape = (weights, 2, rows, columns)
    out, *more = flow.call(
        stack_kernel,
        "stack",
        (first,),
        (1,),
        [whole(one), whole(two)] + extra_ins(extra),
        [(shape, BF16, full_spec(shape))] + extra_outs(extra),
    )
    return (out.reshape(weights, 2 * rows, columns), *more)


def unpack_kernel(tall, owners, core, one_ref, two_ref, *out_refs):
    for index, out_ref in enumerate(out_refs):
        for half, ref in enumerate((one_ref, two_ref)):
            at = core[0] if half == 0 else 1 - core[0]
            value = ref[index].astype(F32)
            rows, columns = value.shape
            parts = owners if columns % (owners * 128) == 0 else 1
            wide = columns // parts
            if tall:
                out_ref[pl.ds(pl.multiple_of(at * rows, rows), rows)] = value
            else:
                for part in range(parts):
                    start = pl.multiple_of((2 * part + at) * wide, wide)
                    out_ref[:, pl.ds(start, wide)] = value[:, part * wide : (part + 1) * wide]


def unpack(flow, links, one, two, tall):
    weights, rows, columns = one.shape
    if rows % 16:
        first = links.core == 0
        one, two = jnp.where(first, one, two), jnp.where(first, two, one)
        if tall:
            mine = jnp.concatenate([one, two], axis=1)
        elif 2 * columns > links.width:
            mine = jnp.stack([one, two], axis=2).reshape(weights, rows, 2, links.owners, -1)
            mine = mine.transpose(0, 1, 3, 2, 4).reshape(weights, rows, 2 * columns)
        else:
            mine = jnp.concatenate([one, two], axis=2)
        return list(mine.astype(F32))
    shape = (2 * rows, columns) if tall else (rows, 2 * columns)
    return flow.call(
        functools.partial(unpack_kernel, tall, links.owners),
        "unpack",
        (links.core_word,),
        (1,),
        [whole(one), whole(two)],
        [(shape, F32, full_spec(shape))] * weights,
    )


def pack_small_kernel(*refs):
    out_ref = refs[-1]
    for index, ref in enumerate(refs[:-1]):
        out_ref[index : index + 1, : ref.shape[1]] = ref[...]


def pack_small(flow, vectors):
    width = max(item.shape[1] for item in vectors)
    shape = (8, width)
    return flow.call(
        pack_small_kernel, "pack_small", (), (1,), [whole(item) for item in vectors], [(shape, F32, full_spec(shape))]
    )[0]


def on_device(
    reps,
    owners,
    hidden,
    memory,
    lengths,
    buckets,
    cotangent,
    self_gain,
    self_query,
    self_key,
    self_value,
    self_out,
    bias_table,
    cross_gain,
    cross_query,
    cross_key,
    cross_value,
    cross_out,
    feed_gain,
    feed_gate,
    feed_up,
    feed_down,
):
    width = hidden.shape[2]
    share = width // owners
    links = Links(reps, owners, width)
    hidden, memory, cotangent = hidden[0], memory[0], cotangent[0]
    flow = Flow()
    core = links.core_word
    far = links.far_to_near()
    order = far + ("first", "second")
    w_feed = gather_feed(links, reps, feed_gate, feed_up, feed_down)
    small = jnp.concatenate([self_gain, cross_gain, feed_gain, bias_table])[None]
    bits = list(range(links.bits - 1, -1, -1))
    a, b = pack(
        links,
        flow,
        (
            (self_query, self_key, self_value),
            (self_out, cross_query, cross_key, cross_value, cross_out),
        ),
    )
    for at, name in enumerate(order[:-1]):
        pairs = [(a, links.step(a, name))]
        if at > 0:
            pairs.append((b, links.step(b, order[at - 1])))
        if bits:
            tiny = links.over_owner(small, bits.pop(0))
            flow.after(tiny)
            small = jnp.concatenate([small, tiny], axis=0)
        if at > 0:
            (a,) = double(flow, pairs[:1])
            (b,) = double(flow, pairs[1:])
        else:
            (a,) = double(flow, pairs)
    apart = jnp.arange(owners) ^ links.owner
    place = sum(((apart >> bit) & 1) << (links.bits - 1 - bit) for bit in range(links.bits))
    small = small[place].astype(F32)
    gain_one = small[:, :share].reshape(1, -1)
    gain_two = small[:, share : 2 * share].reshape(1, -1)
    gain_three = small[:, 2 * share : 3 * share].reshape(1, -1)
    table = small[:, 3 * share :].reshape(BUCKETS, HEADS)
    picks = (buckets[:, None] == jnp.arange(BUCKETS)[None, :]).astype(F32)
    offsets = jnp.dot(picks, table, precision=PRECISE).T.reshape(HEADS // 2, 2, -1)

    memory_got = links.over_core(memory)
    (a,) = double(flow, [(a, links.step(a, order[-1]))])
    flow.after(memory_got)
    cotangent_got = links.over_core(cotangent)
    flow.after(offsets)
    b_got = links.step(b, order[-2])
    w_self = assemble(links, flow, order, a, links.over_core(a))
    flow.after(cotangent_got)
    normed_one, qkv = query_step(flow, core, hidden, gain_one, w_self)
    normed_one_got = links.over_core(normed_one)
    (b,) = double(flow, [(b, b_got)])
    b_got = links.step(b, order[-1])
    mixed_one, lse_one = attend_forward(flow, lengths, offsets, qkv)
    mixed_one_got = links.over_core(mixed_one)
    flow.after(normed_one_got)
    (b,) = double(flow, [(b, b_got)])
    w_cross = assemble(links, flow, order, b, links.over_core(b))
    after_self, normed_two, cross_qkv = cross_step(
        flow, core, mixed_one, hidden, memory, gain_two, w_cross
    )
    normed_two_got = links.over_core(normed_two)
    mixed_two, lse_two = attend_forward(flow, lengths, None, cross_qkv)
    mixed_two_got = links.over_core(mixed_two)
    flow.after(normed_two_got, mixed_one_got)
    after_cross, normed_three = out_step(flow, core, mixed_two, after_self, gain_three, w_cross, 4)
    normed_three_got = links.over_core(normed_three)
    flow.after(mixed_two_got, normed_three_got)
    parts_other, out, back = feed_first(flow, core, normed_three, cotangent, w_feed)
    parts_got = links.over_core(parts_other)
    (
        parts,
        layer_out,
        carry_two,
        gain_three_grad,
        branch_other,
        branch_two,
        mixed_grad,
    ) = feed_second(
        flow,
        core,
        normed_three,
        cotangent,
        w_feed,
        out,
        back,
        after_cross,
        gain_three,
        w_cross,
        4,
    )
    branch_two_got = links.over_core(branch_other)

    down = order[::-1]
    sums_c = Reduce(
        links,
        flow,
        down,
        *weight_grads(
            links,
            flow,
            down,
            [(0, None, 0, 1), (0, None, 0, 2)],
            [normed_three],
            [normed_three_got],
            [parts],
            [parts_got],
        ),
    )
    sums_d = Reduce(
        links,
        flow,
        down,
        *weight_grads(
            links,
            flow,
            down,
            [(0, 0, 0, None)],
            [parts],
            [parts_got],
            [cotangent],
            [cotangent_got],
        ),
        tall=True,
    )
    (cross_other,) = attend_backward(flow, lengths, core, True, None, cross_qkv, mixed_grad, lse_two)
    cross_got = links.over_core(cross_other)
    flow.after(branch_two_got)
    (cross_mine,) = attend_backward(flow, lengths, core, False, None, cross_qkv, mixed_grad, lse_two)
    sums_c.advance()
    carry_one, gain_two_grad, branch_other, branch_one, mixed_grad = middle_step(
        flow, core, cross_other, cross_mine, after_self, gain_two, carry_two, w_cross, 1, 0
    )
    branch_one_got = links.over_core(branch_other)
    sums_d.advance()
    sums_b = Reduce(
        links,
        flow,
        down,
        *weight_grads(
            links,
            flow,
            down,
            [
                (0, None, 0, None),
                (1, None, 1, 0),
                (2, None, 1, 1),
                (2, None, 1, 2),
                (3, None, 2, None),
            ],
            [mixed_one, normed_two, memory, mixed_two],
            [mixed_one_got, normed_two_got, memory_got, mixed_two_got],
            [branch_one, cross_mine, branch_two],
            [branch_one_got, cross_got, branch_two_got],
        ),
    )
    sums_c.advance()
    self_other, offsets_other = attend_backward(
        flow, lengths, core, True, offsets, qkv, mixed_grad, lse_one
    )
    self_got = links.over_core(self_other)
    sums_d.advance()
    self_mine, offsets_mine = attend_backward(
        flow, lengths, core, False, offsets, qkv, mixed_grad, lse_one
    )
    sums_b.advance()
    sums_a = Reduce(
        links,
        flow,
        down,
        *weight_grads(
            links,
            flow,
            down,
            [(0, None, 0, 0), (0, None, 0, 1), (0, None, 0, 2)],
            [normed_one],
            [normed_one_got],
            [self_mine],
            [self_got],
        ),
    )
    sums_c.advance()
    sums_d.advance()
    sums_b.advance()
    input_grad, gain_one_grad = last_step(
        flow, core, self_other, self_mine, hidden, gain_one, carry_one, w_self
    )
    first = links.core == 0
    offset_grad = jnp.concatenate(
        [
            jnp.where(first, offsets_mine, offsets_other),
            jnp.where(first, offsets_other, offsets_mine),
        ],
        axis=0,
    ).reshape(HEADS, -1)
    table_grad = jnp.dot(picks.T, offset_grad.T, precision=PRECISE).reshape(1, -1)
    small = pack_small(flow, [gain_one_grad, gain_two_grad, gain_three_grad, table_grad])
    sums_a.advance()
    moves = [links.over_core, links.over_side] + [
        functools.partial(links.over_owner, bit=bit) for bit in range(links.bits)
    ]
    small_got = moves.pop(0)(small)
    sums_c.rest()
    sums_c.sides()
    sums_d.rest()
    sums_d.sides()
    memory_grad = memory_step(flow, core, cross_other, cross_mine, w_cross, 2)
    while sums_a.taken < len(down):
        small = sums_a.advance(small, small_got)
        small_got = moves.pop(0)(small)
        if sums_b.taken < len(down):
            sums_b.advance()
        else:
            sums_b.sides()
        if sums_a.taken == len(down) - 1:
            sums_c.cores()
            sums_d.cores()
    small = sums_a.sides(small, small_got)
    small_got = moves.pop(0)(small)
    (total_d,) = sums_d.outs()
    total_c = sums_c.outs()
    sums_b.cores()
    small = sums_a.cores(small, small_got)
    small_got = moves.pop(0)(small)
    while moves:
        small = small + small_got
        small_got = moves.pop(0)(small)
    small = small + small_got
    total_b = sums_b.outs()
    total_a = sums_a.outs()
    small_table = lax.dynamic_slice_in_dim(
        small[3], links.owner * bias_table.shape[0], bias_table.shape[0], 0
    )
    small = lax.dynamic_slice_in_dim(small, links.owner * share, share, 1)
    return (
        layer_out[None],
        input_grad[None],
        memory_grad[None],
        small[0],
        total_a[0],
        total_a[1],
        total_a[2],
        total_b[0],
        small_table,
        small[1],
        total_b[1],
        total_b[2],
        total_b[3],
        total_b[4],
        small[2],
        total_c[0],
        total_c[1],
        total_d,
    )


def solution(mesh):
    rows = P(("rep", "fsdp"), None, None)
    vector = P("fsdp")
    matrix = P("fsdp", None)
    attention = (vector,) + (matrix,) * 4
    return jax.shard_map(
        functools.partial(on_device, mesh.shape["rep"], mesh.shape["fsdp"]),
        mesh=mesh,
        in_specs=(rows, rows, P(("rep", "fsdp")), P(), rows)
        + attention
        + (vector,)
        + attention
        + (vector, matrix, matrix, matrix),
        out_specs=(rows, rows, rows)
        + attention
        + (vector,)
        + attention
        + (vector, matrix, matrix, matrix),
        check_vma=False,
    )
```

```python
import functools
import jax
import jax.numpy as jnp
from jax import lax
from jax.experimental import pallas as pl
from jax.experimental.pallas import tpu as pltpu
from jax.sharding import PartitionSpec as P

HEADS = 12
HEAD = 64
BUCKETS = 32
EPSILON = 1e-06
MASKED = -1e30
PRECISE = lax.Precision.HIGHEST
MIB = 1024 * 1024
MICROSECOND = 3e9
F32 = jnp.float32
BF16 = jnp.bfloat16
NT = (((1,), (1,)), ((), ()))
NN = (((1,), (0,)), ((), ()))
TN = (((0,), (0,)), ((), ()))
TILE = 128


def dot(a, b, dims):
    return lax.dot_general(a, b, dims, preferred_element_type=F32)


def bias_tiles(offs, length):
    base = pltpu.roll(jnp.broadcast_to(offs, (TILE, length)), 0, 1, stride=1, stride_axis=0)
    key = lax.broadcasted_iota(jnp.int32, (TILE, TILE), 0)
    item = lax.broadcasted_iota(jnp.int32, (TILE, TILE), 1)
    first = jnp.where(item >= key, base[:, :TILE], MASKED)
    return jnp.concatenate([jnp.full((TILE, TILE), MASKED, F32), first, base[:, TILE:]], axis=1)


def diagonal_sums(spread, length):
    total = spread[:8]
    for at in range(8, TILE, 8):
        total = total + pltpu.roll(spread[at : at + 8], length - at, 1)
    row = lax.broadcasted_iota(jnp.int32, total.shape, 0)
    for bit in (1, 2, 4):
        total = jnp.where((row & bit) != 0, pltpu.roll(total, length - bit, 1), total)
    return jnp.sum(total, axis=0, keepdims=True)


def bias_block(tiles, first, rows, step):
    parts = []
    for block in range(rows // TILE):
        at = first - block * TILE + TILE
        parts.append(tiles[:, at : at + step])
    return jnp.concatenate(parts, axis=0)


def refused(rows, length):
    key = lax.broadcasted_iota(jnp.int32, (rows, 1), 0)
    return jnp.where(key < length, 0.0, MASKED)


def forward_kernel(causal, lengths, *refs):
    if causal:
        offs_ref, q_ref, k_ref, v_ref, mixed_ref, lse_ref = refs
    else:
        q_ref, k_ref, v_ref, mixed_ref, lse_ref = refs
    q_ref, k_ref, v_ref = q_ref.at[0], k_ref.at[0], v_ref.at[0]
    size = q_ref.shape[0]
    step = 256
    length = lengths[0]
    for head in range(2):
        cols = slice(head * HEAD, (head + 1) * HEAD)
        if causal:
            tiles = bias_tiles(offs_ref[0, head : head + 1, :], size)
        for first in range(0, size, step):
            rows = first + step if causal else size
            scores = dot(k_ref[:rows, cols], q_ref[first : first + step, cols], NT)
            if causal:
                scores = scores + bias_block(tiles, first, rows, step)
            scores = scores + refused(rows, length)
            highest = jnp.max(scores, axis=0, keepdims=True)
            weights = jnp.exp(scores - highest)
            total = jnp.sum(weights, axis=0, keepdims=True)
            mixed = dot(v_ref[:rows, cols], weights.astype(BF16), TN) * (1.0 / total)
            mixed_ref[first : first + step, cols] = mixed.T.astype(BF16)
            lse_ref[0, head : head + 1, first : first + step] = highest + jnp.log(total)


def backward_kernel(causal, lengths, core, *refs):
    if causal:
        offs_ref, q_ref, k_ref, v_ref, g_ref, lse_ref, grads_ref, doffs_ref = refs
    else:
        q_ref, k_ref, v_ref, g_ref, lse_ref, grads_ref = refs
    q_ref, k_ref, v_ref = q_ref.at[0], k_ref.at[0], v_ref.at[0]
    dq_ref, dk_ref, dv_ref = grads_ref.at[0], grads_ref.at[1], grads_ref.at[2]
    size = q_ref.shape[0]
    step = 256
    length = lengths[0]
    for head in range(2):
        cols = slice(head * HEAD, (head + 1) * HEAD)
        if causal:
            tiles = bias_tiles(offs_ref[0, head : head + 1, :], size)
            spread = [jnp.zeros((TILE, TILE), F32) for _ in range(size // TILE)]
        dk = [None] * (size // step)
        dv = [None] * (size // step)
        for first in range(0, size, step):
            rows = first + step if causal else size
            q = q_ref[first : first + step, cols]
            g = g_ref[first : first + step, cols]
            k = k_ref[:rows, cols]
            scores = dot(k, q, NT)
            if causal:
                scores = scores + bias_block(tiles, first, rows, step)
            scores = scores + refused(rows, length)
            probs = jnp.exp(scores - lse_ref[0, head : head + 1, first : first + step])
            prob_grad = dot(v_ref[:rows, cols], g, NT)
            delta = jnp.sum(probs * prob_grad, axis=0, keepdims=True)
            score_grad = (probs * (prob_grad - delta)).astype(BF16)
            if causal:
                for block in range(rows // TILE):
                    for lane in range(step // TILE):
                        at = first // TILE + lane - block
                        if at >= 0:
                            spread[at] = spread[at] + score_grad[
                                block * TILE : (block + 1) * TILE, lane * TILE : (lane + 1) * TILE
                            ].astype(F32)
            dk_now = dot(score_grad, q, NN)
            dv_now = dot(probs.astype(BF16), g, NN)
            for block in range(rows // step):
                part = slice(block * step, (block + 1) * step)
                dk[block] = dk_now[part] if dk[block] is None else dk[block] + dk_now[part]
                dv[block] = dv_now[part] if dv[block] is None else dv[block] + dv_now[part]
            dq_ref[first : first + step, cols] = dot(k, score_grad, TN).T.astype(BF16)
        for block in range(size // step):
            part = slice(block * step, (block + 1) * step)
            dk_ref[part, cols] = dk[block].astype(BF16)
            dv_ref[part, cols] = dv[block].astype(BF16)
        if causal:
            doffs_ref[0, head : head + 1, :] = diagonal_sums(jnp.concatenate(spread, axis=1), size)


def full_spec(shape):
    zeros = (0,) * len(shape)
    return pl.BlockSpec(shape, lambda *_: zeros, pipeline_mode=pl.Buffered(1))


def corner_spec(shape):
    rows = 16 if shape[-2] % 16 == 0 else shape[-2]
    columns = 128 if shape[-1] % 128 == 0 else shape[-1]
    zeros = (0,) * len(shape)
    return pl.BlockSpec(
        (1,) * (len(shape) - 2) + (rows, columns), lambda *_: zeros, pipeline_mode=pl.Buffered(1)
    )


def rms(hidden, gain):
    scale = lax.rsqrt(jnp.mean(hidden * hidden, axis=-1, keepdims=True) + EPSILON)
    return hidden * scale * gain


def rms_backward(hidden, gain, upstream):
    scale = lax.rsqrt(jnp.mean(hidden * hidden, axis=-1, keepdims=True) + EPSILON)
    gain_grad = jnp.sum(upstream * (hidden * scale), axis=0, keepdims=True)
    weighted = upstream * gain
    inner = jnp.mean(weighted * hidden, axis=-1, keepdims=True)
    return scale * weighted - hidden * (scale * scale * scale) * inner, gain_grad


def half_at(core, other, width):
    return pl.multiple_of((1 - core if other else core) * width, width)


TICK = (8, 128)


def ticking(kernel, at, count, outputs, *refs):
    refs[outputs][...] = jnp.zeros(TICK, F32)
    kernel(*refs[:at], *refs[at + count : outputs], *refs[outputs + 1 :])


class Flow:
    def __init__(self):
        self.ticks = []

    def after(self, *arrays):
        self.ticks.extend(arrays)

    def call(self, kernel, name, scalars, grid, ins, outs, scratch=(), room=10, cost=1.0):
        count = len(scalars) + len(ins)
        late = len(self.ticks)
        *results, tick = pl.pallas_call(
            functools.partial(ticking, kernel, count, late, count + late + len(outs)),
            out_shape=tuple(jax.ShapeDtypeStruct(shape, kind) for shape, kind, _ in outs)
            + (jax.ShapeDtypeStruct(TICK, F32),),
            grid_spec=pltpu.PrefetchScalarGridSpec(
                num_scalar_prefetch=len(scalars),
                grid=grid,
                in_specs=[spec for _, spec in ins]
                + [corner_spec(item.shape) for item in self.ticks],
                out_specs=[spec for _, _, spec in outs] + [full_spec(TICK)],
                scratch_shapes=list(scratch),
            ),
            compiler_params=pltpu.CompilerParams(vmem_limit_bytes=room * MIB),
            cost_estimate=pl.CostEstimate(flops=int(cost * MICROSECOND), bytes_accessed=0, transcendentals=0),
            name=name,
        )(*scalars, *[array for array, _ in ins], *self.ticks)
        self.ticks = [tick]
        return results


def double_kernel(*refs):
    count = len(refs) // 3
    for one_ref, two_ref, out_ref in zip(refs[:count], refs[count : 2 * count], refs[2 * count :]):
        half = one_ref.shape[0]
        out_ref[:half] = one_ref[...]
        out_ref[half:] = two_ref[...]


def double(flow, pairs):
    shapes = [(2 * one.shape[0],) + one.shape[1:] for one, _ in pairs]
    return flow.call(
        double_kernel,
        "double",
        (),
        (1,),
        [whole(one) for one, _ in pairs] + [whole(two) for _, two in pairs],
        [(shape, BF16, full_spec(shape)) for shape in shapes],
    )


def halve_kernel(*refs):
    keep_one, keep_two, got_one, got_two = refs[:4]
    keep_ref, send_ref = refs[-3:-1] if len(refs) > 6 else refs[-2:]
    keep_ref[...] = (keep_one[...].astype(F32) + got_one[...].astype(F32)).astype(BF16)
    send_ref[...] = (keep_two[...].astype(F32) + got_two[...].astype(F32)).astype(BF16)
    if len(refs) > 6:
        refs[-1][...] = refs[4][...] + refs[5][...]


def extra_ins(extra):
    return [whole(item) for item in extra]


def extra_outs(extra):
    return [(extra[0].shape, F32, full_spec(extra[0].shape))] if extra else []


def halve(flow, keep, got, extra=()):
    half = keep.shape[0] // 2
    steps = min(half, 2)
    rest = keep.shape[1:]
    one = pl.BlockSpec((half // steps,) + rest, lambda i: (i, 0, 0, 0))
    two = pl.BlockSpec((half // steps,) + rest, lambda i: (steps + i, 0, 0, 0))
    out = ((half,) + rest, BF16, one)
    return flow.call(
        halve_kernel,
        "halve",
        (),
        (steps,),
        [(keep, one), (keep, two), (got, one), (got, two)] + extra_ins(extra),
        [out, out] + extra_outs(extra),
    )


def whole(array):
    return (array, full_spec(array.shape))


def query_kernel(core, hidden_ref, gain_ref, weight_ref, normed_ref, out_ref):
    @pl.when(pl.program_id(0) == 0)
    def _():
        normed_ref[...] = rms(hidden_ref[...].astype(F32), gain_ref[...]).astype(BF16)

    out_ref[0] = dot(normed_ref[...], weight_ref[0], NN).astype(BF16)


def query_step(flow, core, hidden, gain, weights):
    size, width = hidden.shape
    return flow.call(
        query_kernel,
        "query_step",
        (core,),
        (3,),
        [whole(hidden), whole(gain), (weights, pl.BlockSpec((1, width, width), lambda i, _: (i, 0, 0)))],
        [
            ((size, width), BF16, full_spec((size, width))),
            ((3, size, width), BF16, pl.BlockSpec((1, size, width), lambda i, _: (i, 0, 0))),
        ], cost=3)


def cross_kernel(core, mixed_ref, hidden_ref, memory_ref, gain_ref, weight_ref, after_ref, normed_ref, out_ref):
    step = pl.program_id(0)

    @pl.when(step == 0)
    def _():
        after = hidden_ref[...].astype(F32) + dot(mixed_ref[...], weight_ref[0], NN)
        after_ref[...] = after
        normed_ref[...] = rms(after, gain_ref[...]).astype(BF16)

    @pl.when(step == 1)
    def _():
        out_ref[0] = dot(normed_ref[...], weight_ref[0], NN).astype(BF16)

    @pl.when(step >= 2)
    def _():
        out_ref[0] = dot(memory_ref[...], weight_ref[0], NN).astype(BF16)


def cross_step(flow, core, mixed, hidden, memory, gain, weights):
    size, width = hidden.shape
    return flow.call(
        cross_kernel,
        "cross_step",
        (core,),
        (4,),
        [
            whole(mixed),
            whole(hidden),
            whole(memory),
            whole(gain),
            (weights, pl.BlockSpec((1, width, width), lambda i, _: (i, 0, 0))),
        ],
        [
            ((size, width), F32, full_spec((size, width))),
            ((size, width), BF16, full_spec((size, width))),
            (
                (3, size, width),
                BF16,
                pl.BlockSpec((1, size, width), lambda i, _: (jnp.maximum(i - 1, 0), 0, 0)),
            ),
        ], cost=5)


def out_kernel(core, mixed_ref, after_ref, gain_ref, weight_ref, out_ref, normed_ref):
    after = after_ref[...] + dot(mixed_ref[...], weight_ref[0], NN)
    out_ref[...] = after
    normed_ref[...] = rms(after, gain_ref[...]).astype(BF16)


def out_step(flow, core, mixed, after, gain, weights, at):
    size, width = mixed.shape
    return flow.call(
        out_kernel,
        "out_step",
        (core,),
        (1,),
        [
            whole(mixed),
            whole(after),
            whole(gain),
            (weights, pl.BlockSpec((1, width, width), lambda *_: (at, 0, 0))),
        ],
        [
            ((size, width), F32, full_spec((size, width))),
            ((size, width), BF16, full_spec((size, width))),
        ], cost=2.5)


def feed_tile(normed, cotangent, gate_w, up_w, down_w):
    gate = dot(normed, gate_w, NN)
    lift = dot(normed, up_w, NN)
    root = 0.7978845608028654
    square = gate * gate
    bend = jnp.tanh(root * gate * (1.0 + 0.044715 * square))
    half = 0.5 + 0.5 * bend
    active = gate * half
    slope = half + 0.5 * gate * (1.0 - bend * bend) * (root * (1.0 + 3 * 0.044715 * square))
    inner = (active * lift).astype(BF16)
    inner_grad = dot(cotangent, down_w, NT)
    gate_grad = (inner_grad * lift * slope).astype(BF16)
    lift_grad = (inner_grad * active).astype(BF16)
    out = dot(inner, down_w, NN)
    back = dot(gate_grad, gate_w, NT) + dot(lift_grad, up_w, NT)
    return inner, gate_grad, lift_grad, out, back


def feed_weights(half, gate_ref, up_ref, down_ref, down_w):
    start = pl.multiple_of(half * 128, 128)
    wide = []
    for ref in (gate_ref, up_ref):
        owners, _, _, rows, columns = ref.shape
        wide.append(
            jnp.concatenate(
                [
                    ref[:, 0, 0, :, pl.ds(start + at, 128)].reshape(owners * rows, 128)
                    for at in range(0, columns, 256)
                ],
                axis=1,
            )
        )
    for owner in range(2):
        for piece in range(2):
            for row in range(4):
                for column in range(6):
                    first = owner * 128 + piece * 64 + row * 16
                    down_w[first : first + 16, column * 128 : column * 128 + 128] = down_ref[
                        owner,
                        2 * half + piece,
                        0,
                        column * 16 : column * 16 + 16,
                        row * 128 : row * 128 + 128,
                    ]
    return wide[0], wide[1], down_w[...]


def feed_add(first, second, outs, values):
    step = pl.program_id(0)

    @pl.when(step == 0)
    def _():
        for ref, start, value in zip(outs, first, values):
            ref[...] = value if second is None else start[...] + value

    @pl.when(step > 0)
    def _():
        for ref, value in zip(outs, values):
            ref[...] += value


def feed_first_kernel(
    core, normed_ref, cot_ref, gate_ref, up_ref, down_ref, parts_ref, out_ref, back_ref, down_w
):
    weights = feed_weights(1 - core[0], gate_ref, up_ref, down_ref, down_w)
    inner, gate_grad, lift_grad, out, back = feed_tile(normed_ref[...], cot_ref[...], *weights)
    parts_ref[0] = inner
    parts_ref[1] = gate_grad
    parts_ref[2] = lift_grad
    feed_add((None, None), None, (out_ref, back_ref), (out, back))


def feed_second_kernel(
    core,
    normed_ref,
    cot_ref,
    gate_ref,
    up_ref,
    down_ref,
    out_in_ref,
    back_in_ref,
    after_ref,
    gain_ref,
    weight_ref,
    parts_ref,
    layer_ref,
    carry_ref,
    gain_grad_ref,
    other_ref,
    mine_ref,
    mixed_grad_ref,
    down_w,
    out_ref,
    back_ref,
    branch_ref,
):
    weights = feed_weights(core[0], gate_ref, up_ref, down_ref, down_w)
    inner, gate_grad, lift_grad, out, back = feed_tile(normed_ref[...], cot_ref[...], *weights)
    parts_ref[0] = inner
    parts_ref[1] = gate_grad
    parts_ref[2] = lift_grad
    feed_add((out_in_ref, back_in_ref), True, (out_ref, back_ref), (out, back))

    @pl.when(pl.program_id(0) == pl.num_programs(0) - 1)
    def _():
        after = after_ref[...]
        layer_ref[...] = (after + out_ref[...]).astype(BF16)
        residual, gain_grad = rms_backward(after, gain_ref[...], back_ref[...])
        gain_grad_ref[...] = gain_grad
        carry = cot_ref[...].astype(F32) + residual
        carry_ref[...] = carry
        branch_ref[...] = carry.astype(BF16)
        width = other_ref.shape[1]
        other_ref[...] = branch_ref[:, pl.ds(half_at(core[0], True, width), width)]
        mine_ref[...] = branch_ref[:, pl.ds(half_at(core[0], False, width), width)]
        mixed_grad_ref[...] = dot(branch_ref[...], weight_ref[0], NT).astype(BF16)


def feed_ins(normed, cotangent, weights):
    owners, pieces, _, rows, columns = weights.shape
    size = normed.shape[0]
    wide = [
        (
            weights,
            pl.BlockSpec(
                (owners, 1, 1, rows, columns), functools.partial(lambda at, i, _: (0, i, at, 0, 0), at)
            ),
        )
        for at in range(2)
    ]
    tall = (weights, pl.BlockSpec((2, pieces, 1, rows, columns), lambda i, _: (i, 0, 2, 0, 0)))
    units = pieces * columns // 2
    return (
        (owners // 2,),
        [whole(normed), whole(cotangent)] + wide + [tall],
        ((3, size, units), BF16, pl.BlockSpec((3, size, 256), lambda i, _: (0, 0, i))),
        pltpu.VMEM((256, normed.shape[1]), BF16),
    )


def feed_first(flow, core, normed, cotangent, weights):
    grid, ins, parts, scratch = feed_ins(normed, cotangent, weights)
    total = (normed.shape, F32, full_spec(normed.shape))
    return flow.call(
        feed_first_kernel, "feed_first", (core,), grid, ins, [parts, total, total], [scratch], room=50, cost=9
    )


def feed_second(flow, core, normed, cotangent, weights, out, back, after, gain, last, at):
    grid, ins, parts, scratch = feed_ins(normed, cotangent, weights)
    size, width = normed.shape
    ins = ins + [
        whole(out),
        whole(back),
        whole(after),
        whole(gain),
        (last, pl.BlockSpec((1, width, width), lambda *_: (at, 0, 0))),
    ]
    narrow = ((size, width // 2), BF16, full_spec((size, width // 2)))
    return flow.call(
        feed_second_kernel,
        "feed_second",
        (core,),
        grid,
        ins,
        [
            parts,
            ((size, width), BF16, full_spec((size, width))),
            ((size, width), F32, full_spec((size, width))),
            ((1, width), F32, full_spec((1, width))),
            narrow,
            narrow,
            ((size, width), BF16, full_spec((size, width))),
        ],
        [
            scratch,
            pltpu.VMEM((size, width), F32),
            pltpu.VMEM((size, width), F32),
            pltpu.VMEM((size, width), BF16),
        ],
        room=50,
        cost=11,
    )


def back_product(core, others, mines, weight_ref, at):
    width = others.shape[-1]
    return dot(
        others[at], weight_ref[0, :, pl.ds(half_at(core[0], True, width), width)], NT
    ) + dot(mines[at], weight_ref[0, :, pl.ds(half_at(core[0], False, width), width)], NT)


def middle_kernel(
    core,
    others,
    mines,
    after_ref,
    gain_ref,
    carry_in_ref,
    query_ref,
    weight_ref,
    carry_ref,
    gain_grad_ref,
    other_ref,
    mine_ref,
    mixed_grad_ref,
    branch_ref,
):
    back = back_product(core, others, mines, query_ref, 0)
    residual, gain_grad = rms_backward(after_ref[...], gain_ref[...], back)
    gain_grad_ref[...] = gain_grad
    carry = carry_in_ref[...] + residual
    carry_ref[...] = carry
    branch_ref[...] = carry.astype(BF16)
    width = other_ref.shape[1]
    other_ref[...] = branch_ref[:, pl.ds(half_at(core[0], True, width), width)]
    mine_ref[...] = branch_ref[:, pl.ds(half_at(core[0], False, width), width)]
    mixed_grad_ref[...] = dot(branch_ref[...], weight_ref[0], NT).astype(BF16)


def middle_step(flow, core, others, mines, after, gain, carry, weights, query_at, out_at):
    size, width = after.shape
    narrow = ((size, width // 2), BF16, full_spec((size, width // 2)))
    return flow.call(
        middle_kernel,
        "middle_step",
        (core,),
        (1,),
        [
            whole(others),
            whole(mines),
            whole(after),
            whole(gain),
            whole(carry),
            (weights, pl.BlockSpec((1, width, width), lambda *_: (query_at, 0, 0))),
            (weights, pl.BlockSpec((1, width, width), lambda *_: (out_at, 0, 0))),
        ],
        [
            ((size, width), F32, full_spec((size, width))),
            ((1, width), F32, full_spec((1, width))),
            narrow,
            narrow,
            ((size, width), BF16, full_spec((size, width))),
        ],
        [pltpu.VMEM((size, width), BF16)], cost=3)


def memory_kernel(core, others, mines, key_ref, value_ref, out_ref):
    out_ref[...] = back_product(core, others, mines, key_ref, 1) + back_product(
        core, others, mines, value_ref, 2
    )


def memory_step(flow, core, others, mines, weights, at):
    size, width = others.shape[1], weights.shape[2]
    return flow.call(
        memory_kernel,
        "memory_step",
        (core,),
        (1,),
        [
            whole(others),
            whole(mines),
            (weights, pl.BlockSpec((1, width, width), lambda *_: (at, 0, 0))),
            (weights, pl.BlockSpec((1, width, width), lambda *_: (at + 1, 0, 0))),
        ],
        [((size, width), F32, full_spec((size, width)))], cost=3)[0]


def last_kernel(core, others, mines, hidden_ref, gain_ref, carry_ref, w_one, w_two, w_three, out_ref, gain_grad_ref):
    back = (
        back_product(core, others, mines, w_one, 0)
        + back_product(core, others, mines, w_two, 1)
        + back_product(core, others, mines, w_three, 2)
    )
    residual, gain_grad = rms_backward(hidden_ref[...].astype(F32), gain_ref[...], back)
    gain_grad_ref[...] = gain_grad
    out_ref[...] = carry_ref[...] + residual


def last_step(flow, core, others, mines, hidden, gain, carry, weights):
    size, width = hidden.shape
    return flow.call(
        last_kernel,
        "last_step",
        (core,),
        (1,),
        [whole(others), whole(mines), whole(hidden), whole(gain), whole(carry)]
        + [
            (weights, pl.BlockSpec((1, width, width), functools.partial(lambda at, *_: (at, 0, 0), at)))
            for at in range(3)
        ],
        [
            ((size, width), F32, full_spec((size, width))),
            ((1, width), F32, full_spec((1, width))),
        ], cost=5.5)


def take(array, part):
    return array[...] if part is None else array[part]


def weight_grads_kernel(plan, row_count, grad_count, picks, *refs):
    rows, rows_got = refs[:row_count], refs[row_count : 2 * row_count]
    refs = refs[2 * row_count :]
    grads, grads_got = refs[:grad_count], refs[grad_count : 2 * grad_count]
    keep_ref, send_ref, total_ref = refs[2 * grad_count :]
    half, tall = keep_ref.shape[0], keep_ref.shape[2]
    for at, (row, row_part, grad, part) in enumerate(plan):
        total = dot(take(rows[row], row_part), take(grads[grad], part), TN)
        total = total + dot(take(rows_got[row], row_part), take(grads_got[grad], part), TN)
        total_ref[...] = total.astype(BF16).reshape(total_ref.shape)
        for place in range(half):
            keep_ref[place, at] = total_ref[picks[place]]
            send_ref[place, at] = total_ref[picks[half + place]]


def weight_grads(links, flow, order, plan, rows, rows_got, grads, grads_got):
    picks = links.places(links.core, order[::-1])
    count = 2 * links.owners
    height = rows[plan[0][0]].shape[-1]
    columns = grads[plan[0][2]].shape[-1]
    tall = height // count
    if tall % 16 == 0:
        shape = (count // 2, len(plan), tall, columns)
        return flow.call(
            functools.partial(weight_grads_kernel, plan, len(rows), len(grads)),
            "weight_grads",
            (picks,),
            (1,),
            [whole(item) for item in (*rows, *rows_got, *grads, *grads_got)],
            [(shape, BF16, full_spec(shape)), (shape, BF16, full_spec(shape))],
            [pltpu.VMEM((count, tall, columns), BF16)],
            room=16, cost=5)
    stack = []
    for row, row_part, grad, part in plan:
        total = dot(take(rows[row], row_part), take(grads[grad], part), TN)
        total = total + dot(take(rows_got[row], row_part), take(grads_got[grad], part), TN)
        stack.append(total.astype(BF16).reshape(count, tall, columns))
    stack = jnp.stack(stack, axis=1)[picks]
    return stack[: count // 2], stack[count // 2 :]


def attend_forward(flow, lengths, offs, stack):
    causal = offs is not None
    _, size, width = stack.shape
    pairs = HEADS // 2

    def part(at):
        return (stack, pl.BlockSpec((1, size, 2 * HEAD), lambda p, *_: (at, 0, p)))

    lanes = pl.BlockSpec((1, 2, size), lambda p, *_: (p, 0, 0))
    ins = [part(0), part(1), part(2)]
    if causal:
        ins = [(offs, lanes)] + ins
    return flow.call(
        functools.partial(forward_kernel, causal),
        "attend_forward_self" if causal else "attend_forward_cross",
        (lengths,),
        (pairs,),
        ins,
        [
            ((size, width), BF16, pl.BlockSpec((size, 2 * HEAD), lambda p, *_: (0, p))),
            ((pairs, 2, size), F32, lanes),
        ],
        cost=11,
    )


def attend_backward(flow, lengths, core, other, offs, stack, g, lse):
    causal = offs is not None
    _, size, width = stack.shape
    pairs = HEADS // 4

    def pair(p, core):
        return (1 - core[0] if other else core[0]) * pairs + p

    def part(at):
        return (stack, pl.BlockSpec((1, size, 2 * HEAD), lambda p, _, core: (at, 0, pair(p, core))))

    lanes = pl.BlockSpec((1, 2, size), lambda p, _, core: (pair(p, core), 0, 0))
    ins = [part(0), part(1), part(2)]
    ins = ins + [(g, pl.BlockSpec((size, 2 * HEAD), lambda p, _, core: (0, pair(p, core)))), (lse, lanes)]
    outs = [((3, size, width // 2), BF16, pl.BlockSpec((3, size, 2 * HEAD), lambda p, *_: (0, 0, p)))]
    if causal:
        ins = [(offs, lanes)] + ins
        outs = outs + [((pairs, 2, size), F32, pl.BlockSpec((1, 2, size), lambda p, *_: (p, 0, 0)))]
    return flow.call(
        functools.partial(backward_kernel, causal),
        "attend_backward_self" if causal else "attend_backward_cross",
        (lengths, core),
        (pairs,),
        ins,
        outs,
        cost=8,
    )


class Links:
    def __init__(self, reps, owners, width):
        self.owners = owners
        self.width = width
        self.bits = owners.bit_length() - 1
        self.count = reps * owners
        self.rep = lax.axis_index("rep")
        self.owner = lax.axis_index("fsdp")
        self.core = self.rep % 2
        self.side = self.rep // 2
        self.core_word = self.core.reshape(1).astype(jnp.int32)
        self.side_word = self.side.reshape(1).astype(jnp.int32)

    def move(self, array, target):
        return lax.ppermute(
            array, ("rep", "fsdp"), [(device, target(device)) for device in range(self.count)]
        )

    def over_owner(self, array, bit):
        return self.move(array, lambda device: device ^ (1 << bit))

    def over_core(self, array):
        return self.move(array, lambda device: device ^ self.owners)

    def over_side(self, array):
        return self.move(array, lambda device: device ^ (2 * self.owners))

    def over_pair(self, array, first):
        def target(device):
            core = (device // self.owners) % 2
            return device ^ (1 if (core == 0) == first else 2 * self.owners)

        return self.move(array, target)

    def step(self, array, name):
        if name == "first":
            return self.over_pair(array, True)
        if name == "second":
            return self.over_pair(array, False)
        return self.over_owner(array, name)

    def far_to_near(self):
        return tuple(range(self.bits - 1, 0, -1))

    def places(self, core, order):
        index = jnp.arange(2 * self.owners)
        owner = jnp.full_like(index, self.owner)
        side = jnp.full_like(index, self.side)
        for at, name in enumerate(order):
            flip = (index >> at) & 1
            if name == "first":
                owner = owner ^ jnp.where(core == 0, flip, 0)
                side = side ^ jnp.where(core == 0, 0, flip)
            elif name == "second":
                owner = owner ^ jnp.where(core == 0, 0, flip)
                side = side ^ jnp.where(core == 0, flip, 0)
            else:
                owner = owner ^ (flip << name)
        return (owner * 2 + side).astype(jnp.int32)


def assemble_kernel(places, core, *refs):
    sources, out_ref, sems = refs[:2], refs[2], refs[3]
    width = sources[0].shape[-1]
    copies = []
    for half in range(2):
        column = core[0] if half == 0 else 1 - core[0]
        start = pl.multiple_of(column * width, width)
        tall = out_ref.shape[-1] == width
        for at in range(sources[half].shape[0]):
            copies.append(
                pltpu.make_async_copy(
                    sources[half].at[at],
                        out_ref.at[pl.ds(column, 1), places[half, at]]
                        if tall
                        else out_ref.at[:, places[half, at], :, pl.ds(start, width)],
                    sems.at[half, at],
                )
            )
    for copy in copies:
        copy.start()
    for copy in copies:
        copy.wait()


def assemble(links, flow, order, own, other, tall=False):
    places = jnp.stack([links.places(links.core, order), links.places(1 - links.core, order)])
    count, weights, rows, columns = own.shape
    if tall:
        shape = (2, count, rows, columns)
    else:
        shape = (weights, count, rows, 2 * columns)
    out = flow.call(
        assemble_kernel,
        "assemble",
        (places, links.core_word),
        (1,),
        [whole(own), whole(other)],
        [(shape, BF16, full_spec(shape))],
        [pltpu.SemaphoreType.DMA((2, count))],
        room=14,
        cost=3.5,
    )[0]
    if tall:
        return out.reshape(2 * count * rows, columns)
    return out.reshape(weights, count * rows, 2 * columns)


def pack_kernel(counts, core, *refs):
    total = sum(counts)
    shards, blocks, sems = refs[:total], refs[total:-1], refs[-1]
    copies = []
    for count, block in zip(counts, blocks):
        high, wide = block.shape[2], block.shape[3]
        rows = pl.ds(pl.multiple_of(core[1] * high, high), high)
        columns = pl.ds(pl.multiple_of(core[0] * wide, wide), wide)
        for index in range(count):
            copies.append(
                pltpu.make_async_copy(
                    shards[len(copies)].at[rows, columns], block.at[0, index], sems.at[len(copies)]
                )
            )
    for copy in copies:
        copy.start()
    for copy in copies:
        copy.wait()


def pack(links, flow, groups):
    high, wide = groups[0][0].shape
    high, wide = high // 2, wide // 2
    counts = [len(group) for group in groups]
    if high % 16 == 0:
        shapes = [(1, count, high, wide) for count in counts]
        return flow.call(
            functools.partial(pack_kernel, counts),
            "pack",
            (jnp.stack([links.core, links.side]).astype(jnp.int32),),
            (1,),
            [(shard, pl.BlockSpec(memory_space=pl.ANY)) for group in groups for shard in group],
            [(shape, BF16, full_spec(shape)) for shape in shapes],
            [pltpu.SemaphoreType.DMA((sum(counts),))],
        )
    at = (links.side * high, links.core * wide)
    return [
        jnp.stack([lax.dynamic_slice(shard, at, (high, wide)) for shard in group])[None] for group in groups
    ]


def gather_feed(links, reps, gate, up, down):
    owners = links.owners
    share, units = gate.shape
    wide = units // reps
    high, width = down.shape
    high = high // reps
    gate = lax.dynamic_slice_in_dim(gate, links.rep * wide, wide, 1)
    up = lax.dynamic_slice_in_dim(up, links.rep * wide, wide, 1)
    down = lax.dynamic_slice_in_dim(down, links.rep * high, high, 0)
    fine = share == width // 8
    if fine:
        down = down.reshape(wide // 128, 16, share // 16, 128).transpose(2, 1, 0, 3)
    down = down.reshape(share, wide)
    full = lax.all_gather(jnp.stack([gate, up, down]), ("fsdp", "rep"), axis=0)
    full = full.reshape(owners, reps, 3, share, wide)
    if fine:
        return full
    half = units // owners // 2
    parts = []
    for at in range(2):
        part = full[:, :, at].transpose(0, 2, 1, 3).reshape(width, 8, owners // 8, 2, half)
        part = part.transpose(0, 1, 3, 2, 4).reshape(8, width // 8, reps, wide)
        parts.append(part.transpose(0, 2, 1, 3))
    down = full[:, :, 2].reshape(8, owners // 8, 2, half, width).transpose(0, 2, 1, 3, 4)
    down = down.reshape(8, reps, wide // 128, 16, width // 128, 128).transpose(0, 1, 4, 3, 2, 5)
    parts.append(down.reshape(8, reps, width // 8, wide))
    return jnp.stack(parts, axis=2)


class Reduce:
    def __init__(self, links, flow, order, keep, send, tall=False):
        self.links, self.flow, self.order, self.tall = links, flow, order, tall
        self.keep, self.send = keep, send
        self.taken = 0
        self.start()

    def start(self):
        self.got = self.links.step(self.send, self.order[self.taken])
        self.taken += 1

    def advance(self, *extra):
        self.keep, self.send, *more = halve(self.flow, self.keep, self.got, extra)
        self.start()
        return more[0] if more else None

    def rest(self):
        while self.taken < len(self.order):
            self.advance()

    def sides(self, *extra):
        mine, *more = add(self.flow, self.keep, self.got, extra)
        self.keep, self.got = mine, self.links.over_side(mine)
        return more[0] if more else None

    def cores(self, *extra):
        mine, *more = stack(self.flow, self.links.side_word, self.keep, self.got, extra)
        self.keep, self.got = mine, self.links.over_core(mine)
        return more[0] if more else None

    def outs(self):
        return unpack(self.flow, self.links, self.keep, self.got, self.tall)


def add_kernel(*refs):
    out_ref = refs[-1] if len(refs) == 3 else refs[-2]
    out_ref[...] = (refs[0][0].astype(F32) + refs[1][0].astype(F32)).astype(BF16)
    if len(refs) > 3:
        refs[-1][...] = refs[2][...] + refs[3][...]


def add(flow, one, two, extra):
    shape = one.shape[1:]
    return flow.call(
        add_kernel,
        "add",
        (),
        (1,),
        [whole(one), whole(two)] + extra_ins(extra),
        [(shape, BF16, full_spec(shape))] + extra_outs(extra),
    )


def stack_kernel(first, *refs):
    out_ref = refs[-1] if len(refs) == 3 else refs[-2]
    out_ref[:, pl.ds(first[0], 1)] = refs[0][...][:, None]
    out_ref[:, pl.ds(1 - first[0], 1)] = refs[1][...][:, None]
    if len(refs) > 3:
        refs[-1][...] = refs[2][...] + refs[3][...]


def stack(flow, first, one, two, extra):
    weights, rows, columns = one.shape
    shape = (weights, 2, rows, columns)
    out, *more = flow.call(
        stack_kernel,
        "stack",
        (first,),
        (1,),
        [whole(one), whole(two)] + extra_ins(extra),
        [(shape, BF16, full_spec(shape))] + extra_outs(extra),
    )
    return (out.reshape(weights, 2 * rows, columns), *more)


def unpack_kernel(tall, owners, core, one_ref, two_ref, *out_refs):
    for index, out_ref in enumerate(out_refs):
        for half, ref in enumerate((one_ref, two_ref)):
            at = core[0] if half == 0 else 1 - core[0]
            value = ref[index].astype(F32)
            rows, columns = value.shape
            parts = owners if columns % (owners * 128) == 0 else 1
            wide = columns // parts
            if tall:
                out_ref[pl.ds(pl.multiple_of(at * rows, rows), rows)] = value
            else:
                for part in range(parts):
                    start = pl.multiple_of((2 * part + at) * wide, wide)
                    out_ref[:, pl.ds(start, wide)] = value[:, part * wide : (part + 1) * wide]


def unpack(flow, links, one, two, tall):
    weights, rows, columns = one.shape
    if rows % 16:
        first = links.core == 0
        one, two = jnp.where(first, one, two), jnp.where(first, two, one)
        if tall:
            mine = jnp.concatenate([one, two], axis=1)
        elif 2 * columns > links.width:
            mine = jnp.stack([one, two], axis=2).reshape(weights, rows, 2, links.owners, -1)
            mine = mine.transpose(0, 1, 3, 2, 4).reshape(weights, rows, 2 * columns)
        else:
            mine = jnp.concatenate([one, two], axis=2)
        return list(mine.astype(F32))
    shape = (2 * rows, columns) if tall else (rows, 2 * columns)
    return flow.call(
        functools.partial(unpack_kernel, tall, links.owners),
        "unpack",
        (links.core_word,),
        (1,),
        [whole(one), whole(two)],
        [(shape, F32, full_spec(shape))] * weights,
    )


def pack_small_kernel(*refs):
    out_ref = refs[-1]
    for index, ref in enumerate(refs[:-1]):
        out_ref[index : index + 1, : ref.shape[1]] = ref[...]


def pack_small(flow, vectors):
    width = max(item.shape[1] for item in vectors)
    shape = (8, width)
    return flow.call(
        pack_small_kernel, "pack_small", (), (1,), [whole(item) for item in vectors], [(shape, F32, full_spec(shape))]
    )[0]


def on_device(
    reps,
    owners,
    hidden,
    memory,
    lengths,
    buckets,
    cotangent,
    self_gain,
    self_query,
    self_key,
    self_value,
    self_out,
    bias_table,
    cross_gain,
    cross_query,
    cross_key,
    cross_value,
    cross_out,
    feed_gain,
    feed_gate,
    feed_up,
    feed_down,
):
    width = hidden.shape[2]
    share = width // owners
    links = Links(reps, owners, width)
    hidden, memory, cotangent = hidden[0], memory[0], cotangent[0]
    flow = Flow()
    core = links.core_word
    far = links.far_to_near()
    order = far + ("first", "second")
    w_feed = gather_feed(links, reps, feed_gate, feed_up, feed_down)
    small = jnp.concatenate([self_gain, cross_gain, feed_gain, bias_table])[None]
    bits = list(range(links.bits - 1, -1, -1))
    a, b = pack(
        links,
        flow,
        (
            (self_query, self_key, self_value),
            (self_out, cross_query, cross_key, cross_value, cross_out),
        ),
    )
    for at, name in enumerate(order[:-1]):
        pairs = [(a, links.step(a, name))]
        if at > 0:
            pairs.append((b, links.step(b, order[at - 1])))
        if bits:
            tiny = links.over_owner(small, bits.pop(0))
            flow.after(tiny)
            small = jnp.concatenate([small, tiny], axis=0)
        if at > 0:
            (a,) = double(flow, pairs[:1])
            (b,) = double(flow, pairs[1:])
        else:
            (a,) = double(flow, pairs)
    apart = jnp.arange(owners) ^ links.owner
    place = sum(((apart >> bit) & 1) << (links.bits - 1 - bit) for bit in range(links.bits))
    small = small[place].astype(F32)
    gain_one = small[:, :share].reshape(1, -1)
    gain_two = small[:, share : 2 * share].reshape(1, -1)
    gain_three = small[:, 2 * share : 3 * share].reshape(1, -1)
    table = small[:, 3 * share :].reshape(BUCKETS, HEADS)
    picks = (buckets[:, None] == jnp.arange(BUCKETS)[None, :]).astype(F32)
    offsets = jnp.dot(picks, table, precision=PRECISE).T.reshape(HEADS // 2, 2, -1)

    memory_got = links.over_core(memory)
    (a,) = double(flow, [(a, links.step(a, order[-1]))])
    flow.after(memory_got)
    cotangent_got = links.over_core(cotangent)
    flow.after(offsets)
    b_got = links.step(b, order[-2])
    w_self = assemble(links, flow, order, a, links.over_core(a))
    flow.after(cotangent_got)
    normed_one, qkv = query_step(flow, core, hidden, gain_one, w_self)
    normed_one_got = links.over_core(normed_one)
    (b,) = double(flow, [(b, b_got)])
    b_got = links.step(b, order[-1])
    mixed_one, lse_one = attend_forward(flow, lengths, offsets, qkv)
    mixed_one_got = links.over_core(mixed_one)
    flow.after(normed_one_got)
    (b,) = double(flow, [(b, b_got)])
    w_cross = assemble(links, flow, order, b, links.over_core(b))
    after_self, normed_two, cross_qkv = cross_step(
        flow, core, mixed_one, hidden, memory, gain_two, w_cross
    )
    normed_two_got = links.over_core(normed_two)
    mixed_two, lse_two = attend_forward(flow, lengths, None, cross_qkv)
    mixed_two_got = links.over_core(mixed_two)
    flow.after(normed_two_got, mixed_one_got)
    after_cross, normed_three = out_step(flow, core, mixed_two, after_self, gain_three, w_cross, 4)
    normed_three_got = links.over_core(normed_three)
    flow.after(mixed_two_got, normed_three_got)
    parts_other, out, back = feed_first(flow, core, normed_three, cotangent, w_feed)
    parts_got = links.over_core(parts_other)
    (
        parts,
        layer_out,
        carry_two,
        gain_three_grad,
        branch_other,
        branch_two,
        mixed_grad,
    ) = feed_second(
        flow,
        core,
        normed_three,
        cotangent,
        w_feed,
        out,
        back,
        after_cross,
        gain_three,
        w_cross,
        4,
    )
    branch_two_got = links.over_core(branch_other)

    down = order[::-1]
    sums_c = Reduce(
        links,
        flow,
        down,
        *weight_grads(
            links,
            flow,
            down,
            [(0, None, 0, 1), (0, None, 0, 2)],
            [normed_three],
            [normed_three_got],
            [parts],
            [parts_got],
        ),
    )
    sums_d = Reduce(
        links,
        flow,
        down,
        *weight_grads(
            links,
            flow,
            down,
            [(0, 0, 0, None)],
            [parts],
            [parts_got],
            [cotangent],
            [cotangent_got],
        ),
        tall=True,
    )
    (cross_other,) = attend_backward(flow, lengths, core, True, None, cross_qkv, mixed_grad, lse_two)
    cross_got = links.over_core(cross_other)
    flow.after(branch_two_got)
    (cross_mine,) = attend_backward(flow, lengths, core, False, None, cross_qkv, mixed_grad, lse_two)
    sums_c.advance()
    carry_one, gain_two_grad, branch_other, branch_one, mixed_grad = middle_step(
        flow, core, cross_other, cross_mine, after_self, gain_two, carry_two, w_cross, 1, 0
    )
    branch_one_got = links.over_core(branch_other)
    sums_d.advance()
    sums_b = Reduce(
        links,
        flow,
        down,
        *weight_grads(
            links,
            flow,
            down,
            [
                (0, None, 0, None),
                (1, None, 1, 0),
                (2, None, 1, 1),
                (2, None, 1, 2),
                (3, None, 2, None),
            ],
            [mixed_one, normed_two, memory, mixed_two],
            [mixed_one_got, normed_two_got, memory_got, mixed_two_got],
            [branch_one, cross_mine, branch_two],
            [branch_one_got, cross_got, branch_two_got],
        ),
    )
    sums_c.advance()
    self_other, offsets_other = attend_backward(
        flow, lengths, core, True, offsets, qkv, mixed_grad, lse_one
    )
    self_got = links.over_core(self_other)
    sums_d.advance()
    self_mine, offsets_mine = attend_backward(
        flow, lengths, core, False, offsets, qkv, mixed_grad, lse_one
    )
    sums_b.advance()
    sums_a = Reduce(
        links,
        flow,
        down,
        *weight_grads(
            links,
            flow,
            down,
            [(0, None, 0, 0), (0, None, 0, 1), (0, None, 0, 2)],
            [normed_one],
            [normed_one_got],
            [self_mine],
            [self_got],
        ),
    )
    sums_c.advance()
    sums_b.advance()
    input_grad, gain_one_grad = last_step(
        flow, core, self_other, self_mine, hidden, gain_one, carry_one, w_self
    )
    first = links.core == 0
    offset_grad = jnp.concatenate(
        [
            jnp.where(first, offsets_mine, offsets_other),
            jnp.where(first, offsets_other, offsets_mine),
        ],
        axis=0,
    ).reshape(HEADS, -1)
    table_grad = jnp.dot(picks.T, offset_grad.T, precision=PRECISE).reshape(1, -1)
    small = pack_small(flow, [gain_one_grad, gain_two_grad, gain_three_grad, table_grad])
    sums_a.advance()
    moves = [links.over_core, links.over_side] + [
        functools.partial(links.over_owner, bit=bit) for bit in range(links.bits)
    ]
    small_got = moves.pop(0)(small)
    sums_c.rest()
    sums_c.sides()
    sums_d.advance()
    memory_grad = memory_step(flow, core, cross_other, cross_mine, w_cross, 2)
    while sums_a.taken < len(down):
        small = sums_a.advance(small, small_got)
        small_got = moves.pop(0)(small)
        if sums_b.taken < len(down):
            sums_b.advance()
        else:
            sums_b.sides()
        if sums_d.taken < len(down):
            sums_d.advance()
        if sums_a.taken == len(down) - 1:
            sums_c.cores()
    sums_d.rest()
    sums_d.sides()
    small = sums_a.sides(small, small_got)
    small_got = moves.pop(0)(small)
    total_c = sums_c.outs()
    sums_b.cores()
    sums_d.cores()
    small = sums_a.cores(small, small_got)
    small_got = moves.pop(0)(small)
    while moves:
        small = small + small_got
        small_got = moves.pop(0)(small)
    small = small + small_got
    total_b = sums_b.outs()
    (total_d,) = sums_d.outs()
    total_a = sums_a.outs()
    small_table = lax.dynamic_slice_in_dim(
        small[3], links.owner * bias_table.shape[0], bias_table.shape[0], 0
    )
    small = lax.dynamic_slice_in_dim(small, links.owner * share, share, 1)
    return (
        layer_out[None],
        input_grad[None],
        memory_grad[None],
        small[0],
        total_a[0],
        total_a[1],
        total_a[2],
        total_b[0],
        small_table,
        small[1],
        total_b[1],
        total_b[2],
        total_b[3],
        total_b[4],
        small[2],
        total_c[0],
        total_c[1],
        total_d,
    )


def solution(mesh):
    rows = P(("rep", "fsdp"), None, None)
    vector = P("fsdp")
    matrix = P("fsdp", None)
    attention = (vector,) + (matrix,) * 4
    return jax.shard_map(
        functools.partial(on_device, mesh.shape["rep"], mesh.shape["fsdp"]),
        mesh=mesh,
        in_specs=(rows, rows, P(("rep", "fsdp")), P(), rows)
        + attention
        + (vector,)
        + attention
        + (vector, matrix, matrix, matrix),
        out_specs=(rows, rows, rows)
        + attention
        + (vector,)
        + attention
        + (vector, matrix, matrix, matrix),
        check_vma=False,
    )
```
